512 devices in a mesh: ctx: 64 (over x_hi, z, core), heads: 8 (over x_lo, y).
Axes of the slice: x: 4 (x_hi: 2, x_lo: 2; x = x_hi * 2 + x_lo), y: 4, z: 16, core: 2. Of those that a mesh axis runs over, the one named last changes fastest.
Arguments:
- queries: bfloat16 [8192, 4096], P('ctx', 'heads'), may hold values from -9 to 9
- keys: bfloat16 [8192, 1024], P('ctx', 'heads'), may hold values from -3 to 3
- values: bfloat16 [8192, 1024], P('ctx', 'heads'), may hold values from -6 to 6
- outputs: bfloat16 [8192, 4096], P(('ctx', 'heads')), may hold values from -6 to 6
- out_grad: bfloat16 [8192, 4096], P(('ctx', 'heads')), may hold values from -6 to 6
- lse: float32 [8192, 32], P('ctx', 'heads'), as said below
- positions: int32 [8192], P('ctx'), may hold values from 0 to 8191, as said below
Outputs:
- query_grad: bfloat16 [8192, 4096], P('ctx', 'heads')
- key_grad: bfloat16 [8192, 1024], P('ctx', 'heads')
- value_grad: bfloat16 [8192, 1024], P('ctx', 'heads')
The draws below stay inside these ranges and needn't reach their ends.
Inputs may be any that keep to these rules, and one draw needn't show every extreme that they name: A permutation of 0 to 8191. Rows d * 128 to (d + 1) * 128 - 1 hold two runs of 64 consecutive positions, blocks c and 127 - c of size 64 for some c, in either order. lse[i, h] = log of the sum over all 8192 tokens j of exp(S[i, j]) for head h, with S as in the first step from the given queries, keys and positions (masked entries at -1e30 included).
All inputs are finite; a program needn't handle non-finite values.
Results may differ from the reference program's by a relative error of at most 0.0049.
Values may be sent and summed in bfloat16 or wider, within the bound.
No kernel may reach another device: no remote copies, remote signals or barrier semaphores. Data moves between devices by JAX's collectives and lax.ppermute only.
A program may use at most 64 MiB of HBM per device.

```python
import math
import jax
import jax.numpy as jnp
from jax import lax

QUERY_HEADS = 32
KEY_VALUE_HEADS = 8
HEAD_SIZE = 128
TOK_DEV = 128
BLK = 64
SEQUENCE_TOKENS = 8192
N_CTX = 64


def draw_queries(key, part):
    key = jax.random.fold_in(key, 1)
    base_offset = jnp.clip(jax.random.normal(key, (SEQUENCE_TOKENS, QUERY_HEADS * HEAD_SIZE), jnp.float32), -3.0, 3.0)
    return base_offset.astype(jnp.bfloat16)


def draw_keys(key, part):
    key = jax.random.fold_in(key, 2)
    base_offset = jnp.clip(jax.random.normal(key, (SEQUENCE_TOKENS, KEY_VALUE_HEADS * HEAD_SIZE), jnp.float32), -3.0, 3.0)
    return base_offset.astype(jnp.bfloat16)


def draw_positions(key, part):
    key = jax.random.fold_in(key, 3)
    pairing = jax.random.permutation(key, N_CTX)
    flipped = jax.random.randint(jax.random.fold_in(key, 4), (N_CTX,), 0, 2)
    index = jnp.arange(SEQUENCE_TOKENS)
    device = index // TOK_DEV
    half = index % TOK_DEV // BLK
    offset = index % BLK
    early = pairing[device]
    late = (half + flipped[device]) % 2
    block_id = jnp.where(late == 1, 2 * N_CTX - 1 - early, early)
    return (block_id * BLK + offset).astype(jnp.int32)


def draw_lse(key, part):
    query_all = draw_queries(key, part).astype(jnp.float32).reshape(SEQUENCE_TOKENS, QUERY_HEADS, HEAD_SIZE)
    key_complete = draw_keys(key, part).astype(jnp.float32).reshape(SEQUENCE_TOKENS, KEY_VALUE_HEADS, HEAD_SIZE)
    position = draw_positions(key, part)
    query_group = QUERY_HEADS // KEY_VALUE_HEADS
    scale = 1.0 / math.sqrt(HEAD_SIZE)
    width = math.gcd(SEQUENCE_TOKENS, 512)
    nblocks = SEQUENCE_TOKENS // width

    def one_head(head):
        key_h = lax.dynamic_index_in_dim(key_complete, head // query_group, 1, keepdims=False)
        query_h = lax.dynamic_index_in_dim(query_all, head, 1, keepdims=False).reshape(nblocks, width, HEAD_SIZE)

        def one_block(item):
            q_blk, p_blk = item
            scores = jnp.dot(q_blk, key_h.T, precision=lax.Precision.HIGHEST) * scale
            scores = jnp.where(position[None, :] <= p_blk[:, None], scores, -1e+30)
            top = jnp.max(scores, axis=-1)
            return top + jnp.log(jnp.sum(jnp.exp(scores - top[:, None]), axis=-1))
        return lax.map(one_block, (query_h, position.reshape(nblocks, width))).reshape(SEQUENCE_TOKENS)
    table = lax.map(one_head, jnp.arange(QUERY_HEADS))
    return table.T.astype(jnp.float32)


def block_scale(own_key, extent, split, least, high):
    gain, own = 1.0, jax.random.fold_in(own_key, 6)
    for axis_at, parts in split:
        steps = jnp.exp(jax.random.uniform(jax.random.fold_in(own, axis_at), (parts,), jnp.float32, least / len(split), high / len(split)))
        gain = gain * jnp.repeat(steps, extent[axis_at] // parts).reshape([-1 if axis == axis_at else 1 for axis in range(len(extent))])
    return gain


def scatter_about(stream_key, dims, scale, bound, pieces=(), held_as=jnp.bfloat16):
    values = jax.random.normal(stream_key, dims, jnp.float32) * scale
    if len(pieces) > 0:
        values = block_scale(stream_key, dims, pieces, -0.22, 0.18) * values
    return jnp.clip(values, min=-bound, max=bound).astype(held_as)


def setup_inputs(seed: int = 0) -> dict:
    arg_keys = jax.random.split(jax.random.key(seed), 8)
    queries = draw_queries(jax.random.fold_in(arg_keys[7], 71), 0)
    keys = draw_keys(jax.random.fold_in(arg_keys[7], 71), 0)
    values = scatter_about(arg_keys[2], (SEQUENCE_TOKENS, KEY_VALUE_HEADS * HEAD_SIZE), 1.0, 6.0, ((0, 64), (1, 8)))
    outputs = scatter_about(arg_keys[3], (SEQUENCE_TOKENS, QUERY_HEADS * HEAD_SIZE), 1.0, 6.0, ((0, 512),))
    out_grad = scatter_about(arg_keys[4], (SEQUENCE_TOKENS, QUERY_HEADS * HEAD_SIZE), 1.0, 6.0, ((0, 512),))
    lse = draw_lse(jax.random.fold_in(arg_keys[7], 71), 0)
    positions = draw_positions(jax.random.fold_in(arg_keys[7], 71), 0)
    return dict(queries=queries, keys=keys, values=values, outputs=outputs, out_grad=out_grad, lse=lse, positions=positions)


def reference(queries, keys, values, outputs, out_grad, lse, positions):
    tokens = queries.shape[0]
    query_group = QUERY_HEADS // KEY_VALUE_HEADS
    scale = 1.0 / math.sqrt(HEAD_SIZE)
    width = math.gcd(tokens, 512)
    nblocks = tokens // width
    query_pos = positions.reshape(nblocks, width)
    dq_cols = []
    dk_cols = []
    dv_cols = []
    for key_value_head in range(KEY_VALUE_HEADS):
        key_h = keys[:, key_value_head * HEAD_SIZE:(key_value_head + 1) * HEAD_SIZE]
        val_h = values[:, key_value_head * HEAD_SIZE:(key_value_head + 1) * HEAD_SIZE]
        dk_sum = jnp.zeros((tokens, HEAD_SIZE), jnp.float32)
        dv_sum = jnp.zeros((tokens, HEAD_SIZE), jnp.float32)
        for member in range(query_group):
            head = key_value_head * query_group + member
            cols = slice(head * HEAD_SIZE, (head + 1) * HEAD_SIZE)
            query_h = queries[:, cols].reshape(nblocks, width, HEAD_SIZE)
            out_h = outputs[:, cols].reshape(nblocks, width, HEAD_SIZE)
            grad_h = out_grad[:, cols].reshape(nblocks, width, HEAD_SIZE)
            lse_h = lse[:, head].reshape(nblocks, width)

            def block(carry, item):
                dk_acc, dv_acc = carry
                q_blk, o_blk, g_blk, p_blk, l_blk = item
                scores = jnp.dot(q_blk, key_h.T, preferred_element_type=jnp.float32) * scale
                scores = jnp.where(positions[None, :] <= p_blk[:, None], scores, -1e+30)
                probs = jnp.exp(scores - l_blk[:, None])
                probs_b = probs.astype(jnp.bfloat16)
                delta = lax.optimization_barrier(jnp.sum(o_blk.astype(jnp.float32) * g_blk.astype(jnp.float32), axis=-1))
                dprob = jnp.dot(g_blk, val_h.T, preferred_element_type=jnp.float32)
                dscore = (probs * (dprob - delta[:, None])).astype(jnp.bfloat16)
                dq_blk = jnp.dot(dscore, key_h, preferred_element_type=jnp.float32) * scale
                dk_acc = dk_acc + jnp.dot(dscore.T, q_blk, preferred_element_type=jnp.float32)
                dv_acc = dv_acc + jnp.dot(probs_b.T, g_blk, preferred_element_type=jnp.float32)
                return ((dk_acc, dv_acc), dq_blk.astype(jnp.bfloat16))
            (dk_sum, dv_sum), dq_h = lax.scan(block, (dk_sum, dv_sum), (query_h, out_h, grad_h, query_pos, lse_h))
            dq_cols.append(dq_h.reshape(tokens, HEAD_SIZE))
        dk_cols.append((dk_sum * scale).astype(jnp.bfloat16))
        dv_cols.append(dv_sum.astype(jnp.bfloat16))
    return (jnp.concatenate(dq_cols, axis=1), jnp.concatenate(dk_cols, axis=1), jnp.concatenate(dv_cols, axis=1))
```

```python
import math

import jax
import jax.numpy as jnp
from jax import lax
from jax.experimental import pallas as pl
from jax.experimental.pallas import tpu as pltpu
from jax.sharding import PartitionSpec as P

HEAD = 128
BLK = 64
TOK = 2 * BLK
GROUP = 4
ROWS = GROUP * BLK
SET = 4
LOG2E = math.log2(math.e)
SCALE = 1.0 / math.sqrt(HEAD)
FAR = 1e30
F32 = jnp.float32
BF16 = jnp.bfloat16
FOLD = None


def dot_nt(a, b):
    return lax.dot_general(a, b, (((1,), (1,)), ((), ())), preferred_element_type=F32)


def dot_nn(a, b):
    return lax.dot_general(a, b, (((1,), (0,)), ((), ())), preferred_element_type=F32)


def dot_tn(a, b):
    return lax.dot_general(a, b, (((0,), (0,)), ((), ())), preferred_element_type=F32)


def backward(x_ref, xx_ref, y_ref, s_ref, p_ref, m_ref, h1_ref, h2_ref, *rest):
    own_out, p_out, m_out, h1_out, h2_out, dq_out, dq_core_out, acc, dq_acc = rest
    seen = lax.broadcasted_iota(jnp.int32, (BLK, ROWS), 0) <= (
        lax.broadcasted_iota(jnp.int32, (BLK, ROWS), 1) % BLK
    )
    acc[...] = jnp.zeros_like(acc)

    def grads(scores, dprob, lse, delta):
        probs = jnp.exp2(scores * (SCALE * LOG2E) - lse)
        dscore = probs * (dprob - delta)
        return probs.astype(BF16), dscore.astype(BF16)

    def row_vectors(table):
        return [
            jnp.concatenate([table[h : h + 1, s : s + BLK] for h in range(GROUP)], axis=1)
            for s in (0, BLK)
        ]

    def half_rows(block):
        return [
            jnp.concatenate(
                [block[s : s + BLK, h * HEAD : (h + 1) * HEAD] for h in range(GROUP)], axis=0
            )
            for s in (0, BLK)
        ]

    def query_side(block):
        wide = GROUP * HEAD
        tail = jnp.transpose(block[:, wide : wide + HEAD].astype(F32))
        lse = tail[0:8, :] + tail[8:16, :] + tail[16:24, :]
        c_row, swapped = tail[24:25, :], tail[25:26, :] > 0.5
        tail = jnp.transpose(block[:, 2 * wide + HEAD :].astype(F32))
        delta = tail[0:8, :] + tail[8:16, :] + tail[16:24, :]
        d0, d1 = row_vectors(delta)
        g0, g1 = half_rows(block[:, wide + HEAD : 2 * wide + HEAD])
        two = jnp.concatenate([swapped, swapped], axis=1)
        tall = jnp.broadcast_to(swapped, (ROWS, HEAD))
        return (
            c_row,
            row_vectors(lse * LOG2E),
            (jnp.where(two, d1, d0), jnp.where(two, d0, d1)),
            half_rows(block[:, :wide]),
            (jnp.where(tall, g1, g0), jnp.where(tall, g0, g1)),
        )

    def pick(i, j):
        if i < 3:
            return (s_ref, p_ref, m_ref)[i][:, j]
        return jnp.concatenate([h1_ref[:, j], h2_ref[:, j]], axis=0)

    def flat(x):
        return x.reshape(SET * BLK, HEAD)

    def visit(block, e, own=False):
        own_c, lse, delta, q, g = query_side(block)
        (lse_early, lse_late), (delta_early, delta_late) = lse, delta
        q_late, g_late = q[1], g[1]
        q_both = jnp.concatenate(q, axis=1)
        g_both = jnp.concatenate(g, axis=1)
        dq_a = jnp.zeros((HEAD, ROWS), F32)
        dq_b = jnp.zeros((2 * HEAD, ROWS), F32)
        for i in range(4):
            c = pick(i, slice(4 * BLK, 4 * BLK + 16)).astype(F32)[:, 0:1, :]
            before = c < own_c[None]
            after = c > own_c[None]
            wide = jnp.broadcast_to(before, (SET, BLK, HEAD))
            k_early, k_late, v_early, v_late = [
                pick(i, slice(j * BLK, (j + 1) * BLK)) for j in range(4)
            ]
            k_both = jnp.concatenate(
                [flat(jnp.where(wide, k_early, 0)), flat(jnp.where(wide, 0, k_late))], axis=1
            )
            v_both = jnp.concatenate(
                [flat(jnp.where(wide, v_early, 0)), flat(jnp.where(wide, 0, v_late))], axis=1
            )
            k_early, v_early = flat(k_early), flat(v_early)
            before2 = jnp.concatenate([before, before], axis=2)
            after2 = jnp.concatenate([after, after], axis=2)
            lse_b = jnp.where(before2, lse_early[None], jnp.where(after2, lse_late[None], FAR))
            delta_b = jnp.where(before2, delta_early[None], delta_late[None])
            lse_b = jnp.broadcast_to(lse_b, (SET, BLK, ROWS)).reshape(SET * BLK, ROWS)
            delta_b = jnp.broadcast_to(delta_b, (SET, BLK, ROWS)).reshape(SET * BLK, ROWS)

            p_a, ds_a = grads(
                dot_nt(k_early, q_late), dot_nt(v_early, g_late), lse_late, delta_late
            )
            p_b, ds_b = grads(dot_nt(k_both, q_both), dot_nt(v_both, g_both), lse_b, delta_b)
            dv_a, dk_a = dot_nn(p_a, g_late), dot_nn(ds_a, q_late)
            dv_b, dk_b = dot_nn(p_b, g_both), dot_nn(ds_b, q_both)
            dq_a = dq_a + dot_tn(k_early, ds_a)
            dq_b = dq_b + dot_tn(k_both, ds_b)
            for j, one, two in ((0, dk_a, dk_b), (2, dv_a, dv_b)):
                one = one.reshape(SET, BLK, HEAD)
                two = two.reshape(SET, BLK, 2 * HEAD)
                acc[i, :, j * BLK : (j + 1) * BLK] += one + jnp.where(wide, two[:, :, :HEAD], 0.0)
                acc[i, :, (j + 1) * BLK : (j + 2) * BLK] += jnp.where(
                    wide, 0.0, two[:, :, HEAD:]
                )
        dq = [dq_b[:HEAD], dq_b[HEAD:] + dq_a]
        if own:
            for i in range(2):
                at = slice(i * BLK, (i + 1) * BLK)
                k, v = s_ref[0, at], s_ref[0, (2 + i) * BLK : (3 + i) * BLK]
                scores = jnp.where(seen, dot_nt(k, q[i]), -FAR)
                p, ds = grads(scores, dot_nt(v, g[i]), lse[i], delta[i])
                acc[0, 0, at] += dot_nn(ds, q[i])
                acc[0, 0, (2 + i) * BLK : (3 + i) * BLK] += dot_nn(p, g[i])
                dq[i] = dq[i] + dot_tn(k, ds)
        for i in range(2):
            grad = jnp.transpose(dq[i]) * SCALE
            for h in range(GROUP):
                dq_acc[e, i * BLK : (i + 1) * BLK, h * HEAD : (h + 1) * HEAD] = grad[
                    h * BLK : (h + 1) * BLK
                ]

    visit(x_ref[...], 0, own=True)
    visit(xx_ref[...], 1)

    @pl.loop(0, 2)
    def _(e):
        visit(y_ref[e], e + 2)

    dq_out[...] = dq_acc[:2]
    dq_core_out[...] = dq_acc[2:].astype(BF16)
    acc[:, :, : 2 * BLK] = acc[:, :, : 2 * BLK] * SCALE
    own_out[...] = acc[0]
    p_out[...] = acc[1].astype(BF16)
    m_out[...] = acc[2].astype(BF16)
    h1_out[...] = acc[3, :2].astype(BF16)
    h2_out[...] = acc[3, 2:].astype(BF16)


def bf16_terms(x):
    hi = lax.reduce_precision(x, 8, 7)
    rest = x - hi
    mid = lax.reduce_precision(rest, 8, 7)
    return [hi.astype(BF16), mid.astype(BF16), (rest - mid).astype(BF16)]


def tail_of(x, *flags):
    lead = x.shape[:-1]
    gap = jnp.zeros(lead + (8 - GROUP,), BF16)
    parts = [part for term in bf16_terms(x) for part in (term, gap)]
    parts += [jnp.broadcast_to(f.astype(BF16), lead + (1,)) for f in flags]
    parts.append(jnp.zeros(lead + (HEAD - 24 - len(flags),), BF16))
    return jnp.concatenate(parts, axis=-1)


HEADS = ("xl", "y")


def shifted(x, by):
    n = lax.axis_size("z")
    return lax.ppermute(x, "z", [(i, (i + by) % n) for i in range(n)])


def swapped_with(x, axis):
    return lax.ppermute(x, axis, [(0, 1), (1, 0)])


def shards(queries, keys, values, outputs, out_grad, lse, positions):
    n_heads = lax.axis_size(HEADS)
    quarter = lax.axis_size("z") // 4
    first, second = positions[0], positions[BLK]
    swapped = (first > second).astype(jnp.int32)
    c = jnp.minimum(first, second) // BLK

    def early_then_late(x):
        return jnp.where(swapped == 1, jnp.concatenate([x[BLK:], x[:BLK]]), x)

    own = jnp.concatenate(
        [
            early_then_late(keys),
            early_then_late(values),
            jnp.broadcast_to(c.astype(BF16), (16, HEAD)),
        ]
    )
    far = shifted(own, 2 * quarter)
    s_set = jnp.stack([own, shifted(own, quarter), shifted(own, -quarter), far])
    p_set, m_set = shifted(s_set, 1), shifted(s_set, -1)
    h1 = shifted(s_set[:2], 2)
    h2 = shifted(jnp.stack([s_set[0], s_set[2]]), -2)

    tok = out_grad.shape[0]
    delta = jnp.sum(
        (outputs.astype(F32) * out_grad.astype(F32)).reshape(tok, n_heads, GROUP, HEAD), axis=-1
    )
    send = jnp.concatenate(
        [out_grad.reshape(tok, n_heads, GROUP * HEAD), tail_of(delta)], axis=-1
    ).transpose(1, 0, 2)
    grad = lax.all_to_all(send, HEADS, split_axis=0, concat_axis=0, tiled=True)
    own_q = early_then_late(jnp.concatenate([queries, tail_of(lse, c, swapped)], axis=1))
    x = jnp.concatenate([own_q, grad.reshape(TOK, (GROUP + 1) * HEAD)], axis=1)
    xx = swapped_with(x, "xh")
    y = swapped_with(jnp.stack([x, xx]), "core")

    vmem = pl.BlockSpec(memory_space=pltpu.VMEM)
    four, two = (SET, 4 * BLK, HEAD), (2, 4 * BLK, HEAD)
    own_g, p_g, m_g, h1_g, h2_g, dq, dq_core = pl.pallas_call(
        backward,
        out_shape=(
            jax.ShapeDtypeStruct(four, F32),
            jax.ShapeDtypeStruct(four, BF16),
            jax.ShapeDtypeStruct(four, BF16),
            jax.ShapeDtypeStruct(two, BF16),
            jax.ShapeDtypeStruct(two, BF16),
            jax.ShapeDtypeStruct((2, TOK, GROUP * HEAD), F32),
            jax.ShapeDtypeStruct((2, TOK, GROUP * HEAD), BF16),
        ),
        in_specs=[vmem] * 8,
        out_specs=[vmem] * 7,
        scratch_shapes=[
            pltpu.VMEM((4,) + four, F32),
            pltpu.VMEM((4, TOK, GROUP * HEAD), F32),
        ],
        compiler_params=pltpu.CompilerParams(vmem_limit_bytes=40 * 1024 * 1024),
        name="backward",
    )(x, xx, y, s_set, p_set, m_set, h1, h2)

    p_in, m_in = shifted(p_g, -1).astype(F32), shifted(m_g, 1).astype(F32)
    h1_in, h2_in = shifted(h1_g, -2).astype(F32), shifted(h2_g, 2).astype(F32)
    total = own_g + p_in + m_in
    mine = total[0] + h1_in[0] + h2_in[0]
    back = shifted((total[3]).astype(BF16), 2 * quarter).astype(F32)
    left = shifted((total[1] + h1_in[1]).astype(BF16), -quarter).astype(F32)
    right = shifted((total[2] + h2_in[1]).astype(BF16), quarter).astype(F32)
    mine = mine + left + right + back

    dq = dq + swapped_with(dq_core, "core").astype(F32)
    dq = dq[0] + swapped_with(dq[1].astype(BF16), "xh").astype(F32)
    return (
        early_then_late(dq).astype(BF16),
        early_then_late(mine[:TOK]).astype(BF16),
        early_then_late(mine[TOK:]).astype(BF16),
    )


def solution(mesh):
    shape = FOLD or (2, 16, 2, 2, 4)
    split = jax.sharding.Mesh(mesh.devices.reshape(shape), ("xh", "z", "core", "xl", "y"))
    ctx, heads = ("xh", "z", "core"), ("xl", "y")
    return jax.shard_map(
        shards,
        mesh=split,
        in_specs=(
            P(ctx, heads),
            P(ctx, heads),
            P(ctx, heads),
            P(ctx + heads, None),
            P(ctx + heads, None),
            P(ctx, heads),
            P(ctx),
        ),
        out_specs=(P(ctx, heads), P(ctx, heads), P(ctx, heads)),
        check_vma=False,
    )
```

```python
import math

import jax
import jax.numpy as jnp
from jax import lax
from jax.experimental import pallas as pl
from jax.experimental.pallas import tpu as pltpu
from jax.sharding import PartitionSpec as P

HEAD = 128
BLK = 64
TOK = 2 * BLK
GROUP = 4
ROWS = GROUP * BLK
SET = 4
LOG2E = math.log2(math.e)
SCALE = 1.0 / math.sqrt(HEAD)
FAR = 1e30
F32 = jnp.float32
BF16 = jnp.bfloat16
FOLD = None


def dot_nt(a, b):
    return lax.dot_general(a, b, (((1,), (1,)), ((), ())), preferred_element_type=F32)


def dot_nn(a, b):
    return lax.dot_general(a, b, (((1,), (0,)), ((), ())), preferred_element_type=F32)


def dot_tn(a, b):
    return lax.dot_general(a, b, (((0,), (0,)), ((), ())), preferred_element_type=F32)


def backward(info, x_ref, y_ref, s_ref, p_ref, m_ref, h_ref, *rest):
    own_out, p_out, m_out, h_out, dq_out, dq_core_out, acc, dq_acc = rest
    seen = lax.broadcasted_iota(jnp.int32, (BLK, ROWS), 0) <= (
        lax.broadcasted_iota(jnp.int32, (BLK, ROWS), 1) % BLK
    )
    acc[...] = jnp.zeros_like(acc)

    def grads(scores, dprob, lse, delta):
        probs = jnp.exp2(scores * (SCALE * LOG2E) - lse)
        dscore = probs * (dprob - delta)
        return probs.astype(BF16), dscore.astype(BF16)

    def row_vectors(table):
        return [
            jnp.concatenate([table[h : h + 1, s : s + BLK] for h in range(GROUP)], axis=1)
            for s in (0, BLK)
        ]

    def half_rows(block):
        return [
            jnp.concatenate(
                [block[s : s + BLK, h * HEAD : (h + 1) * HEAD] for h in range(GROUP)], axis=0
            )
            for s in (0, BLK)
        ]

    def query_side(block):
        wide = GROUP * HEAD
        tail = jnp.transpose(block[:, wide : wide + HEAD].astype(F32))
        lse = tail[0:8, :] + tail[8:16, :] + tail[16:24, :]
        c_row, swapped = tail[24:25, :], tail[25:26, :] > 0.5
        tail = jnp.transpose(block[:, 2 * wide + HEAD :].astype(F32))
        delta = tail[0:8, :] + tail[8:16, :] + tail[16:24, :]
        d0, d1 = row_vectors(delta)
        g0, g1 = half_rows(block[:, wide + HEAD : 2 * wide + HEAD])
        two = jnp.concatenate([swapped, swapped], axis=1)
        tall = jnp.broadcast_to(swapped, (ROWS, HEAD))
        return (
            c_row,
            row_vectors(lse * LOG2E),
            (jnp.where(two, d1, d0), jnp.where(two, d0, d1)),
            half_rows(block[:, :wide]),
            (jnp.where(tall, g1, g0), jnp.where(tall, g0, g1)),
        )

    def pick(i, j):
        return (s_ref, p_ref, m_ref, h_ref)[i][:, j]

    def flat(x):
        return x.reshape(SET * BLK, HEAD)

    def visit(block, e, own=False):
        own_c, lse, delta, q, g = query_side(block)
        (lse_early, lse_late), (delta_early, delta_late) = lse, delta
        q_late, g_late = q[1], g[1]
        q_both = jnp.concatenate(q, axis=1)
        g_both = jnp.concatenate(g, axis=1)
        dq_a = jnp.zeros((HEAD, ROWS), F32)
        dq_b = jnp.zeros((2 * HEAD, ROWS), F32)
        for i in range(4):
            c = pick(i, slice(4 * BLK, 4 * BLK + 16)).astype(F32)[:, 0:1, :]
            before = c < own_c[None]
            after = c > own_c[None]
            wide = jnp.broadcast_to(before, (SET, BLK, HEAD))
            k_early, k_late, v_early, v_late = [
                pick(i, slice(j * BLK, (j + 1) * BLK)) for j in range(4)
            ]
            k_both = jnp.concatenate(
                [flat(jnp.where(wide, k_early, 0)), flat(jnp.where(wide, 0, k_late))], axis=1
            )
            v_both = jnp.concatenate(
                [flat(jnp.where(wide, v_early, 0)), flat(jnp.where(wide, 0, v_late))], axis=1
            )
            k_early, v_early = flat(k_early), flat(v_early)
            before2 = jnp.concatenate([before, before], axis=2)
            after2 = jnp.concatenate([after, after], axis=2)
            lse_b = jnp.where(before2, lse_early[None], jnp.where(after2, lse_late[None], FAR))
            delta_b = jnp.where(before2, delta_early[None], delta_late[None])
            lse_b = jnp.broadcast_to(lse_b, (SET, BLK, ROWS)).reshape(SET * BLK, ROWS)
            delta_b = jnp.broadcast_to(delta_b, (SET, BLK, ROWS)).reshape(SET * BLK, ROWS)

            p_a, ds_a = grads(
                dot_nt(k_early, q_late), dot_nt(v_early, g_late), lse_late, delta_late
            )
            p_b, ds_b = grads(dot_nt(k_both, q_both), dot_nt(v_both, g_both), lse_b, delta_b)
            dv_a, dk_a = dot_nn(p_a, g_late), dot_nn(ds_a, q_late)
            dv_b, dk_b = dot_nn(p_b, g_both), dot_nn(ds_b, q_both)
            dq_a = dq_a + dot_tn(k_early, ds_a)
            dq_b = dq_b + dot_tn(k_both, ds_b)
            for j, one, two in ((0, dk_a, dk_b), (2, dv_a, dv_b)):
                one = one.reshape(SET, BLK, HEAD)
                two = two.reshape(SET, BLK, 2 * HEAD)
                acc[i, :, j * BLK : (j + 1) * BLK] += one + jnp.where(wide, two[:, :, :HEAD], 0.0)
                acc[i, :, (j + 1) * BLK : (j + 2) * BLK] += jnp.where(
                    wide, 0.0, two[:, :, HEAD:]
                )
        dq = [dq_b[:HEAD], dq_b[HEAD:] + dq_a]
        if own:
            mine = info[0]
            for i in range(2):
                at = slice(i * BLK, (i + 1) * BLK)
                k, v = s_ref[mine, at], s_ref[mine, (2 + i) * BLK : (3 + i) * BLK]
                scores = jnp.where(seen, dot_nt(k, q[i]), -FAR)
                p, ds = grads(scores, dot_nt(v, g[i]), lse[i], delta[i])
                acc[0, mine, at] += dot_nn(ds, q[i])
                acc[0, mine, (2 + i) * BLK : (3 + i) * BLK] += dot_nn(p, g[i])
                dq[i] = dq[i] + dot_tn(k, ds)
        for i in range(2):
            grad = jnp.transpose(dq[i]) * SCALE
            for h in range(GROUP):
                dq_acc[e, i * BLK : (i + 1) * BLK, h * HEAD : (h + 1) * HEAD] = grad[
                    h * BLK : (h + 1) * BLK
                ]

    visit(x_ref[0], 0, own=True)
    visit(x_ref[1], 1)

    @pl.loop(0, 2)
    def _(e):
        visit(y_ref[e], e + 2)

    dq_out[...] = dq_acc[:2]
    dq_core_out[...] = dq_acc[2:].astype(BF16)
    acc[:, :, : 2 * BLK] = acc[:, :, : 2 * BLK] * SCALE
    own_out[...] = acc[0]
    p_out[...] = acc[1].astype(BF16)
    m_out[...] = acc[2].astype(BF16)
    h_out[...] = acc[3].astype(BF16)


def join(info, own_ref, other_ref, grad_ref, after_ref, x_ref):
    wide = (GROUP + 1) * HEAD
    x_ref[0, :, :wide] = own_ref[...]
    x_ref[1, :, :wide] = other_ref[...]
    x_ref[0, :, wide:] = grad_ref[info[1]]
    x_ref[1, :, wide:] = grad_ref[1 - info[1]]


def bf16_terms(x):
    hi = lax.reduce_precision(x, 8, 7)
    rest = x - hi
    mid = lax.reduce_precision(rest, 8, 7)
    return [hi.astype(BF16), mid.astype(BF16), (rest - mid).astype(BF16)]


def tail_of(x, *flags):
    lead = x.shape[:-1]
    gap = jnp.zeros(lead + (8 - GROUP,), BF16)
    parts = [part for term in bf16_terms(x) for part in (term, gap)]
    parts += [jnp.broadcast_to(f.astype(BF16), lead + (1,)) for f in flags]
    parts.append(jnp.zeros(lead + (HEAD - 24 - len(flags),), BF16))
    return jnp.concatenate(parts, axis=-1)


HEADS = ("xl", "y")
RING = ("zq", "zr")


def along_ring(x, to):
    n = lax.axis_size(RING)
    return lax.ppermute(x, RING, [(i, to(i) % n) for i in range(n)])


def plus(i):
    return i + 1


def minus(i):
    return i - 1


def two_on(i):
    return i + 2 if i % 2 == 0 else i - 2


def two_back(i):
    return i - 2 if i % 2 == 0 else i + 2


def swapped_with(x, axis):
    return lax.ppermute(x, axis, [(0, 1), (1, 0)])


def shards(queries, keys, values, outputs, out_grad, lse, positions):
    n_heads = lax.axis_size(HEADS)
    first, second = positions[0], positions[BLK]
    swapped = (first > second).astype(jnp.int32)
    c = jnp.minimum(first, second) // BLK

    def early_then_late(x):
        return jnp.where(swapped == 1, jnp.concatenate([x[BLK:], x[:BLK]]), x)

    own = jnp.concatenate(
        [
            early_then_late(keys),
            early_then_late(values),
            jnp.broadcast_to(c.astype(BF16), (16, HEAD)),
        ]
    )
    s_set = lax.all_to_all(
        jnp.broadcast_to(own[None], (SET,) + own.shape), "zq", split_axis=0, concat_axis=0, tiled=True
    )
    h_set = along_ring(s_set, two_on)
    p_set, m_set = along_ring(s_set, plus), along_ring(s_set, minus)

    tok = out_grad.shape[0]
    wide = (GROUP + 1) * HEAD
    delta = jnp.sum(
        (outputs.astype(F32) * out_grad.astype(F32)).reshape(tok, n_heads, GROUP, HEAD), axis=-1
    )
    send = jnp.concatenate(
        [out_grad.reshape(tok, n_heads, GROUP * HEAD), tail_of(delta)], axis=-1
    ).transpose(1, 0, 2)
    send = jnp.concatenate([send, send])
    grad = lax.all_to_all(send, ("xh",) + HEADS, split_axis=0, concat_axis=0, tiled=True)
    grad = grad.reshape(2, TOK, wide)
    own_q = early_then_late(jnp.concatenate([queries, tail_of(lse, c, swapped)], axis=1))
    other_q = swapped_with(own_q, "xh")
    info = jnp.stack([lax.axis_index("zq"), lax.axis_index("xh")]).astype(jnp.int32)
    smem = pl.BlockSpec(memory_space=pltpu.SMEM)
    vmem = pl.BlockSpec(memory_space=pltpu.VMEM)
    x = pl.pallas_call(
        join,
        out_shape=jax.ShapeDtypeStruct((2, TOK, 2 * wide), BF16),
        in_specs=[smem, vmem, vmem, vmem, pl.BlockSpec(memory_space=pl.ANY)],
        out_specs=vmem,
        name="join",
    )(info, own_q, other_q, grad, s_set)
    y = swapped_with(x, "core")

    four, dq_shape = (SET, 4 * BLK, HEAD), (2, TOK, GROUP * HEAD)
    own_g, p_g, m_g, h_g, dq, dq_core = pl.pallas_call(
        backward,
        out_shape=(
            jax.ShapeDtypeStruct(four, F32),
            jax.ShapeDtypeStruct(four, BF16),
            jax.ShapeDtypeStruct(four, BF16),
            jax.ShapeDtypeStruct(four, BF16),
            jax.ShapeDtypeStruct(dq_shape, F32),
            jax.ShapeDtypeStruct(dq_shape, BF16),
        ),
        in_specs=[smem] + [vmem] * 6,
        out_specs=[vmem] * 6,
        scratch_shapes=[
            pltpu.VMEM((4,) + four, F32),
            pltpu.VMEM((4, TOK, GROUP * HEAD), F32),
        ],
        compiler_params=pltpu.CompilerParams(vmem_limit_bytes=40 * 1024 * 1024),
        name="backward",
    )(info, x, y, s_set, p_set, m_set, h_set)

    h_in = along_ring(h_g, two_back).astype(F32)
    p_in, m_in = along_ring(p_g, minus).astype(F32), along_ring(m_g, plus).astype(F32)
    total = (own_g + p_in + m_in + h_in).astype(BF16)
    mine = lax.all_to_all(total, "zq", split_axis=0, concat_axis=0, tiled=True)
    mine = jnp.sum(mine.astype(F32), axis=0)

    dq = dq + swapped_with(dq_core, "core").astype(F32)
    dq = dq[0] + swapped_with(dq[1].astype(BF16), "xh").astype(F32)
    return (
        early_then_late(dq).astype(BF16),
        early_then_late(mine[:TOK]).astype(BF16),
        early_then_late(mine[TOK:]).astype(BF16),
    )


def solution(mesh):
    shape = FOLD or (2, 4, 4, 2, 2, 4)
    split = jax.sharding.Mesh(mesh.devices.reshape(shape), ("xh", "zq", "zr", "core", "xl", "y"))
    ctx, heads = ("xh", "zq", "zr", "core"), ("xl", "y")
    return jax.shard_map(
        shards,
        mesh=split,
        in_specs=(
            P(ctx, heads),
            P(ctx, heads),
            P(ctx, heads),
            P(ctx + heads, None),
            P(ctx + heads, None),
            P(ctx, heads),
            P(ctx),
        ),
        out_specs=(P(ctx, heads), P(ctx, heads), P(ctx, heads)),
        check_vma=False,
    )
```

```python
import math

import jax
import jax.numpy as jnp
from jax import lax
from jax.experimental import pallas as pl
from jax.experimental.pallas import tpu as pltpu
from jax.sharding import PartitionSpec as P

HEAD = 128
BLK = 64
TOK = 2 * BLK
GROUP = 4
ROWS = GROUP * BLK
SET = 4
NEAR = 5
LOG2E = math.log2(math.e)
SCALE = 1.0 / math.sqrt(HEAD)
FAR = 1e30
F32 = jnp.float32
BF16 = jnp.bfloat16
FOLD = None


def dot_nt(a, b):
    return lax.dot_general(a, b, (((1,), (1,)), ((), ())), preferred_element_type=F32)


def dot_nn(a, b):
    return lax.dot_general(a, b, (((1,), (0,)), ((), ())), preferred_element_type=F32)


def dot_tn(a, b):
    return lax.dot_general(a, b, (((0,), (0,)), ((), ())), preferred_element_type=F32)


def backward(x_ref, y_ref, s_ref, p_ref, m_ref, e_ref, *rest):
    own_out, p_out, m_out, e_out, dq_out, dq_core_out, kv, acc, dq_acc = rest
    kv[:NEAR] = s_ref[...]
    kv[NEAR : 2 * NEAR] = p_ref[...]
    kv[2 * NEAR : 3 * NEAR] = m_ref[...]
    kv[3 * NEAR] = e_ref[...]
    seen = lax.broadcasted_iota(jnp.int32, (BLK, ROWS), 0) <= (
        lax.broadcasted_iota(jnp.int32, (BLK, ROWS), 1) % BLK
    )
    acc[...] = jnp.zeros_like(acc)

    def grads(scores, dprob, lse, delta):
        probs = jnp.exp2(scores * (SCALE * LOG2E) - lse)
        dscore = probs * (dprob - delta)
        return probs.astype(BF16), dscore.astype(BF16)

    def row_vectors(table):
        return [
            jnp.concatenate([table[h : h + 1, s : s + BLK] for h in range(GROUP)], axis=1)
            for s in (0, BLK)
        ]

    def half_rows(block):
        return [
            jnp.concatenate(
                [block[s : s + BLK, h * HEAD : (h + 1) * HEAD] for h in range(GROUP)], axis=0
            )
            for s in (0, BLK)
        ]

    def query_side(block):
        wide = GROUP * HEAD
        tail = jnp.transpose(block[:, wide : wide + HEAD].astype(F32))
        lse = tail[0:8, :] + tail[8:16, :] + tail[16:24, :]
        c_row, swapped = tail[24:25, :], tail[25:26, :] > 0.5
        tail = jnp.transpose(block[:, 2 * wide + HEAD :].astype(F32))
        delta = tail[0:8, :] + tail[8:16, :] + tail[16:24, :]
        d0, d1 = row_vectors(delta)
        g0, g1 = half_rows(block[:, wide + HEAD : 2 * wide + HEAD])
        two = jnp.concatenate([swapped, swapped], axis=1)
        tall = jnp.broadcast_to(swapped, (ROWS, HEAD))
        return (
            c_row,
            row_vectors(lse * LOG2E),
            (jnp.where(two, d1, d0), jnp.where(two, d0, d1)),
            half_rows(block[:, :wide]),
            (jnp.where(tall, g1, g0), jnp.where(tall, g0, g1)),
        )

    def pick(i, j):
        return kv[i * SET : (i + 1) * SET, j]

    def flat(x):
        return x.reshape(SET * BLK, HEAD)

    def visit(block, e, own=False):
        own_c, lse, delta, q, g = query_side(block)
        (lse_early, lse_late), (delta_early, delta_late) = lse, delta
        q_late, g_late = q[1], g[1]
        q_both = jnp.concatenate(q, axis=1)
        g_both = jnp.concatenate(g, axis=1)
        dq_a = jnp.zeros((HEAD, ROWS), F32)
        dq_b = jnp.zeros((2 * HEAD, ROWS), F32)
        for i in range(4):
            c = pick(i, slice(4 * BLK, 4 * BLK + 16)).astype(F32)[:, 0:1, :]
            before = c < own_c[None]
            after = c > own_c[None]
            wide = jnp.broadcast_to(before, (SET, BLK, HEAD))
            k_early, k_late, v_early, v_late = [
                pick(i, slice(j * BLK, (j + 1) * BLK)) for j in range(4)
            ]
            k_both = jnp.concatenate(
                [flat(jnp.where(wide, k_early, 0)), flat(jnp.where(wide, 0, k_late))], axis=1
            )
            v_both = jnp.concatenate(
                [flat(jnp.where(wide, v_early, 0)), flat(jnp.where(wide, 0, v_late))], axis=1
            )
            k_early, v_early = flat(k_early), flat(v_early)
            before2 = jnp.concatenate([before, before], axis=2)
            after2 = jnp.concatenate([after, after], axis=2)
            lse_b = jnp.where(before2, lse_early[None], jnp.where(after2, lse_late[None], FAR))
            delta_b = jnp.where(before2, delta_early[None], delta_late[None])
            lse_b = jnp.broadcast_to(lse_b, (SET, BLK, ROWS)).reshape(SET * BLK, ROWS)
            delta_b = jnp.broadcast_to(delta_b, (SET, BLK, ROWS)).reshape(SET * BLK, ROWS)

            p_a, ds_a = grads(
                dot_nt(k_early, q_late), dot_nt(v_early, g_late), lse_late, delta_late
            )
            p_b, ds_b = grads(dot_nt(k_both, q_both), dot_nt(v_both, g_both), lse_b, delta_b)
            dv_a, dk_a = dot_nn(p_a, g_late), dot_nn(ds_a, q_late)
            dv_b, dk_b = dot_nn(p_b, g_both), dot_nn(ds_b, q_both)
            dq_a = dq_a + dot_tn(k_early, ds_a)
            dq_b = dq_b + dot_tn(k_both, ds_b)
            for j, one, two in ((0, dk_a, dk_b), (2, dv_a, dv_b)):
                one = one.reshape(SET, BLK, HEAD)
                two = two.reshape(SET, BLK, 2 * HEAD)
                acc[i * SET : (i + 1) * SET, j * BLK : (j + 1) * BLK] += one + jnp.where(wide, two[:, :, :HEAD], 0.0)
                acc[i * SET : (i + 1) * SET, (j + 1) * BLK : (j + 2) * BLK] += jnp.where(
                    wide, 0.0, two[:, :, HEAD:]
                )
        dq = [dq_b[:HEAD], dq_b[HEAD:] + dq_a]
        if own:
            for i in range(2):
                at = slice(i * BLK, (i + 1) * BLK)
                k, v = kv[0, at], kv[0, (2 + i) * BLK : (3 + i) * BLK]
                scores = jnp.where(seen, dot_nt(k, q[i]), -FAR)
                p, ds = grads(scores, dot_nt(v, g[i]), lse[i], delta[i])
                acc[0, at] += dot_nn(ds, q[i])
                acc[0, (2 + i) * BLK : (3 + i) * BLK] += dot_nn(p, g[i])
                dq[i] = dq[i] + dot_tn(k, ds)
        for i in range(2):
            grad = jnp.transpose(dq[i]) * SCALE
            for h in range(GROUP):
                dq_acc[e, i * BLK : (i + 1) * BLK, h * HEAD : (h + 1) * HEAD] = grad[
                    h * BLK : (h + 1) * BLK
                ]

    visit(x_ref[0], 0, own=True)
    visit(x_ref[1], 1)

    @pl.loop(0, 2)
    def _(e):
        visit(y_ref[e], e + 2)

    dq_out[...] = dq_acc[:2]
    dq_core_out[...] = dq_acc[2:]
    for j, factor in ((slice(0, 2 * BLK), SCALE), (slice(2 * BLK, 4 * BLK), 1.0)):
        own_out[:, j] = acc[:NEAR, j] * factor
        p_out[:, j] = (acc[NEAR : 2 * NEAR, j] * factor).astype(BF16)
        m_out[:, j] = (acc[2 * NEAR : 3 * NEAR, j] * factor).astype(BF16)
        e_out[j] = (acc[3 * NEAR, j] * factor).astype(BF16)


def in_terms(x, lanes):
    out = jnp.zeros(lanes.shape, F32)
    for h in range(GROUP):
        rest = x[h]
        for n in range(3):
            term = rest.astype(BF16).astype(F32)
            out = jnp.where(lanes == 8 * n + h, term, out)
            rest = rest - term
    return out


def pack_keys(pos, k_ref, v_ref, out):
    start = pl.multiple_of(jnp.where(pos[0] > pos[BLK], BLK, 0), BLK)
    other = pl.multiple_of(BLK - start, BLK)
    out[:BLK] = k_ref[pl.ds(start, BLK), :]
    out[BLK : 2 * BLK] = k_ref[pl.ds(other, BLK), :]
    out[2 * BLK : 3 * BLK] = v_ref[pl.ds(start, BLK), :]
    out[3 * BLK : 4 * BLK] = v_ref[pl.ds(other, BLK), :]
    c = jnp.minimum(pos[0], pos[BLK]) // BLK
    out[4 * BLK :] = jnp.full((16, HEAD), c, jnp.int32).astype(F32).astype(BF16)


def pack_queries(pos, q_ref, lse_ref, o_ref, g_ref, q_out, g_out):
    wide = GROUP * HEAD
    swapped = pos[0] > pos[BLK]
    start = pl.multiple_of(jnp.where(swapped, BLK, 0), BLK)
    lanes = lax.broadcasted_iota(jnp.int32, (BLK, HEAD), 1)
    c = jnp.minimum(pos[0], pos[BLK]) // BLK
    for i in range(2):
        rows = pl.ds(start if i == 0 else pl.multiple_of(BLK - start, BLK), BLK)
        q_out[i * BLK : (i + 1) * BLK, :wide] = q_ref[rows, :]
        lse = lse_ref[rows, :]
        tail = in_terms([lse[:, h : h + 1] for h in range(GROUP)], lanes)
        tail = jnp.where(lanes == 24, c.astype(F32), tail)
        tail = jnp.where(lanes == 25, swapped.astype(F32), tail)
        q_out[i * BLK : (i + 1) * BLK, wide:] = tail.astype(BF16)
    n_heads = g_ref.shape[1] // wide
    lanes = lax.broadcasted_iota(jnp.int32, (g_ref.shape[0], HEAD), 1)
    for d in range(n_heads):
        g = g_ref[:, d * wide : (d + 1) * wide]
        product = g.astype(F32) * o_ref[:, d * wide : (d + 1) * wide].astype(F32)
        delta = [
            jnp.sum(product[:, h * HEAD : (h + 1) * HEAD], axis=1, keepdims=True)
            for h in range(GROUP)
        ]
        tail = in_terms(delta, lanes).astype(BF16)
        for twin in range(2):
            g_out[twin * n_heads + d, :, :wide] = g
            g_out[twin * n_heads + d, :, wide:] = tail


def join(info, own_ref, other_ref, grad_ref, after_ref, x_ref):
    wide = (GROUP + 1) * HEAD
    x_ref[0, :, :wide] = own_ref[...]
    x_ref[1, :, :wide] = other_ref[...]
    x_ref[0, :, wide:] = grad_ref[info[0]]
    x_ref[1, :, wide:] = grad_ref[1 - info[0]]


def narrow(dq_ref, after_ref, out):
    out[...] = dq_ref[...].astype(BF16)


HEADS = ("xl", "y")


def shifted(x, by):
    n = lax.axis_size("z")
    return lax.ppermute(x, "z", [(i, (i + by) % n) for i in range(n)])


def by_parity(x, even):
    n = lax.axis_size("z")
    return lax.ppermute(x, "z", [(i, (i + (even if i % 2 == 0 else -even)) % n) for i in range(n)])


def swapped_with(x, axis):
    return lax.ppermute(x, axis, [(0, 1), (1, 0)])


def local_call(body, out_shape, mib, name):
    vmem, smem = pl.BlockSpec(memory_space=pltpu.VMEM), pl.BlockSpec(memory_space=pltpu.SMEM)

    def call(*args, scratch=()):
        return pl.pallas_call(
            body,
            out_shape=out_shape,
            in_specs=[smem if a.dtype == jnp.int32 else vmem for a in args],
            out_specs=jax.tree.map(lambda _: vmem, out_shape),
            scratch_shapes=scratch,
            compiler_params=pltpu.CompilerParams(vmem_limit_bytes=mib * 1024 * 1024),
            name=name,
        )(*args)

    return call


def shards(queries, keys, values, outputs, out_grad, lse, positions):
    n_heads = lax.axis_size(HEADS)
    even = lax.axis_index("z") % 2 == 0
    swapped = positions[0] > positions[BLK]
    wide = (GROUP + 1) * HEAD
    like = jax.ShapeDtypeStruct

    def early_then_late(x):
        return jnp.where(swapped, jnp.concatenate([x[BLK:], x[:BLK]]), x)

    own = local_call(pack_keys, like((4 * BLK + 16, HEAD), BF16), 4, "pack_keys")(
        positions, keys, values
    )
    far = [shifted(own, by) for by in (6, -6, 3, -3)]
    s_set = jnp.stack([own] + far)
    p_set, m_set = shifted(s_set, 1), shifted(s_set, -1)
    e_one = by_parity(jnp.where(even, far[1], far[0]), -2)

    own_q, send = local_call(
        pack_queries,
        (like((TOK, wide), BF16), like((2 * n_heads, TOK // n_heads, wide), BF16)),
        8,
        "pack_queries",
    )(positions, queries, lse, outputs, out_grad)
    grad = lax.all_to_all(send, ("xh",) + HEADS, split_axis=0, concat_axis=0, tiled=True)
    other_q = swapped_with(own_q, "xh")
    info = lax.axis_index("xh").astype(jnp.int32).reshape(1)
    x = local_call(join, like((2, TOK, 2 * wide), BF16), 4, "join")(
        info, own_q, other_q, grad.reshape(2, TOK, wide), far[2]
    )
    y = swapped_with(x, "core")

    five, one = (NEAR, 4 * BLK, HEAD), (4 * BLK, HEAD)
    dq_shape = (2, TOK, GROUP * HEAD)
    own_g, p_g, m_g, e_g, dq, dq_core = local_call(
        backward,
        (
            like(five, F32),
            like(five, BF16),
            like(five, BF16),
            like(one, BF16),
            like(dq_shape, F32),
            like(dq_shape, F32),
        ),
        20,
        "backward",
    )(
        x,
        y,
        s_set,
        p_set,
        m_set,
        e_one,
        scratch=[
            pltpu.VMEM((3 * NEAR + 1, 4 * BLK + 16, HEAD), BF16),
            pltpu.VMEM((3 * NEAR + 1,) + one, F32),
            pltpu.VMEM((4, TOK, GROUP * HEAD), F32),
        ],
    )

    p_in, m_in = shifted(p_g, -1), shifted(m_g, 1)
    e_in = by_parity(e_g, 2).astype(F32)
    total = own_g + p_in.astype(F32) + m_in.astype(F32)
    parts = [
        total[1] + jnp.where(even, 0.0, e_in),
        total[2] + jnp.where(even, e_in, 0.0),
        total[3],
        total[4],
    ]
    mine = total[0]
    for part, by in zip(parts, (-6, 6, -3, 3)):
        mine = mine + shifted(part.astype(BF16), by).astype(F32)

    dq_core = local_call(narrow, like(dq_shape, BF16), 4, "narrow")(dq_core, m_in)
    dq = dq + swapped_with(dq_core, "core").astype(F32)
    dq = dq[0] + swapped_with(dq[1].astype(BF16), "xh").astype(F32)
    return (
        early_then_late(dq).astype(BF16),
        early_then_late(mine[:TOK]).astype(BF16),
        early_then_late(mine[TOK:]).astype(BF16),
    )


def solution(mesh):
    shape = FOLD or (2, 16, 2, 2, 4)
    split = jax.sharding.Mesh(mesh.devices.reshape(shape), ("xh", "z", "core", "xl", "y"))
    ctx, heads = ("xh", "z", "core"), ("xl", "y")
    return jax.shard_map(
        shards,
        mesh=split,
        in_specs=(
            P(ctx, heads),
            P(ctx, heads),
            P(ctx, heads),
            P(ctx + heads, None),
            P(ctx + heads, None),
            P(ctx, heads),
            P(ctx),
        ),
        out_specs=(P(ctx, heads), P(ctx, heads), P(ctx, heads)),
        check_vma=False,
    )
```

```python
import math

import jax
import jax.numpy as jnp
from jax import lax
from jax.experimental import pallas as pl
from jax.experimental.pallas import tpu as pltpu
from jax.sharding import PartitionSpec as P

HEAD = 128
BLK = 64
TOK = 2 * BLK
GROUP = 4
ROWS = GROUP * BLK
NEAR = 3
LOG2E = math.log2(math.e)
SCALE = 1.0 / math.sqrt(HEAD)
FAR = 1e30
F32 = jnp.float32
BF16 = jnp.bfloat16
FOLD = None


def dot_nt(a, b):
    return lax.dot_general(a, b, (((1,), (1,)), ((), ())), preferred_element_type=F32)


def dot_nn(a, b):
    return lax.dot_general(a, b, (((1,), (0,)), ((), ())), preferred_element_type=F32)


def dot_tn(a, b):
    return lax.dot_general(a, b, (((0,), (0,)), ((), ())), preferred_element_type=F32)


def backward(x_ref, y_ref, kv, acc, dq_acc, tiles, own):
    seen = lax.broadcasted_iota(jnp.int32, (BLK, ROWS), 0) <= (
        lax.broadcasted_iota(jnp.int32, (BLK, ROWS), 1) % BLK
    )

    def grads(scores, dprob, lse, delta):
        probs = jnp.exp2(scores * (SCALE * LOG2E) - lse)
        dscore = probs * (dprob - delta)
        return probs.astype(BF16), dscore.astype(BF16)

    def row_vectors(table):
        return [
            jnp.concatenate([table[h : h + 1, s : s + BLK] for h in range(GROUP)], axis=1)
            for s in (0, BLK)
        ]

    def half_rows(block):
        return [
            jnp.concatenate(
                [block[s : s + BLK, h * HEAD : (h + 1) * HEAD] for h in range(GROUP)], axis=0
            )
            for s in (0, BLK)
        ]

    def query_side(block):
        wide = GROUP * HEAD
        tail = jnp.transpose(block[:, wide : wide + HEAD].astype(F32))
        lse = tail[0:8, :] + tail[8:16, :] + tail[16:24, :]
        c_row, swapped = tail[24:25, :], tail[25:26, :] > 0.5
        tail = jnp.transpose(block[:, 2 * wide + HEAD :].astype(F32))
        delta = tail[0:8, :] + tail[8:16, :] + tail[16:24, :]
        d0, d1 = row_vectors(delta)
        g0, g1 = half_rows(block[:, wide + HEAD : 2 * wide + HEAD])
        two = jnp.concatenate([swapped, swapped], axis=1)
        tall = jnp.broadcast_to(swapped, (ROWS, HEAD))
        return (
            c_row,
            row_vectors(lse * LOG2E),
            (jnp.where(two, d1, d0), jnp.where(two, d0, d1)),
            half_rows(block[:, :wide]),
            (jnp.where(tall, g1, g0), jnp.where(tall, g0, g1)),
        )

    def flat(x):
        return x.reshape(x.shape[0] * x.shape[1], x.shape[2])

    def visit(block, e, own=False):
        own_c, lse, delta, q, g = query_side(block)
        (lse_early, lse_late), (delta_early, delta_late) = lse, delta
        q_late, g_late = q[1], g[1]
        q_both = jnp.concatenate(q, axis=1)
        g_both = jnp.concatenate(g, axis=1)
        dq_a = jnp.zeros((HEAD, ROWS), F32)
        dq_b = jnp.zeros((2 * HEAD, ROWS), F32)
        for first, last in tiles:
            size = last - first

            def pick(j):
                return kv[first:last, j * BLK : (j + 1) * BLK]

            c = kv[first:last, 4 * BLK : 4 * BLK + 16].astype(F32)[:, 0:1, :]
            before = c < own_c[None]
            after = c > own_c[None]
            wide = jnp.broadcast_to(before, (size, BLK, HEAD))
            k_early, k_late, v_early, v_late = [pick(j) for j in range(4)]
            k_both = jnp.concatenate(
                [flat(jnp.where(wide, k_early, 0)), flat(jnp.where(wide, 0, k_late))], axis=1
            )
            v_both = jnp.concatenate(
                [flat(jnp.where(wide, v_early, 0)), flat(jnp.where(wide, 0, v_late))], axis=1
            )
            k_early, v_early = flat(k_early), flat(v_early)
            before2 = jnp.concatenate([before, before], axis=2)
            after2 = jnp.concatenate([after, after], axis=2)
            lse_b = jnp.where(before2, lse_early[None], jnp.where(after2, lse_late[None], FAR))
            delta_b = jnp.where(before2, delta_early[None], delta_late[None])
            lse_b = jnp.broadcast_to(lse_b, (size, BLK, ROWS)).reshape(size * BLK, ROWS)
            delta_b = jnp.broadcast_to(delta_b, (size, BLK, ROWS)).reshape(size * BLK, ROWS)

            p_a, ds_a = grads(
                dot_nt(k_early, q_late), dot_nt(v_early, g_late), lse_late, delta_late
            )
            p_b, ds_b = grads(dot_nt(k_both, q_both), dot_nt(v_both, g_both), lse_b, delta_b)
            dv_a, dk_a = dot_nn(p_a, g_late), dot_nn(ds_a, q_late)
            dv_b, dk_b = dot_nn(p_b, g_both), dot_nn(ds_b, q_both)
            dq_a = dq_a + dot_tn(k_early, ds_a)
            dq_b = dq_b + dot_tn(k_both, ds_b)
            for j, one, two in ((0, dk_a, dk_b), (2, dv_a, dv_b)):
                one = one.reshape(size, BLK, HEAD)
                two = two.reshape(size, BLK, 2 * HEAD)
                acc[first:last, j * BLK : (j + 1) * BLK] += one + jnp.where(wide, two[:, :, :HEAD], 0.0)
                acc[first:last, (j + 1) * BLK : (j + 2) * BLK] += jnp.where(
                    wide, 0.0, two[:, :, HEAD:]
                )
        dq = [dq_b[:HEAD], dq_b[HEAD:] + dq_a]
        if own:
            for i in range(2):
                at = slice(i * BLK, (i + 1) * BLK)
                k, v = kv[0, at], kv[0, (2 + i) * BLK : (3 + i) * BLK]
                scores = jnp.where(seen, dot_nt(k, q[i]), -FAR)
                p, ds = grads(scores, dot_nt(v, g[i]), lse[i], delta[i])
                acc[0, at] += dot_nn(ds, q[i])
                acc[0, (2 + i) * BLK : (3 + i) * BLK] += dot_nn(p, g[i])
                dq[i] = dq[i] + dot_tn(k, ds)
        for i in range(2):
            grad = jnp.transpose(dq[i]) * SCALE
            for h in range(GROUP):
                dq_acc[e, i * BLK : (i + 1) * BLK, h * HEAD : (h + 1) * HEAD] += grad[
                    h * BLK : (h + 1) * BLK
                ]

    acc[...] = jnp.zeros_like(acc)
    visit(x_ref[0], 0, own=own)
    visit(x_ref[1], 1)

    @pl.loop(0, 2)
    def _(e):
        visit(y_ref[e], e + 2)


def scaled(acc, rows):
    return jnp.concatenate([acc[rows, : 2 * BLK] * SCALE, acc[rows, 2 * BLK :]], axis=-2)


def with_nearest(x_ref, y_ref, s_ref, p_ref, m_ref, e_ref, *rest):
    own_out, p_out, m_out, e_out, dq_out, kv, acc = rest
    kv[:NEAR] = s_ref[...]
    kv[NEAR : 2 * NEAR] = p_ref[...]
    kv[2 * NEAR : 3 * NEAR] = m_ref[...]
    kv[3 * NEAR] = e_ref[...]
    dq_out[...] = jnp.zeros_like(dq_out)
    backward(x_ref, y_ref, kv, acc, dq_out, ((0, 5), (5, 10)), True)
    own_out[...] = scaled(acc, slice(0, NEAR))
    p_out[...] = scaled(acc, slice(NEAR, 2 * NEAR)).astype(BF16)
    m_out[...] = scaled(acc, slice(2 * NEAR, 3 * NEAR)).astype(BF16)
    e_out[...] = scaled(acc, 3 * NEAR).astype(BF16)


def with_next(x_ref, y_ref, p_ref, m_ref, dq_ref, *rest):
    p_out, m_out, dq_out, dq_core_out, kv, acc, dq = rest
    kv[:NEAR] = p_ref[...]
    kv[NEAR:] = m_ref[...]
    dq[...] = dq_ref[...]
    backward(x_ref, y_ref, kv, acc, dq, ((0, 3), (3, 6)), False)
    p_out[...] = scaled(acc, slice(0, NEAR)).astype(BF16)
    m_out[...] = scaled(acc, slice(NEAR, 2 * NEAR)).astype(BF16)
    dq_out[...] = dq[:2]
    dq_core_out[...] = dq[2:].astype(BF16)


def in_terms(x, lanes):
    out = jnp.zeros(lanes.shape, F32)
    for h in range(GROUP):
        rest = x[h]
        for n in range(3):
            term = rest.astype(BF16).astype(F32)
            out = jnp.where(lanes == 8 * n + h, term, out)
            rest = rest - term
    return out


def pack_keys(pos, k_ref, v_ref, out):
    start = pl.multiple_of(jnp.where(pos[0] > pos[BLK], BLK, 0), BLK)
    other = pl.multiple_of(BLK - start, BLK)
    out[:BLK] = k_ref[pl.ds(start, BLK), :]
    out[BLK : 2 * BLK] = k_ref[pl.ds(other, BLK), :]
    out[2 * BLK : 3 * BLK] = v_ref[pl.ds(start, BLK), :]
    out[3 * BLK : 4 * BLK] = v_ref[pl.ds(other, BLK), :]
    c = jnp.minimum(pos[0], pos[BLK]) // BLK
    out[4 * BLK :] = jnp.full((16, HEAD), c, jnp.int32).astype(F32).astype(BF16)


def pack_queries(pos, q_ref, lse_ref, o_ref, g_ref, q_out, g_out):
    wide = GROUP * HEAD
    swapped = pos[0] > pos[BLK]
    start = pl.multiple_of(jnp.where(swapped, BLK, 0), BLK)
    lanes = lax.broadcasted_iota(jnp.int32, (BLK, HEAD), 1)
    c = jnp.minimum(pos[0], pos[BLK]) // BLK
    for i in range(2):
        rows = pl.ds(start if i == 0 else pl.multiple_of(BLK - start, BLK), BLK)
        q_out[i * BLK : (i + 1) * BLK, :wide] = q_ref[rows, :]
        lse = lse_ref[rows, :]
        tail = in_terms([lse[:, h : h + 1] for h in range(GROUP)], lanes)
        tail = jnp.where(lanes == 24, c.astype(F32), tail)
        tail = jnp.where(lanes == 25, swapped.astype(F32), tail)
        q_out[i * BLK : (i + 1) * BLK, wide:] = tail.astype(BF16)
    n_heads = g_ref.shape[1] // wide
    lanes = lax.broadcasted_iota(jnp.int32, (g_ref.shape[0], HEAD), 1)
    for d in range(n_heads):
        g = g_ref[:, d * wide : (d + 1) * wide]
        product = g.astype(F32) * o_ref[:, d * wide : (d + 1) * wide].astype(F32)
        delta = [
            jnp.sum(product[:, h * HEAD : (h + 1) * HEAD], axis=1, keepdims=True)
            for h in range(GROUP)
        ]
        tail = in_terms(delta, lanes).astype(BF16)
        for twin in range(2):
            g_out[twin * n_heads + d, :, :wide] = g
            g_out[twin * n_heads + d, :, wide:] = tail


def join(info, own_ref, plus_ref, minus_ref, q_ref, qx_ref, grad_ref, s_out, e_out, x_out):
    s_out[0] = own_ref[...]
    s_out[1] = plus_ref[...]
    s_out[2] = minus_ref[...]
    e_out[...] = jnp.where(info[1] == 0, minus_ref[...], plus_ref[...])
    wide = (GROUP + 1) * HEAD
    x_out[0, :, :wide] = q_ref[...]
    x_out[1, :, :wide] = qx_ref[...]
    x_out[0, :, wide:] = grad_ref[info[0]]
    x_out[1, :, wide:] = grad_ref[1 - info[0]]


def sum_near(info, own_ref, p1, m1, p2, m2, e_ref, dq_ref, core_ref, *outs):
    own_out, plus_out, minus_out, dq_out, dqx_out = outs
    extra = e_ref[...].astype(F32)
    even = info[1] == 0
    for i, out in enumerate((own_out, plus_out, minus_out)):
        total = own_ref[i]
        for ref in (p1, m1, p2, m2):
            total = total + ref[i].astype(F32)
        if i:
            total = total + jnp.where(even == (i == 2), extra, 0.0)
        out[...] = total.astype(out.dtype)
    dq_out[...] = dq_ref[0] + core_ref[0].astype(F32)
    dqx_out[...] = (dq_ref[1] + core_ref[1].astype(F32)).astype(BF16)


def finish(pos, own_ref, plus_ref, minus_ref, dq_ref, dqx_ref, q_out, k_out, v_out):
    start = pl.multiple_of(jnp.where(pos[0] > pos[BLK], BLK, 0), BLK)
    total = own_ref[...] + plus_ref[...].astype(F32) + minus_ref[...].astype(F32)
    dq = dq_ref[...] + dqx_ref[...].astype(F32)
    for i in range(2):
        rows = pl.ds(start if i == 0 else pl.multiple_of(BLK - start, BLK), BLK)
        q_out[rows, :] = dq[i * BLK : (i + 1) * BLK].astype(BF16)
        k_out[rows, :] = total[i * BLK : (i + 1) * BLK].astype(BF16)
        v_out[rows, :] = total[(2 + i) * BLK : (3 + i) * BLK].astype(BF16)


HEADS = ("xl", "y")


def shifted(x, by):
    n = lax.axis_size("z")
    return lax.ppermute(x, "z", [(i, (i + by) % n) for i in range(n)])


def by_parity(x, even):
    n = lax.axis_size("z")
    return lax.ppermute(x, "z", [(i, (i + (even if i % 2 == 0 else -even)) % n) for i in range(n)])


def swapped_with(x, axis):
    return lax.ppermute(x, axis, [(0, 1), (1, 0)])


def local_call(body, out_shape, mib, stream_in=False, stream_out=False):
    vmem, smem = pl.BlockSpec(memory_space=pltpu.VMEM), pl.BlockSpec(memory_space=pltpu.SMEM)
    free = pl.BlockSpec()

    def call(*args, scratch=()):
        return pl.pallas_call(
            body,
            out_shape=out_shape,
            in_specs=[
                smem if a.dtype == jnp.int32 else free if stream_in else vmem for a in args
            ],
            out_specs=jax.tree.map(lambda _: free if stream_out else vmem, out_shape),
            scratch_shapes=scratch,
            compiler_params=pltpu.CompilerParams(vmem_limit_bytes=mib * 1024 * 1024),
            name=body.__name__,
        )(*args)

    return call


def shards(queries, keys, values, outputs, out_grad, lse, positions):
    n_heads = lax.axis_size(HEADS)
    wide = (GROUP + 1) * HEAD
    info = jnp.stack([lax.axis_index("xh"), lax.axis_index("z") % 2]).astype(jnp.int32)

    def like(shape, dtype=BF16):
        return jax.ShapeDtypeStruct(shape, dtype)

    packed, block = (4 * BLK + 16, HEAD), (4 * BLK, HEAD)
    own = local_call(pack_keys, like(packed), 56, stream_in=True)(positions, keys, values)
    plus, minus = shifted(own, -5), shifted(own, 5)

    own_q, send = local_call(
        pack_queries,
        (like((TOK, wide)), like((2 * n_heads, TOK // n_heads, wide))),
        56,
        stream_in=True,
    )(positions, queries, lse, outputs, out_grad)
    grad = lax.all_to_all(send, ("xh",) + HEADS, split_axis=0, concat_axis=0, tiled=True)
    other_q = swapped_with(own_q, "xh")
    s_set, e_one, x = local_call(
        join, (like((NEAR,) + packed), like(packed), like((2, TOK, 2 * wide))), 8, stream_in=True
    )(info, own, plus, minus, own_q, other_q, grad.reshape(2, TOK, wide))
    p1, m1, p2, m2 = [shifted(s_set, by) for by in (1, -1, 2, -2)]
    e_one = by_parity(e_one, 3)
    y = swapped_with(x, "core")

    near, dq_shape = (NEAR,) + block, (2, TOK, GROUP * HEAD)
    own_g, p1_g, m1_g, e_g, dq = local_call(
        with_nearest,
        (
            like(near, F32),
            like(near),
            like(near),
            like(block),
            like((4,) + dq_shape[1:], F32),
        ),
        16,
    )(
        x,
        y,
        s_set,
        p1,
        m1,
        e_one,
        scratch=[
            pltpu.VMEM((3 * NEAR + 1,) + packed, BF16),
            pltpu.VMEM((3 * NEAR + 1,) + block, F32),
        ],
    )
    p2_g, m2_g, dq, dq_core = local_call(
        with_next, (like(near), like(near), like(dq_shape, F32), like(dq_shape)), 16
    )(
        x,
        y,
        p2,
        m2,
        dq,
        scratch=[
            pltpu.VMEM((2 * NEAR,) + packed, BF16),
            pltpu.VMEM((2 * NEAR,) + block, F32),
            pltpu.VMEM((4,) + dq_shape[1:], F32),
        ],
    )

    p1_in, m1_in, e_in = shifted(p1_g, -1), shifted(m1_g, 1), by_parity(e_g, 3)
    p2_in, m2_in = shifted(p2_g, -2), shifted(m2_g, 2)
    dq_core = swapped_with(dq_core, "core")
    own_g, plus_g, minus_g, dq, dqx = local_call(
        sum_near,
        (
            like(block, F32),
            like(block),
            like(block),
            like(dq_shape[1:], F32),
            like(dq_shape[1:]),
        ),
        8,
    )(info, own_g, p1_in, m1_in, p2_in, m2_in, e_in, dq, dq_core)
    plus_g, minus_g = shifted(plus_g, 5), shifted(minus_g, -5)
    dqx = swapped_with(dqx, "xh")
    return local_call(
        finish,
        (like(queries.shape), like(keys.shape), like(values.shape)),
        8,
        stream_out=True,
    )(positions, own_g, plus_g, minus_g, dq, dqx)


def solution(mesh):
    shape = FOLD or (2, 16, 2, 2, 4)
    split = jax.sharding.Mesh(mesh.devices.reshape(shape), ("xh", "z", "core", "xl", "y"))
    ctx, heads = ("xh", "z", "core"), ("xl", "y")
    return jax.shard_map(
        shards,
        mesh=split,
        in_specs=(
            P(ctx, heads),
            P(ctx, heads),
            P(ctx, heads),
            P(ctx + heads, None),
            P(ctx + heads, None),
            P(ctx, heads),
            P(ctx),
        ),
        out_specs=(P(ctx, heads), P(ctx, heads), P(ctx, heads)),
        check_vma=False,
    )
```

```python
import math

import jax
import jax.numpy as jnp
from jax import lax
from jax.experimental import pallas as pl
from jax.experimental.pallas import tpu as pltpu
from jax.sharding import PartitionSpec as P

HEAD = 128
BLK = 64
TOK = 2 * BLK
GROUP = 4
ROWS = GROUP * BLK
NEAR = 3
LOG2E = math.log2(math.e)
SCALE = 1.0 / math.sqrt(HEAD)
FAR = 1e30
F32 = jnp.float32
BF16 = jnp.bfloat16
FOLD = None


def dot_nt(a, b):
    return lax.dot_general(a, b, (((1,), (1,)), ((), ())), preferred_element_type=F32)


def dot_nn(a, b):
    return lax.dot_general(a, b, (((1,), (0,)), ((), ())), preferred_element_type=F32)


def dot_tn(a, b):
    return lax.dot_general(a, b, (((0,), (0,)), ((), ())), preferred_element_type=F32)


def backward(x_ref, y_ref, kv, acc, dq_acc, tiles, own):
    seen = lax.broadcasted_iota(jnp.int32, (BLK, ROWS), 0) <= (
        lax.broadcasted_iota(jnp.int32, (BLK, ROWS), 1) % BLK
    )

    def grads(scores, dprob, lse, delta):
        probs = jnp.exp2(scores * (SCALE * LOG2E) - lse)
        dscore = probs * (dprob - delta)
        return probs.astype(BF16), dscore.astype(BF16)

    def row_vectors(table):
        return [
            jnp.concatenate([table[h : h + 1, s : s + BLK] for h in range(GROUP)], axis=1)
            for s in (0, BLK)
        ]

    def half_rows(block):
        return [
            jnp.concatenate(
                [block[s : s + BLK, h * HEAD : (h + 1) * HEAD] for h in range(GROUP)], axis=0
            )
            for s in (0, BLK)
        ]

    def query_side(block):
        wide = GROUP * HEAD
        tail = jnp.transpose(block[:, wide : wide + HEAD].astype(F32))
        lse = tail[0:8, :] + tail[8:16, :] + tail[16:24, :]
        c_row, swapped = tail[24:25, :], tail[25:26, :] > 0.5
        tail = jnp.transpose(block[:, 2 * wide + HEAD :].astype(F32))
        delta = tail[0:8, :] + tail[8:16, :] + tail[16:24, :]
        d0, d1 = row_vectors(delta)
        g0, g1 = half_rows(block[:, wide + HEAD : 2 * wide + HEAD])
        two = jnp.concatenate([swapped, swapped], axis=1)
        tall = jnp.broadcast_to(swapped, (ROWS, HEAD))
        return (
            c_row,
            row_vectors(lse * LOG2E),
            (jnp.where(two, d1, d0), jnp.where(two, d0, d1)),
            half_rows(block[:, :wide]),
            (jnp.where(tall, g1, g0), jnp.where(tall, g0, g1)),
        )

    def flat(x):
        return x.reshape(x.shape[0] * x.shape[1], x.shape[2])

    def visit(block, e, own=False):
        own_c, lse, delta, q, g = query_side(block)
        (lse_early, lse_late), (delta_early, delta_late) = lse, delta
        q_late, g_late = q[1], g[1]
        q_both = jnp.concatenate(q, axis=1)
        g_both = jnp.concatenate(g, axis=1)
        dq_a = jnp.zeros((HEAD, ROWS), F32)
        dq_b = jnp.zeros((2 * HEAD, ROWS), F32)
        for first, last in tiles:
            size = last - first

            def pick(j):
                return kv[first:last, j * BLK : (j + 1) * BLK]

            c = kv[first:last, 4 * BLK : 4 * BLK + 16].astype(F32)[:, 0:1, :]
            before = c < own_c[None]
            after = c > own_c[None]
            wide = jnp.broadcast_to(before, (size, BLK, HEAD))
            k_early, k_late, v_early, v_late = [pick(j) for j in range(4)]
            k_both = jnp.concatenate(
                [flat(jnp.where(wide, k_early, 0)), flat(jnp.where(wide, 0, k_late))], axis=1
            )
            v_both = jnp.concatenate(
                [flat(jnp.where(wide, v_early, 0)), flat(jnp.where(wide, 0, v_late))], axis=1
            )
            k_early, v_early = flat(k_early), flat(v_early)
            before2 = jnp.concatenate([before, before], axis=2)
            after2 = jnp.concatenate([after, after], axis=2)
            lse_b = jnp.where(before2, lse_early[None], jnp.where(after2, lse_late[None], FAR))
            delta_b = jnp.where(before2, delta_early[None], delta_late[None])
            lse_b = jnp.broadcast_to(lse_b, (size, BLK, ROWS)).reshape(size * BLK, ROWS)
            delta_b = jnp.broadcast_to(delta_b, (size, BLK, ROWS)).reshape(size * BLK, ROWS)

            p_a, ds_a = grads(
                dot_nt(k_early, q_late), dot_nt(v_early, g_late), lse_late, delta_late
            )
            p_b, ds_b = grads(dot_nt(k_both, q_both), dot_nt(v_both, g_both), lse_b, delta_b)
            dv_a, dk_a = dot_nn(p_a, g_late), dot_nn(ds_a, q_late)
            dv_b, dk_b = dot_nn(p_b, g_both), dot_nn(ds_b, q_both)
            dq_a = dq_a + dot_tn(k_early, ds_a)
            dq_b = dq_b + dot_tn(k_both, ds_b)
            for j, one, two in ((0, dk_a, dk_b), (2, dv_a, dv_b)):
                one = one.reshape(size, BLK, HEAD)
                two = two.reshape(size, BLK, 2 * HEAD)
                acc[first:last, j * BLK : (j + 1) * BLK] += one + jnp.where(wide, two[:, :, :HEAD], 0.0)
                acc[first:last, (j + 1) * BLK : (j + 2) * BLK] += jnp.where(
                    wide, 0.0, two[:, :, HEAD:]
                )
        dq = [dq_b[:HEAD], dq_b[HEAD:] + dq_a]
        if own:
            for i in range(2):
                at = slice(i * BLK, (i + 1) * BLK)
                k, v = kv[0, at], kv[0, (2 + i) * BLK : (3 + i) * BLK]
                scores = jnp.where(seen, dot_nt(k, q[i]), -FAR)
                p, ds = grads(scores, dot_nt(v, g[i]), lse[i], delta[i])
                acc[0, at] += dot_nn(ds, q[i])
                acc[0, (2 + i) * BLK : (3 + i) * BLK] += dot_nn(p, g[i])
                dq[i] = dq[i] + dot_tn(k, ds)
        for i in range(2):
            grad = jnp.transpose(dq[i]) * SCALE
            for h in range(GROUP):
                dq_acc[e, i * BLK : (i + 1) * BLK, h * HEAD : (h + 1) * HEAD] += grad[
                    h * BLK : (h + 1) * BLK
                ]

    acc[...] = jnp.zeros_like(acc)
    visit(x_ref[0], 0, own=own)
    visit(x_ref[1], 1)

    @pl.loop(0, 2)
    def _(e):
        visit(y_ref[e], e + 2)


def scaled(acc, rows):
    return jnp.concatenate([acc[rows, : 2 * BLK] * SCALE, acc[rows, 2 * BLK :]], axis=-2)


def with_nearest(x_ref, y_ref, s_ref, p_ref, m_ref, e_ref, *rest):
    own_out, p_out, m_out, e_out, dq_out, kv, acc = rest
    kv[:NEAR] = s_ref[...]
    kv[NEAR : 2 * NEAR] = p_ref[...]
    kv[2 * NEAR : 3 * NEAR] = m_ref[...]
    kv[3 * NEAR] = e_ref[...]
    dq_out[...] = jnp.zeros_like(dq_out)
    backward(x_ref, y_ref, kv, acc, dq_out, ((0, 5), (5, 10)), True)
    own_out[...] = scaled(acc, slice(0, NEAR))
    p_out[...] = scaled(acc, slice(NEAR, 2 * NEAR)).astype(BF16)
    m_out[...] = scaled(acc, slice(2 * NEAR, 3 * NEAR)).astype(BF16)
    e_out[...] = scaled(acc, 3 * NEAR).astype(BF16)


def with_next(x_ref, y_ref, p_ref, m_ref, dq_ref, *rest):
    p_out, m_out, dq_out, dq_core_out, kv, acc, dq = rest
    kv[:NEAR] = p_ref[...]
    kv[NEAR:] = m_ref[...]
    dq[...] = dq_ref[...]
    backward(x_ref, y_ref, kv, acc, dq, ((0, 3), (3, 6)), False)
    p_out[...] = scaled(acc, slice(0, NEAR)).astype(BF16)
    m_out[...] = scaled(acc, slice(NEAR, 2 * NEAR)).astype(BF16)
    dq_out[...] = dq[:2]
    dq_core_out[...] = dq[2:].astype(BF16)


def in_terms(x, lanes):
    out = jnp.zeros(lanes.shape, F32)
    for h in range(GROUP):
        rest = x[h]
        for n in range(3):
            term = rest.astype(BF16).astype(F32)
            out = jnp.where(lanes == 8 * n + h, term, out)
            rest = rest - term
    return out


def pack_keys(pos, k_ref, v_ref, out):
    start = pl.multiple_of(jnp.where(pos[0] > pos[BLK], BLK, 0), BLK)
    other = pl.multiple_of(BLK - start, BLK)
    out[:BLK] = k_ref[pl.ds(start, BLK), :]
    out[BLK : 2 * BLK] = k_ref[pl.ds(other, BLK), :]
    out[2 * BLK : 3 * BLK] = v_ref[pl.ds(start, BLK), :]
    out[3 * BLK : 4 * BLK] = v_ref[pl.ds(other, BLK), :]
    c = jnp.minimum(pos[0], pos[BLK]) // BLK
    out[4 * BLK :] = jnp.full((16, HEAD), c, jnp.int32).astype(F32).astype(BF16)


def pack_queries(pos, q_ref, lse_ref, o_ref, g_ref, q_out, g_out):
    wide = GROUP * HEAD
    swapped = pos[0] > pos[BLK]
    start = pl.multiple_of(jnp.where(swapped, BLK, 0), BLK)
    lanes = lax.broadcasted_iota(jnp.int32, (BLK, HEAD), 1)
    c = jnp.minimum(pos[0], pos[BLK]) // BLK
    lse = jnp.concatenate([lse_ref[...], jnp.zeros((HEAD - GROUP, TOK), F32)])
    turned = jnp.transpose(lse)
    turned = jnp.where(swapped, jnp.concatenate([turned[BLK:], turned[:BLK]]), turned)
    for i in range(2):
        rows = pl.ds(start if i == 0 else pl.multiple_of(BLK - start, BLK), BLK)
        q_out[i * BLK : (i + 1) * BLK, :wide] = q_ref[rows, :]
        lse = turned[i * BLK : (i + 1) * BLK, :]
        tail = in_terms([lse[:, h : h + 1] for h in range(GROUP)], lanes)
        tail = jnp.where(lanes == 24, c.astype(F32), tail)
        tail = jnp.where(lanes == 25, swapped.astype(F32), tail)
        q_out[i * BLK : (i + 1) * BLK, wide:] = tail.astype(BF16)
    n_heads = g_ref.shape[1] // wide
    lanes = lax.broadcasted_iota(jnp.int32, (g_ref.shape[0], HEAD), 1)
    for d in range(n_heads):
        g = g_ref[:, d * wide : (d + 1) * wide]
        product = g.astype(F32) * o_ref[:, d * wide : (d + 1) * wide].astype(F32)
        delta = [
            jnp.sum(product[:, h * HEAD : (h + 1) * HEAD], axis=1, keepdims=True)
            for h in range(GROUP)
        ]
        tail = in_terms(delta, lanes).astype(BF16)
        for twin in range(2):
            g_out[twin * n_heads + d, :, :wide] = g
            g_out[twin * n_heads + d, :, wide:] = tail


def join(info, own_ref, u_ref, w_ref, q_ref, qx_ref, grad_ref, s_out, x_out):
    s_out[0] = own_ref[...]
    s_out[1] = u_ref[...]
    s_out[2] = w_ref[...]
    wide = (GROUP + 1) * HEAD
    x_out[0, :, :wide] = q_ref[...]
    x_out[1, :, :wide] = qx_ref[...]
    x_out[0, :, wide:] = grad_ref[info[0]]
    x_out[1, :, wide:] = grad_ref[1 - info[0]]


def sum_first(own_ref, a_ref, b_ref, c_ref, d_ref, own_out, c_out, d_out):
    own_out[...] = own_ref[...] + a_ref[...].astype(F32) + b_ref[...].astype(F32)
    c_out[...] = c_ref[...]
    d_out[...] = d_ref[...]


def sum_near(own_ref, c_ref, d_ref, e_ref, own_out, u_out, w_out):
    total = own_ref[...] + c_ref[...].astype(F32) + d_ref[...].astype(F32)
    own_out[...] = total[0]
    u_out[...] = total[1].astype(BF16)
    w_out[...] = (total[2] + e_ref[...].astype(F32)).astype(BF16)


def sum_cores(dq_ref, core_ref, dq_out, dqx_out):
    dq_out[...] = dq_ref[0] + core_ref[0].astype(F32)
    dqx_out[...] = (dq_ref[1] + core_ref[1].astype(F32)).astype(BF16)


def finish(info, own_ref, u_ref, w_ref, dq_ref, dqx_ref, q_out, k_out, v_out):
    start = pl.multiple_of(info[1] * BLK, BLK)
    total = own_ref[...] + u_ref[...].astype(F32) + w_ref[...].astype(F32)
    dq = dq_ref[...] + dqx_ref[...].astype(F32)
    for i in range(2):
        rows = pl.ds(start if i == 0 else pl.multiple_of(BLK - start, BLK), BLK)
        q_out[rows, :] = dq[i * BLK : (i + 1) * BLK].astype(BF16)
        k_out[rows, :] = total[i * BLK : (i + 1) * BLK].astype(BF16)
        v_out[rows, :] = total[(2 + i) * BLK : (3 + i) * BLK].astype(BF16)


HEADS = ("xl", "y")


def by_parity(x, distance):
    n = lax.axis_size("z")
    to = [(i + (distance if i % 2 == 0 else -distance)) % n for i in range(n)]
    return lax.ppermute(x, "z", list(enumerate(to)))


def swapped_with(x, axis):
    return lax.ppermute(x, axis, [(0, 1), (1, 0)])


def local_call(body, out_shape, mib, stream_in=False, stream_out=False):
    vmem, smem = pl.BlockSpec(memory_space=pltpu.VMEM), pl.BlockSpec(memory_space=pltpu.SMEM)
    free = pl.BlockSpec()

    def call(*args, scratch=()):
        return pl.pallas_call(
            body,
            out_shape=out_shape,
            in_specs=[
                smem if a.dtype == jnp.int32 else free if stream_in else vmem for a in args
            ],
            out_specs=jax.tree.map(lambda _: free if stream_out else vmem, out_shape),
            scratch_shapes=scratch,
            compiler_params=pltpu.CompilerParams(vmem_limit_bytes=mib * 1024 * 1024),
            name=body.__name__,
        )(*args)

    return call


def shards(queries, keys, values, outputs, out_grad, lse, positions):
    n_heads = lax.axis_size(HEADS)
    wide = (GROUP + 1) * HEAD
    swapped = positions[0] > positions[BLK]
    info = jnp.stack([lax.axis_index("xh"), swapped]).astype(jnp.int32)

    def like(shape, dtype=BF16):
        return jax.ShapeDtypeStruct(shape, dtype)

    packed, block = (4 * BLK + 16, HEAD), (4 * BLK, HEAD)
    own = local_call(pack_keys, like(packed), 56, stream_in=True)(positions, keys, values)
    u, w = by_parity(own, 5), by_parity(own, -5)

    own_q, send = local_call(
        pack_queries,
        (like((TOK, wide)), like((2 * n_heads, TOK // n_heads, wide))),
        56,
        stream_in=True,
    )(positions, queries, lse.T, outputs, out_grad)
    grad = lax.all_to_all(send, ("xh",) + HEADS, split_axis=0, concat_axis=0, tiled=True)
    other_q = swapped_with(own_q, "xh")
    s_set, x = local_call(
        join, (like((NEAR,) + packed), like((2, TOK, 2 * wide))), 8, stream_in=True
    )(info, own, u, w, own_q, other_q, grad.reshape(2, TOK, wide))
    p1, m1, p2, m2 = [by_parity(s_set, by) for by in (1, -1, 2, -2)]
    e_one = by_parity(w, 3)
    y = swapped_with(x, "core")

    near, dq_shape = (NEAR,) + block, (2, TOK, GROUP * HEAD)
    own_g, p1_g, m1_g, e_g, dq = local_call(
        with_nearest,
        (
            like(near, F32),
            like(near),
            like(near),
            like(block),
            like((4,) + dq_shape[1:], F32),
        ),
        16,
    )(
        x,
        y,
        s_set,
        p1,
        m1,
        e_one,
        scratch=[
            pltpu.VMEM((3 * NEAR + 1,) + packed, BF16),
            pltpu.VMEM((3 * NEAR + 1,) + block, F32),
        ],
    )
    p2_g, m2_g, dq, dq_core = local_call(
        with_next, (like(near), like(near), like(dq_shape, F32), like(dq_shape)), 16
    )(
        x,
        y,
        p2,
        m2,
        dq,
        scratch=[
            pltpu.VMEM((2 * NEAR,) + packed, BF16),
            pltpu.VMEM((2 * NEAR,) + block, F32),
            pltpu.VMEM((4,) + dq_shape[1:], F32),
        ],
    )

    p1_in, m1_in, e_in = by_parity(p1_g, 1), by_parity(m1_g, -1), by_parity(e_g, 3)
    own_g, p2_g, m2_g = local_call(sum_first, (like(near, F32), like(near), like(near)), 8)(
        own_g, p1_in, m1_in, p2_g, m2_g
    )
    p2_in, m2_in = by_parity(p2_g, -2), by_parity(m2_g, 2)
    dq_core = swapped_with(dq_core, "core")
    dq, dqx = local_call(sum_cores, (like(dq_shape[1:], F32), like(dq_shape[1:])), 8)(dq, dq_core)
    dqx = swapped_with(dqx, "xh")
    own_g, u_g, w_g = local_call(sum_near, (like(block, F32), like(block), like(block)), 8)(
        own_g, p2_in, m2_in, e_in
    )
    u_g, w_g = by_parity(u_g, 5), by_parity(w_g, -5)
    return local_call(
        finish,
        (like(queries.shape), like(keys.shape), like(values.shape)),
        8,
        stream_out=True,
    )(info, own_g, u_g, w_g, dq, dqx)


def solution(mesh):
    shape = FOLD or (2, 16, 2, 2, 4)
    split = jax.sharding.Mesh(mesh.devices.reshape(shape), ("xh", "z", "core", "xl", "y"))
    ctx, heads = ("xh", "z", "core"), ("xl", "y")
    return jax.shard_map(
        shards,
        mesh=split,
        in_specs=(
            P(ctx, heads),
            P(ctx, heads),
            P(ctx, heads),
            P(ctx + heads, None),
            P(ctx + heads, None),
            P(ctx, heads),
            P(ctx),
        ),
        out_specs=(P(ctx, heads), P(ctx, heads), P(ctx, heads)),
        check_vma=False,
    )
```

```python
import math

import jax
import jax.numpy as jnp
from jax import lax
from jax.experimental import pallas as pl
from jax.experimental.pallas import tpu as pltpu
from jax.sharding import PartitionSpec as P

HEAD = 128
BLK = 64
TOK = 2 * BLK
GROUP = 4
ROWS = GROUP * BLK
NEAR = 3
LOG2E = math.log2(math.e)
SCALE = 1.0 / math.sqrt(HEAD)
FAR = 1e30
F32 = jnp.float32
BF16 = jnp.bfloat16
FOLD = None


def dot_nt(a, b):
    return lax.dot_general(a, b, (((1,), (1,)), ((), ())), preferred_element_type=F32)


def dot_nn(a, b):
    return lax.dot_general(a, b, (((1,), (0,)), ((), ())), preferred_element_type=F32)


def dot_tn(a, b):
    return lax.dot_general(a, b, (((0,), (0,)), ((), ())), preferred_element_type=F32)


def backward(x_ref, y_ref, kv, acc, dq_acc, tiles, own):
    seen = lax.broadcasted_iota(jnp.int32, (BLK, ROWS), 0) <= (
        lax.broadcasted_iota(jnp.int32, (BLK, ROWS), 1) % BLK
    )

    def grads(scores, dprob, lse, delta):
        probs = jnp.exp2(scores * (SCALE * LOG2E) - lse)
        dscore = probs * (dprob - delta)
        return probs.astype(BF16), dscore.astype(BF16)

    def row_vectors(table):
        return [
            jnp.concatenate([table[h : h + 1, s : s + BLK] for h in range(GROUP)], axis=1)
            for s in (0, BLK)
        ]

    def half_rows(block):
        return [
            jnp.concatenate(
                [block[s : s + BLK, h * HEAD : (h + 1) * HEAD] for h in range(GROUP)], axis=0
            )
            for s in (0, BLK)
        ]

    def query_side(block):
        wide = GROUP * HEAD
        tail = jnp.transpose(block[:, wide : wide + HEAD].astype(F32))
        lse = tail[0:8, :] + tail[8:16, :] + tail[16:24, :]
        c_row, swapped = tail[24:25, :], tail[25:26, :] > 0.5
        tail = jnp.transpose(block[:, 2 * wide + HEAD :].astype(F32))
        delta = tail[0:8, :] + tail[8:16, :] + tail[16:24, :]
        d0, d1 = row_vectors(delta)
        g0, g1 = half_rows(block[:, wide + HEAD : 2 * wide + HEAD])
        two = jnp.concatenate([swapped, swapped], axis=1)
        tall = jnp.broadcast_to(swapped, (ROWS, HEAD))
        return (
            c_row,
            row_vectors(lse * LOG2E),
            (jnp.where(two, d1, d0), jnp.where(two, d0, d1)),
            half_rows(block[:, :wide]),
            (jnp.where(tall, g1, g0), jnp.where(tall, g0, g1)),
        )

    def flat(x):
        return x.reshape(x.shape[0] * x.shape[1], x.shape[2])

    def visit(block, e, own=False):
        own_c, lse, delta, q, g = query_side(block)
        (lse_early, lse_late), (delta_early, delta_late) = lse, delta
        q_late, g_late = q[1], g[1]
        q_both = jnp.concatenate(q, axis=1)
        g_both = jnp.concatenate(g, axis=1)
        dq_a = jnp.zeros((HEAD, ROWS), F32)
        dq_b = jnp.zeros((2 * HEAD, ROWS), F32)
        for first, last in tiles:
            size = last - first

            def pick(j):
                return kv[first:last, j * BLK : (j + 1) * BLK]

            c = kv[first:last, 4 * BLK : 4 * BLK + 16].astype(F32)[:, 0:1, :]
            before = c < own_c[None]
            after = c > own_c[None]
            wide = jnp.broadcast_to(before, (size, BLK, HEAD))
            k_early, k_late, v_early, v_late = [pick(j) for j in range(4)]
            k_both = jnp.concatenate(
                [flat(jnp.where(wide, k_early, 0)), flat(jnp.where(wide, 0, k_late))], axis=1
            )
            v_both = jnp.concatenate(
                [flat(jnp.where(wide, v_early, 0)), flat(jnp.where(wide, 0, v_late))], axis=1
            )
            k_early, v_early = flat(k_early), flat(v_early)
            before2 = jnp.concatenate([before, before], axis=2)
            after2 = jnp.concatenate([after, after], axis=2)
            lse_b = jnp.where(before2, lse_early[None], jnp.where(after2, lse_late[None], FAR))
            delta_b = jnp.where(before2, delta_early[None], delta_late[None])
            lse_b = jnp.broadcast_to(lse_b, (size, BLK, ROWS)).reshape(size * BLK, ROWS)
            delta_b = jnp.broadcast_to(delta_b, (size, BLK, ROWS)).reshape(size * BLK, ROWS)

            p_a, ds_a = grads(
                dot_nt(k_early, q_late), dot_nt(v_early, g_late), lse_late, delta_late
            )
            p_b, ds_b = grads(dot_nt(k_both, q_both), dot_nt(v_both, g_both), lse_b, delta_b)
            dv_a, dk_a = dot_nn(p_a, g_late), dot_nn(ds_a, q_late)
            dv_b, dk_b = dot_nn(p_b, g_both), dot_nn(ds_b, q_both)
            dq_a = dq_a + dot_tn(k_early, ds_a)
            dq_b = dq_b + dot_tn(k_both, ds_b)
            for j, one, two in ((0, dk_a, dk_b), (2, dv_a, dv_b)):
                one = one.reshape(size, BLK, HEAD)
                two = two.reshape(size, BLK, 2 * HEAD)
                acc[first:last, j * BLK : (j + 1) * BLK] += one + jnp.where(wide, two[:, :, :HEAD], 0.0)
                acc[first:last, (j + 1) * BLK : (j + 2) * BLK] += jnp.where(
                    wide, 0.0, two[:, :, HEAD:]
                )
        dq = [dq_b[:HEAD], dq_b[HEAD:] + dq_a]
        if own:
            for i in range(2):
                at = slice(i * BLK, (i + 1) * BLK)
                k, v = kv[0, at], kv[0, (2 + i) * BLK : (3 + i) * BLK]
                scores = jnp.where(seen, dot_nt(k, q[i]), -FAR)
                p, ds = grads(scores, dot_nt(v, g[i]), lse[i], delta[i])
                acc[0, at] += dot_nn(ds, q[i])
                acc[0, (2 + i) * BLK : (3 + i) * BLK] += dot_nn(p, g[i])
                dq[i] = dq[i] + dot_tn(k, ds)
        for i in range(2):
            grad = jnp.transpose(dq[i]) * SCALE
            for h in range(GROUP):
                dq_acc[e, i * BLK : (i + 1) * BLK, h * HEAD : (h + 1) * HEAD] += grad[
                    h * BLK : (h + 1) * BLK
                ]

    acc[...] = jnp.zeros_like(acc)
    visit(x_ref[0], 0, own=own)
    visit(x_ref[1], 1)

    @pl.loop(0, 2)
    def _(e):
        visit(y_ref[e], e + 2)


def scaled(acc, rows):
    return jnp.concatenate([acc[rows, : 2 * BLK] * SCALE, acc[rows, 2 * BLK :]], axis=-2)


def with_next(x_ref, y_ref, p_ref, m_ref, e_ref, p_out, m_out, dq_out, kv, acc):
    kv[:NEAR] = p_ref[...]
    kv[NEAR : 2 * NEAR] = m_ref[...]
    kv[2 * NEAR] = e_ref[...]
    dq_out[...] = jnp.zeros_like(dq_out)
    backward(x_ref, y_ref, kv, acc, dq_out, ((0, 4), (4, 7)), False)
    p_out[...] = scaled(acc, slice(0, NEAR)).astype(BF16)
    m_out[...] = scaled(acc, slice(NEAR, 2 * NEAR + 1)).astype(BF16)


def with_nearest(x_ref, y_ref, s_ref, p_ref, m_ref, dq_ref, *rest):
    own_out, p_out, m_out, dq_out, dq_core_out, kv, acc, dq = rest
    kv[:NEAR] = s_ref[...]
    kv[NEAR : 2 * NEAR] = p_ref[...]
    kv[2 * NEAR :] = m_ref[...]
    dq[...] = dq_ref[...]
    backward(x_ref, y_ref, kv, acc, dq, ((0, 5), (5, 9)), True)
    own_out[...] = scaled(acc, slice(0, NEAR))
    p_out[...] = scaled(acc, slice(NEAR, 2 * NEAR)).astype(BF16)
    m_out[...] = scaled(acc, slice(2 * NEAR, 3 * NEAR)).astype(BF16)
    dq_out[...] = dq[:2]
    dq_core_out[...] = dq[2:].astype(BF16)


def in_terms(x, lanes):
    out = jnp.zeros(lanes.shape, F32)
    for h in range(GROUP):
        rest = x[h]
        for n in range(3):
            term = rest.astype(BF16).astype(F32)
            out = jnp.where(lanes == 8 * n + h, term, out)
            rest = rest - term
    return out


def pack_keys(pos, k_ref, v_ref, out):
    start = pl.multiple_of(jnp.where(pos[0] > pos[BLK], BLK, 0), BLK)
    other = pl.multiple_of(BLK - start, BLK)
    out[:BLK] = k_ref[pl.ds(start, BLK), :]
    out[BLK : 2 * BLK] = k_ref[pl.ds(other, BLK), :]
    out[2 * BLK : 3 * BLK] = v_ref[pl.ds(start, BLK), :]
    out[3 * BLK : 4 * BLK] = v_ref[pl.ds(other, BLK), :]
    c = jnp.minimum(pos[0], pos[BLK]) // BLK
    out[4 * BLK :] = jnp.full((16, HEAD), c, jnp.int32).astype(F32).astype(BF16)


def pack_queries(pos, q_ref, lse_ref, o_ref, g_ref, q_out, g_out):
    wide = GROUP * HEAD
    swapped = pos[0] > pos[BLK]
    start = pl.multiple_of(jnp.where(swapped, BLK, 0), BLK)
    lanes = lax.broadcasted_iota(jnp.int32, (BLK, HEAD), 1)
    c = jnp.minimum(pos[0], pos[BLK]) // BLK
    lse = jnp.concatenate([lse_ref[...], jnp.zeros((HEAD - GROUP, TOK), F32)])
    turned = jnp.transpose(lse)
    turned = jnp.where(swapped, jnp.concatenate([turned[BLK:], turned[:BLK]]), turned)
    for i in range(2):
        rows = pl.ds(start if i == 0 else pl.multiple_of(BLK - start, BLK), BLK)
        q_out[i * BLK : (i + 1) * BLK, :wide] = q_ref[rows, :]
        lse = turned[i * BLK : (i + 1) * BLK, :]
        tail = in_terms([lse[:, h : h + 1] for h in range(GROUP)], lanes)
        tail = jnp.where(lanes == 24, c.astype(F32), tail)
        tail = jnp.where(lanes == 25, swapped.astype(F32), tail)
        q_out[i * BLK : (i + 1) * BLK, wide:] = tail.astype(BF16)
    n_heads = g_ref.shape[1] // wide
    lanes = lax.broadcasted_iota(jnp.int32, (g_ref.shape[0], HEAD), 1)
    for d in range(n_heads):
        g = g_ref[:, d * wide : (d + 1) * wide]
        product = g.astype(F32) * o_ref[:, d * wide : (d + 1) * wide].astype(F32)
        delta = [
            jnp.sum(product[:, h * HEAD : (h + 1) * HEAD], axis=1, keepdims=True)
            for h in range(GROUP)
        ]
        tail = in_terms(delta, lanes).astype(BF16)
        for twin in range(2):
            g_out[twin * n_heads + d, :, :wide] = g
            g_out[twin * n_heads + d, :, wide:] = tail


def join(own_ref, u_ref, w_ref, q_ref, qx_ref, grad_ref, s_out, x_out):
    s_out[0] = own_ref[...]
    s_out[1] = u_ref[...]
    s_out[2] = w_ref[...]
    wide = (GROUP + 1) * HEAD
    x_out[0, :, :wide] = q_ref[...]
    x_out[1, :, :wide] = qx_ref[...]
    half = lax.axis_index("xh")
    x_out[0, :, wide:] = grad_ref[half]
    x_out[1, :, wide:] = grad_ref[1 - half]


def sum_first(own_ref, c_ref, d_ref, p_ref, m_ref, own_out, p_out, m_out):
    own_out[...] = own_ref[...] + c_ref[...].astype(F32) + d_ref[:NEAR].astype(F32)
    p_out[: NEAR - 1] = p_ref[: NEAR - 1]
    last = p_ref[NEAR - 1].astype(F32) + d_ref[NEAR].astype(F32)
    p_out[NEAR - 1] = last.astype(BF16)
    m_out[...] = m_ref[...]


def sum_near(own_ref, p_ref, m_ref, own_out, u_out, w_out):
    total = own_ref[...] + p_ref[...].astype(F32) + m_ref[...].astype(F32)
    own_out[...] = total[0]
    u_out[...] = total[1].astype(BF16)
    w_out[...] = total[2].astype(BF16)


def sum_cores(dq_ref, core_ref, x_ref, dq_out, dqx_out, flag_out):
    dq_out[...] = dq_ref[0] + core_ref[0].astype(F32)
    dqx_out[...] = (dq_ref[1] + core_ref[1].astype(F32)).astype(BF16)
    at = GROUP * HEAD + 25
    flag_out[...] = jnp.broadcast_to(x_ref[0, :BLK, at : at + 1].astype(F32), flag_out.shape)


def finish(flag_ref, own_ref, u_ref, w_ref, dq_ref, dqx_ref, q_out, k_out, v_out):
    swapped = flag_ref[...] > 0.5
    total = own_ref[...] + u_ref[...].astype(F32) + w_ref[...].astype(F32)
    dq = dq_ref[...] + dqx_ref[...].astype(F32)
    for i in range(2):
        here, there = slice(i * BLK, (i + 1) * BLK), slice((1 - i) * BLK, (2 - i) * BLK)
        for h in range(GROUP):
            cols = slice(h * HEAD, (h + 1) * HEAD)
            q_out[here, cols] = jnp.where(swapped, dq[there, cols], dq[here, cols]).astype(BF16)
        k_out[here, :] = jnp.where(swapped, total[there], total[here]).astype(BF16)
        there, of_v = slice((3 - i) * BLK, (4 - i) * BLK), slice((2 + i) * BLK, (3 + i) * BLK)
        v_out[here, :] = jnp.where(swapped, total[there], total[of_v]).astype(BF16)


HEADS = ("xl", "y")


def by_parity(x, distance):
    n = lax.axis_size("z")
    to = [(i + (distance if i % 2 == 0 else -distance)) % n for i in range(n)]
    return lax.ppermute(x, "z", list(enumerate(to)))


def swapped_with(x, axis):
    return lax.ppermute(x, axis, [(0, 1), (1, 0)])


def local_call(body, out_shape, mib, stream_in=False, stream_out=False):
    vmem, smem = pl.BlockSpec(memory_space=pltpu.VMEM), pl.BlockSpec(memory_space=pltpu.SMEM)
    free = pl.BlockSpec()

    def call(*args, scratch=()):
        return pl.pallas_call(
            body,
            out_shape=out_shape,
            in_specs=[
                smem if a.dtype == jnp.int32 else free if stream_in else vmem for a in args
            ],
            out_specs=jax.tree.map(lambda _: free if stream_out else vmem, out_shape),
            scratch_shapes=scratch,
            compiler_params=pltpu.CompilerParams(vmem_limit_bytes=mib * 1024 * 1024),
            name=body.__name__,
        )(*args)

    return call


def shards(queries, keys, values, outputs, out_grad, lse, positions):
    n_heads = lax.axis_size(HEADS)
    wide = (GROUP + 1) * HEAD

    def like(shape, dtype=BF16):
        return jax.ShapeDtypeStruct(shape, dtype)

    packed, block = (4 * BLK + 16, HEAD), (4 * BLK, HEAD)
    own = local_call(pack_keys, like(packed), 56, stream_in=True)(positions, keys, values)
    u, w = by_parity(own, 5), by_parity(own, -5)

    own_q, send = local_call(
        pack_queries,
        (like((TOK, wide)), like((2 * n_heads, TOK // n_heads, wide))),
        56,
        stream_in=True,
    )(positions, queries, lse.T, outputs, out_grad)
    grad = lax.all_to_all(send, ("xh",) + HEADS, split_axis=0, concat_axis=0, tiled=True)
    other_q = swapped_with(own_q, "xh")
    s_set, x = local_call(
        join, (like((NEAR,) + packed), like((2, TOK, 2 * wide))), 8, stream_in=True
    )(own, u, w, own_q, other_q, grad.reshape(2, TOK, wide))
    p1, m1, p2, m2 = [by_parity(s_set, by) for by in (1, -1, 2, -2)]
    e_one = by_parity(w, 3)
    y = swapped_with(x, "core")

    near, dq_shape = (NEAR,) + block, (2, TOK, GROUP * HEAD)
    p2_g, m2_g, dq = local_call(
        with_next,
        (like(near), like((NEAR + 1,) + block), like((4,) + dq_shape[1:], F32)),
        16,
    )(
        x,
        y,
        p2,
        m2,
        e_one,
        scratch=[
            pltpu.VMEM((2 * NEAR + 1,) + packed, BF16),
            pltpu.VMEM((2 * NEAR + 1,) + block, F32),
        ],
    )
    own_g, p1_g, m1_g, dq, dq_core = local_call(
        with_nearest,
        (like(near, F32), like(near), like(near), like(dq_shape, F32), like(dq_shape)),
        16,
    )(
        x,
        y,
        s_set,
        p1,
        m1,
        dq,
        scratch=[
            pltpu.VMEM((3 * NEAR,) + packed, BF16),
            pltpu.VMEM((3 * NEAR,) + block, F32),
            pltpu.VMEM((4,) + dq_shape[1:], F32),
        ],
    )

    p2_in, m2_in = by_parity(p2_g, -2), by_parity(m2_g, 2)
    own_g, p1_g, m1_g = local_call(sum_first, (like(near, F32), like(near), like(near)), 8)(
        own_g, p2_in, m2_in, p1_g, m1_g
    )
    p1_in, m1_in = by_parity(p1_g, 1), by_parity(m1_g, -1)
    dq_core = swapped_with(dq_core, "core")
    dq, dqx, flag = local_call(
        sum_cores, (like(dq_shape[1:], F32), like(dq_shape[1:]), like((BLK, HEAD), F32)), 8
    )(dq, dq_core, x)
    dqx = swapped_with(dqx, "xh")
    own_g, u_g, w_g = local_call(sum_near, (like(block, F32), like(block), like(block)), 8)(
        own_g, p1_in, m1_in
    )
    u_g, w_g = by_parity(u_g, 5), by_parity(w_g, -5)
    return local_call(
        finish,
        (like(queries.shape), like(keys.shape), like(values.shape)),
        8,
        stream_out=True,
    )(flag, own_g, u_g, w_g, dq, dqx)


def solution(mesh):
    shape = FOLD or (2, 16, 2, 2, 4)
    split = jax.sharding.Mesh(mesh.devices.reshape(shape), ("xh", "z", "core", "xl", "y"))
    ctx, heads = ("xh", "z", "core"), ("xl", "y")
    return jax.shard_map(
        shards,
        mesh=split,
        in_specs=(
            P(ctx, heads),
            P(ctx, heads),
            P(ctx, heads),
            P(ctx + heads, None),
            P(ctx + heads, None),
            P(ctx, heads),
            P(ctx),
        ),
        out_specs=(P(ctx, heads), P(ctx, heads), P(ctx, heads)),
        check_vma=False,
    )
```

```python
import math

import jax
import jax.numpy as jnp
from jax import lax
from jax.experimental import pallas as pl
from jax.experimental.pallas import tpu as pltpu
from jax.sharding import PartitionSpec as P

HEAD = 128
BLK = 64
TOK = 2 * BLK
GROUP = 4
ROWS = GROUP * BLK
NEAR = 3
LOG2E = math.log2(math.e)
SCALE = 1.0 / math.sqrt(HEAD)
FAR = 1e30
F32 = jnp.float32
BF16 = jnp.bfloat16
FOLD = None


def dot_nt(a, b):
    return lax.dot_general(a, b, (((1,), (1,)), ((), ())), preferred_element_type=F32)


def dot_nn(a, b):
    return lax.dot_general(a, b, (((1,), (0,)), ((), ())), preferred_element_type=F32)


def dot_tn(a, b):
    return lax.dot_general(a, b, (((0,), (0,)), ((), ())), preferred_element_type=F32)


def backward(x_ref, y_ref, kv, acc, dq_acc, tiles, own):
    seen = lax.broadcasted_iota(jnp.int32, (BLK, ROWS), 0) <= (
        lax.broadcasted_iota(jnp.int32, (BLK, ROWS), 1) % BLK
    )

    def grads(scores, dprob, lse, delta):
        probs = jnp.exp2(scores * (SCALE * LOG2E) - lse)
        dscore = probs * (dprob - delta)
        return probs.astype(BF16), dscore.astype(BF16)

    def row_vectors(table):
        return [
            jnp.concatenate([table[h : h + 1, s : s + BLK] for h in range(GROUP)], axis=1)
            for s in (0, BLK)
        ]

    def half_rows(block):
        return [
            jnp.concatenate(
                [block[s : s + BLK, h * HEAD : (h + 1) * HEAD] for h in range(GROUP)], axis=0
            )
            for s in (0, BLK)
        ]

    def query_side(block):
        wide = GROUP * HEAD
        tail = jnp.transpose(block[:, wide : wide + HEAD].astype(F32))
        lse = tail[0:8, :] + tail[8:16, :] + tail[16:24, :]
        c_row, swapped = tail[24:25, :], tail[25:26, :] > 0.5
        tail = jnp.transpose(block[:, 2 * wide + HEAD :].astype(F32))
        delta = tail[0:8, :] + tail[8:16, :] + tail[16:24, :]
        d0, d1 = row_vectors(delta)
        g0, g1 = half_rows(block[:, wide + HEAD : 2 * wide + HEAD])
        two = jnp.concatenate([swapped, swapped], axis=1)
        tall = jnp.broadcast_to(swapped, (ROWS, HEAD))
        return (
            c_row,
            row_vectors(lse * LOG2E),
            (jnp.where(two, d1, d0), jnp.where(two, d0, d1)),
            half_rows(block[:, :wide]),
            (jnp.where(tall, g1, g0), jnp.where(tall, g0, g1)),
        )

    def flat(x):
        return x.reshape(x.shape[0] * x.shape[1], x.shape[2])

    def visit(block, e, own=False):
        own_c, lse, delta, q, g = query_side(block)
        (lse_early, lse_late), (delta_early, delta_late) = lse, delta
        q_late, g_late = q[1], g[1]
        q_both = jnp.concatenate(q, axis=1)
        g_both = jnp.concatenate(g, axis=1)
        dq_a = jnp.zeros((HEAD, ROWS), F32)
        dq_b = jnp.zeros((2 * HEAD, ROWS), F32)
        for first, last in tiles:
            size = last - first

            def pick(j):
                return kv[first:last, j * BLK : (j + 1) * BLK]

            c = kv[first:last, 4 * BLK : 4 * BLK + 16].astype(F32)[:, 0:1, :]
            before = c < own_c[None]
            after = c > own_c[None]
            wide = jnp.broadcast_to(before, (size, BLK, HEAD))
            k_early, k_late, v_early, v_late = [pick(j) for j in range(4)]
            k_both = jnp.concatenate(
                [flat(jnp.where(wide, k_early, 0)), flat(jnp.where(wide, 0, k_late))], axis=1
            )
            v_both = jnp.concatenate(
                [flat(jnp.where(wide, v_early, 0)), flat(jnp.where(wide, 0, v_late))], axis=1
            )
            k_early, v_early = flat(k_early), flat(v_early)
            before2 = jnp.concatenate([before, before], axis=2)
            after2 = jnp.concatenate([after, after], axis=2)
            lse_b = jnp.where(before2, lse_early[None], jnp.where(after2, lse_late[None], FAR))
            delta_b = jnp.where(before2, delta_early[None], delta_late[None])
            lse_b = jnp.broadcast_to(lse_b, (size, BLK, ROWS)).reshape(size * BLK, ROWS)
            delta_b = jnp.broadcast_to(delta_b, (size, BLK, ROWS)).reshape(size * BLK, ROWS)

            p_a, ds_a = grads(
                dot_nt(k_early, q_late), dot_nt(v_early, g_late), lse_late, delta_late
            )
            p_b, ds_b = grads(dot_nt(k_both, q_both), dot_nt(v_both, g_both), lse_b, delta_b)
            dv_a, dk_a = dot_nn(p_a, g_late), dot_nn(ds_a, q_late)
            dv_b, dk_b = dot_nn(p_b, g_both), dot_nn(ds_b, q_both)
            dq_a = dq_a + dot_tn(k_early, ds_a)
            dq_b = dq_b + dot_tn(k_both, ds_b)
            for j, one, two in ((0, dk_a, dk_b), (2, dv_a, dv_b)):
                one = one.reshape(size, BLK, HEAD)
                two = two.reshape(size, BLK, 2 * HEAD)
                acc[first:last, j * BLK : (j + 1) * BLK] += one + jnp.where(wide, two[:, :, :HEAD], 0.0)
                acc[first:last, (j + 1) * BLK : (j + 2) * BLK] += jnp.where(
                    wide, 0.0, two[:, :, HEAD:]
                )
        dq = [dq_b[:HEAD], dq_b[HEAD:] + dq_a]
        if own:
            for i in range(2):
                at = slice(i * BLK, (i + 1) * BLK)
                k, v = kv[0, at], kv[0, (2 + i) * BLK : (3 + i) * BLK]
                scores = jnp.where(seen, dot_nt(k, q[i]), -FAR)
                p, ds = grads(scores, dot_nt(v, g[i]), lse[i], delta[i])
                acc[0, at] += dot_nn(ds, q[i])
                acc[0, (2 + i) * BLK : (3 + i) * BLK] += dot_nn(p, g[i])
                dq[i] = dq[i] + dot_tn(k, ds)
        for i in range(2):
            grad = jnp.transpose(dq[i]) * SCALE
            for h in range(GROUP):
                dq_acc[e, i * BLK : (i + 1) * BLK, h * HEAD : (h + 1) * HEAD] += grad[
                    h * BLK : (h + 1) * BLK
                ]

    acc[...] = jnp.zeros_like(acc)
    visit(x_ref[0], 0, own=own)
    visit(x_ref[1], 1)

    @pl.loop(0, 2)
    def _(e):
        visit(y_ref[e], e + 2)


def scaled(acc, rows):
    return jnp.concatenate([acc[rows, : 2 * BLK] * SCALE, acc[rows, 2 * BLK :]], axis=-2)


def with_next(x_ref, y_ref, p_ref, m_ref, e_ref, p_out, m_out, dq_out, kv, acc):
    kv[:NEAR] = p_ref[...]
    kv[NEAR : 2 * NEAR] = m_ref[...]
    kv[2 * NEAR] = e_ref[...]
    dq_out[...] = jnp.zeros_like(dq_out)
    backward(x_ref, y_ref, kv, acc, dq_out, ((0, 4), (4, 7)), False)
    p_out[...] = scaled(acc, slice(0, NEAR)).astype(BF16)
    m_out[...] = scaled(acc, slice(NEAR, 2 * NEAR + 1)).astype(BF16)


def with_nearest(x_ref, y_ref, s_ref, p_ref, m_ref, dq_ref, *rest):
    own_out, p_out, m_out, dq_out, dq_core_out, kv, acc, dq = rest
    kv[:NEAR] = s_ref[...]
    kv[NEAR : 2 * NEAR] = p_ref[...]
    kv[2 * NEAR :] = m_ref[...]
    dq[...] = dq_ref[...]
    backward(x_ref, y_ref, kv, acc, dq, ((0, 5), (5, 9)), True)
    own_out[...] = scaled(acc, slice(0, NEAR))
    p_out[...] = scaled(acc, slice(NEAR, 2 * NEAR)).astype(BF16)
    m_out[...] = scaled(acc, slice(2 * NEAR, 3 * NEAR)).astype(BF16)
    dq_out[...] = dq[:2]
    dq_core_out[...] = dq[2:].astype(BF16)


def in_terms(x, lanes):
    out = jnp.zeros(lanes.shape, F32)
    for h in range(GROUP):
        rest = x[h]
        for n in range(3):
            term = rest.astype(BF16).astype(F32)
            out = jnp.where(lanes == 8 * n + h, term, out)
            rest = rest - term
    return out


def pack_keys(pos, k_ref, v_ref, out):
    start = pl.multiple_of(jnp.where(pos[0] > pos[BLK], BLK, 0), BLK)
    other = pl.multiple_of(BLK - start, BLK)
    out[:BLK] = k_ref[pl.ds(start, BLK), :]
    out[BLK : 2 * BLK] = k_ref[pl.ds(other, BLK), :]
    out[2 * BLK : 3 * BLK] = v_ref[pl.ds(start, BLK), :]
    out[3 * BLK : 4 * BLK] = v_ref[pl.ds(other, BLK), :]
    c = jnp.minimum(pos[0], pos[BLK]) // BLK
    out[4 * BLK :] = jnp.full((16, HEAD), c, jnp.int32).astype(F32).astype(BF16)


def pack_queries(pos, q_ref, lse_ref, o_ref, g_ref, after_ref, q_out, g_out):
    wide = GROUP * HEAD
    swapped = pos[0] > pos[BLK]
    start = pl.multiple_of(jnp.where(swapped, BLK, 0), BLK)
    lanes = lax.broadcasted_iota(jnp.int32, (BLK, HEAD), 1)
    c = jnp.minimum(pos[0], pos[BLK]) // BLK
    lse = jnp.concatenate([lse_ref[...], jnp.zeros((HEAD - GROUP, TOK), F32)])
    turned = jnp.transpose(lse)
    turned = jnp.where(swapped, jnp.concatenate([turned[BLK:], turned[:BLK]]), turned)
    for i in range(2):
        rows = pl.ds(start if i == 0 else pl.multiple_of(BLK - start, BLK), BLK)
        q_out[i * BLK : (i + 1) * BLK, :wide] = q_ref[rows, :]
        lse = turned[i * BLK : (i + 1) * BLK, :]
        tail = in_terms([lse[:, h : h + 1] for h in range(GROUP)], lanes)
        tail = jnp.where(lanes == 24, c.astype(F32), tail)
        tail = jnp.where(lanes == 25, swapped.astype(F32), tail)
        q_out[i * BLK : (i + 1) * BLK, wide:] = tail.astype(BF16)
    n_heads = g_ref.shape[1] // wide
    lanes = lax.broadcasted_iota(jnp.int32, (g_ref.shape[0], HEAD), 1)
    for d in range(n_heads):
        g = g_ref[:, d * wide : (d + 1) * wide]
        product = g.astype(F32) * o_ref[:, d * wide : (d + 1) * wide].astype(F32)
        delta = [
            jnp.sum(product[:, h * HEAD : (h + 1) * HEAD], axis=1, keepdims=True)
            for h in range(GROUP)
        ]
        tail = in_terms(delta, lanes).astype(BF16)
        for twin in range(2):
            g_out[twin * n_heads + d, :, :wide] = g
            g_out[twin * n_heads + d, :, wide:] = tail


def join(own_ref, u_ref, w_ref, e_ref, q_ref, qx_ref, grad_ref, s_out, x_out):
    s_out[0] = own_ref[...]
    s_out[1] = u_ref[...]
    s_out[2] = w_ref[...]
    wide = (GROUP + 1) * HEAD
    x_out[0, :, :wide] = q_ref[...]
    x_out[1, :, :wide] = qx_ref[...]
    half = lax.axis_index("xh")
    x_out[0, :, wide:] = grad_ref[half]
    x_out[1, :, wide:] = grad_ref[1 - half]


def sum_first(own_ref, c_ref, d_ref, p_ref, m_ref, own_out, p_out, m_out):
    own_out[...] = own_ref[...] + c_ref[...].astype(F32) + d_ref[:NEAR].astype(F32)
    p_out[: NEAR - 1] = p_ref[: NEAR - 1]
    last = p_ref[NEAR - 1].astype(F32) + d_ref[NEAR].astype(F32)
    p_out[NEAR - 1] = last.astype(BF16)
    m_out[...] = m_ref[...]


def sum_near(own_ref, p_ref, m_ref, own_out, u_out, w_out):
    total = own_ref[...] + p_ref[...].astype(F32) + m_ref[...].astype(F32)
    own_out[...] = total[0]
    u_out[...] = total[1].astype(BF16)
    w_out[...] = total[2].astype(BF16)


def sum_cores(dq_ref, core_ref, x_ref, dq_out, dqx_out, flag_out):
    dq_out[...] = dq_ref[0] + core_ref[0].astype(F32)
    dqx_out[...] = (dq_ref[1] + core_ref[1].astype(F32)).astype(BF16)
    at = GROUP * HEAD + 25
    flag_out[...] = jnp.broadcast_to(x_ref[0, :BLK, at : at + 1].astype(F32), flag_out.shape)


def finish(flag_ref, own_ref, u_ref, w_ref, dq_ref, dqx_ref, q_out, k_out, v_out):
    swapped = flag_ref[...] > 0.5
    total = own_ref[...] + u_ref[...].astype(F32) + w_ref[...].astype(F32)
    dq = dq_ref[...] + dqx_ref[...].astype(F32)
    for i in range(2):
        here, there = slice(i * BLK, (i + 1) * BLK), slice((1 - i) * BLK, (2 - i) * BLK)
        for h in range(GROUP):
            cols = slice(h * HEAD, (h + 1) * HEAD)
            q_out[here, cols] = jnp.where(swapped, dq[there, cols], dq[here, cols]).astype(BF16)
        k_out[here, :] = jnp.where(swapped, total[there], total[here]).astype(BF16)
        there, of_v = slice((3 - i) * BLK, (4 - i) * BLK), slice((2 + i) * BLK, (3 + i) * BLK)
        v_out[here, :] = jnp.where(swapped, total[there], total[of_v]).astype(BF16)


HEADS = ("xl", "y")


def by_parity(x, distance):
    n = lax.axis_size("z")
    to = [(i + (distance if i % 2 == 0 else -distance)) % n for i in range(n)]
    return lax.ppermute(x, "z", list(enumerate(to)))


def half_round(x):
    n = lax.axis_size("z")
    return lax.ppermute(x, "z", [(i, (i + n // 2) % n) for i in range(n)])


def swapped_with(x, axis):
    return lax.ppermute(x, axis, [(0, 1), (1, 0)])


def local_call(body, out_shape, mib, stream_in=False, stream_out=False):
    vmem, smem = pl.BlockSpec(memory_space=pltpu.VMEM), pl.BlockSpec(memory_space=pltpu.SMEM)
    free = pl.BlockSpec()

    def call(*args, scratch=()):
        return pl.pallas_call(
            body,
            out_shape=out_shape,
            in_specs=[
                smem if a.dtype == jnp.int32 else free if stream_in else vmem for a in args
            ],
            out_specs=jax.tree.map(lambda _: free if stream_out else vmem, out_shape),
            scratch_shapes=scratch,
            compiler_params=pltpu.CompilerParams(vmem_limit_bytes=mib * 1024 * 1024),
            name=body.__name__,
        )(*args)

    return call


def shards(queries, keys, values, outputs, out_grad, lse, positions):
    n_heads = lax.axis_size(HEADS)
    wide = (GROUP + 1) * HEAD

    def like(shape, dtype=BF16):
        return jax.ShapeDtypeStruct(shape, dtype)

    packed, block = (4 * BLK + 16, HEAD), (4 * BLK, HEAD)
    own = local_call(pack_keys, like(packed), 56, stream_in=True)(positions, keys, values)
    u, w = by_parity(own, 5), by_parity(own, -5)
    e_one = half_round(own)

    own_q, send = local_call(
        pack_queries,
        (like((TOK, wide)), like((2 * n_heads, TOK // n_heads, wide))),
        56,
        stream_in=True,
    )(positions, queries, lse.T, outputs, out_grad, own)
    grad = lax.all_to_all(send, ("xh",) + HEADS, split_axis=0, concat_axis=0, tiled=True)
    other_q = swapped_with(own_q, "xh")
    s_set, x = local_call(
        join, (like((NEAR,) + packed), like((2, TOK, 2 * wide))), 8, stream_in=True
    )(own, u, w, e_one, own_q, other_q, grad.reshape(2, TOK, wide))
    p1, m1, p2, m2 = [by_parity(s_set, by) for by in (1, -1, 2, -2)]
    y = swapped_with(x, "core")

    near, dq_shape = (NEAR,) + block, (2, TOK, GROUP * HEAD)
    p2_g, m2_g, dq = local_call(
        with_next,
        (like(near), like((NEAR + 1,) + block), like((4,) + dq_shape[1:], F32)),
        16,
    )(
        x,
        y,
        p2,
        m2,
        e_one,
        scratch=[
            pltpu.VMEM((2 * NEAR + 1,) + packed, BF16),
            pltpu.VMEM((2 * NEAR + 1,) + block, F32),
        ],
    )
    own_g, p1_g, m1_g, dq, dq_core = local_call(
        with_nearest,
        (like(near, F32), like(near), like(near), like(dq_shape, F32), like(dq_shape)),
        16,
    )(
        x,
        y,
        s_set,
        p1,
        m1,
        dq,
        scratch=[
            pltpu.VMEM((3 * NEAR,) + packed, BF16),
            pltpu.VMEM((3 * NEAR,) + block, F32),
            pltpu.VMEM((4,) + dq_shape[1:], F32),
        ],
    )

    p2_in, m2_in = by_parity(p2_g, -2), by_parity(m2_g, 2)
    own_g, p1_g, m1_g = local_call(sum_first, (like(near, F32), like(near), like(near)), 8)(
        own_g, p2_in, m2_in, p1_g, m1_g
    )
    p1_in, m1_in = by_parity(p1_g, 1), by_parity(m1_g, -1)
    dq_core = swapped_with(dq_core, "core")
    dq, dqx, flag = local_call(
        sum_cores, (like(dq_shape[1:], F32), like(dq_shape[1:]), like((BLK, HEAD), F32)), 8
    )(dq, dq_core, x)
    dqx = swapped_with(dqx, "xh")
    own_g, u_g, w_g = local_call(sum_near, (like(block, F32), like(block), like(block)), 8)(
        own_g, p1_in, m1_in
    )
    u_g, w_g = by_parity(u_g, 5), by_parity(w_g, -5)
    return local_call(
        finish,
        (like(queries.shape), like(keys.shape), like(values.shape)),
        8,
        stream_out=True,
    )(flag, own_g, u_g, w_g, dq, dqx)


def solution(mesh):
    shape = FOLD or (2, 16, 2, 2, 4)
    split = jax.sharding.Mesh(mesh.devices.reshape(shape), ("xh", "z", "core", "xl", "y"))
    ctx, heads = ("xh", "z", "core"), ("xl", "y")
    return jax.shard_map(
        shards,
        mesh=split,
        in_specs=(
            P(ctx, heads),
            P(ctx, heads),
            P(ctx, heads),
            P(ctx + heads, None),
            P(ctx + heads, None),
            P(ctx, heads),
            P(ctx),
        ),
        out_specs=(P(ctx, heads), P(ctx, heads), P(ctx, heads)),
        check_vma=False,
    )
```

```python
import math

import jax
import jax.numpy as jnp
from jax import lax
from jax.experimental import pallas as pl
from jax.experimental.pallas import tpu as pltpu
from jax.sharding import PartitionSpec as P

HEAD = 128
BLK = 64
TOK = 2 * BLK
GROUP = 4
ROWS = GROUP * BLK
NEAR = 3
LOG2E = math.log2(math.e)
SCALE = 1.0 / math.sqrt(HEAD)
FAR = 1e30
F32 = jnp.float32
BF16 = jnp.bfloat16
FOLD = None


def dot_nt(a, b):
    return lax.dot_general(a, b, (((1,), (1,)), ((), ())), preferred_element_type=F32)


def dot_nn(a, b):
    return lax.dot_general(a, b, (((1,), (0,)), ((), ())), preferred_element_type=F32)


def dot_tn(a, b):
    return lax.dot_general(a, b, (((0,), (0,)), ((), ())), preferred_element_type=F32)


def backward(x_ref, y_ref, kv, acc, dq_acc, tiles, own):
    seen = lax.broadcasted_iota(jnp.int32, (BLK, ROWS), 0) <= (
        lax.broadcasted_iota(jnp.int32, (BLK, ROWS), 1) % BLK
    )

    def grads(scores, dprob, lse, delta):
        probs = jnp.exp2(scores * (SCALE * LOG2E) - lse)
        dscore = probs * (dprob - delta)
        return probs.astype(BF16), dscore.astype(BF16)

    def row_vectors(table):
        return [
            jnp.concatenate([table[h : h + 1, s : s + BLK] for h in range(GROUP)], axis=1)
            for s in (0, BLK)
        ]

    def half_rows(block):
        return [
            jnp.concatenate(
                [block[s : s + BLK, h * HEAD : (h + 1) * HEAD] for h in range(GROUP)], axis=0
            )
            for s in (0, BLK)
        ]

    def query_side(block):
        wide = GROUP * HEAD
        tail = jnp.transpose(block[:, wide : wide + HEAD].astype(F32))
        lse = tail[0:8, :] + tail[8:16, :] + tail[16:24, :]
        c_row, swapped = tail[24:25, :], tail[25:26, :] > 0.5
        tail = jnp.transpose(block[:, 2 * wide + HEAD :].astype(F32))
        delta = tail[0:8, :] + tail[8:16, :] + tail[16:24, :]
        d0, d1 = row_vectors(delta)
        g0, g1 = half_rows(block[:, wide + HEAD : 2 * wide + HEAD])
        two = jnp.concatenate([swapped, swapped], axis=1)
        tall = jnp.broadcast_to(swapped, (ROWS, HEAD))
        return (
            c_row,
            row_vectors(lse * LOG2E),
            (jnp.where(two, d1, d0), jnp.where(two, d0, d1)),
            half_rows(block[:, :wide]),
            (jnp.where(tall, g1, g0), jnp.where(tall, g0, g1)),
        )

    def flat(x):
        return x.reshape(x.shape[0] * x.shape[1], x.shape[2])

    def visit(block, e, own=False):
        own_c, lse, delta, q, g = query_side(block)
        (lse_early, lse_late), (delta_early, delta_late) = lse, delta
        q_late, g_late = q[1], g[1]
        q_both = jnp.concatenate(q, axis=1)
        g_both = jnp.concatenate(g, axis=1)
        dq_a = jnp.zeros((HEAD, ROWS), F32)
        dq_b = jnp.zeros((2 * HEAD, ROWS), F32)
        for first, last in tiles:
            size = last - first

            def pick(j):
                return kv[first:last, j * BLK : (j + 1) * BLK]

            c = kv[first:last, 4 * BLK : 4 * BLK + 16].astype(F32)[:, 0:1, :]
            before = c < own_c[None]
            after = c > own_c[None]
            wide = jnp.broadcast_to(before, (size, BLK, HEAD))
            k_early, k_late, v_early, v_late = [pick(j) for j in range(4)]
            k_both = jnp.concatenate(
                [flat(jnp.where(wide, k_early, 0)), flat(jnp.where(wide, 0, k_late))], axis=1
            )
            v_both = jnp.concatenate(
                [flat(jnp.where(wide, v_early, 0)), flat(jnp.where(wide, 0, v_late))], axis=1
            )
            k_early, v_early = flat(k_early), flat(v_early)
            before2 = jnp.concatenate([before, before], axis=2)
            after2 = jnp.concatenate([after, after], axis=2)
            lse_b = jnp.where(before2, lse_early[None], jnp.where(after2, lse_late[None], FAR))
            delta_b = jnp.where(before2, delta_early[None], delta_late[None])
            lse_b = jnp.broadcast_to(lse_b, (size, BLK, ROWS)).reshape(size * BLK, ROWS)
            delta_b = jnp.broadcast_to(delta_b, (size, BLK, ROWS)).reshape(size * BLK, ROWS)

            p_a, ds_a = grads(
                dot_nt(k_early, q_late), dot_nt(v_early, g_late), lse_late, delta_late
            )
            p_b, ds_b = grads(dot_nt(k_both, q_both), dot_nt(v_both, g_both), lse_b, delta_b)
            dv_a, dk_a = dot_nn(p_a, g_late), dot_nn(ds_a, q_late)
            dv_b, dk_b = dot_nn(p_b, g_both), dot_nn(ds_b, q_both)
            dq_a = dq_a + dot_tn(k_early, ds_a)
            dq_b = dq_b + dot_tn(k_both, ds_b)
            for j, one, two in ((0, dk_a, dk_b), (2, dv_a, dv_b)):
                one = one.reshape(size, BLK, HEAD)
                two = two.reshape(size, BLK, 2 * HEAD)
                acc[first:last, j * BLK : (j + 1) * BLK] += one + jnp.where(wide, two[:, :, :HEAD], 0.0)
                acc[first:last, (j + 1) * BLK : (j + 2) * BLK] += jnp.where(
                    wide, 0.0, two[:, :, HEAD:]
                )
        dq = [dq_b[:HEAD], dq_b[HEAD:] + dq_a]
        if own:
            for i in range(2):
                at = slice(i * BLK, (i + 1) * BLK)
                k, v = kv[0, at], kv[0, (2 + i) * BLK : (3 + i) * BLK]
                scores = jnp.where(seen, dot_nt(k, q[i]), -FAR)
                p, ds = grads(scores, dot_nt(v, g[i]), lse[i], delta[i])
                acc[0, at] += dot_nn(ds, q[i])
                acc[0, (2 + i) * BLK : (3 + i) * BLK] += dot_nn(p, g[i])
                dq[i] = dq[i] + dot_tn(k, ds)
        for i in range(2):
            grad = jnp.transpose(dq[i]) * SCALE
            for h in range(GROUP):
                dq_acc[e, i * BLK : (i + 1) * BLK, h * HEAD : (h + 1) * HEAD] += grad[
                    h * BLK : (h + 1) * BLK
                ]

    acc[...] = jnp.zeros_like(acc)
    visit(x_ref[0], 0, own=own)
    visit(x_ref[1], 1)

    @pl.loop(0, 2)
    def _(e):
        visit(y_ref[e], e + 2)


def scaled(acc, rows):
    return jnp.concatenate([acc[rows, : 2 * BLK] * SCALE, acc[rows, 2 * BLK :]], axis=-2)


def with_next(x_ref, y_ref, p_ref, m_ref, e_ref, p_out, m_out, dq_out, kv, acc):
    kv[:NEAR] = p_ref[...]
    kv[NEAR : 2 * NEAR] = m_ref[...]
    kv[2 * NEAR] = e_ref[...]
    dq_out[...] = jnp.zeros_like(dq_out)
    backward(x_ref, y_ref, kv, acc, dq_out, ((0, 4), (4, 7)), False)
    p_out[...] = scaled(acc, slice(0, NEAR)).astype(BF16)
    m_out[...] = scaled(acc, slice(NEAR, 2 * NEAR + 1)).astype(BF16)


def with_nearest(x_ref, y_ref, s_ref, p_ref, m_ref, dq_ref, *rest):
    own_out, p_out, m_out, dq_out, dq_core_out, kv, acc, dq = rest
    kv[:NEAR] = s_ref[...]
    kv[NEAR : 2 * NEAR] = p_ref[...]
    kv[2 * NEAR :] = m_ref[...]
    dq[...] = dq_ref[...]
    backward(x_ref, y_ref, kv, acc, dq, ((0, 5), (5, 9)), True)
    own_out[...] = scaled(acc, slice(0, NEAR))
    p_out[...] = scaled(acc, slice(NEAR, 2 * NEAR)).astype(BF16)
    m_out[...] = scaled(acc, slice(2 * NEAR, 3 * NEAR)).astype(BF16)
    dq_out[...] = dq[:2]
    dq_core_out[...] = dq[2:].astype(BF16)


def in_terms(x, lanes):
    out = jnp.zeros(lanes.shape, F32)
    for h in range(GROUP):
        rest = x[h]
        for n in range(3):
            term = rest.astype(BF16).astype(F32)
            out = jnp.where(lanes == 8 * n + h, term, out)
            rest = rest - term
    return out


def pack_keys(pos, k_ref, v_ref, out):
    start = pl.multiple_of(jnp.where(pos[0] > pos[BLK], BLK, 0), BLK)
    other = pl.multiple_of(BLK - start, BLK)
    out[:BLK] = k_ref[pl.ds(start, BLK), :]
    out[BLK : 2 * BLK] = k_ref[pl.ds(other, BLK), :]
    out[2 * BLK : 3 * BLK] = v_ref[pl.ds(start, BLK), :]
    out[3 * BLK : 4 * BLK] = v_ref[pl.ds(other, BLK), :]
    c = jnp.minimum(pos[0], pos[BLK]) // BLK
    out[4 * BLK :] = jnp.full((16, HEAD), c, jnp.int32).astype(F32).astype(BF16)


def pack_queries(pos, q_ref, lse_ref, o_ref, g_ref, u_ref, w_ref, q_out, g_out):
    wide = GROUP * HEAD
    swapped = pos[0] > pos[BLK]
    start = pl.multiple_of(jnp.where(swapped, BLK, 0), BLK)
    lanes = lax.broadcasted_iota(jnp.int32, (BLK, HEAD), 1)
    c = jnp.minimum(pos[0], pos[BLK]) // BLK
    lse = jnp.concatenate([lse_ref[...], jnp.zeros((HEAD - GROUP, TOK), F32)])
    turned = jnp.transpose(lse)
    turned = jnp.where(swapped, jnp.concatenate([turned[BLK:], turned[:BLK]]), turned)
    for i in range(2):
        rows = pl.ds(start if i == 0 else pl.multiple_of(BLK - start, BLK), BLK)
        q_out[i * BLK : (i + 1) * BLK, :wide] = q_ref[rows, :]
        lse = turned[i * BLK : (i + 1) * BLK, :]
        tail = in_terms([lse[:, h : h + 1] for h in range(GROUP)], lanes)
        tail = jnp.where(lanes == 24, c.astype(F32), tail)
        tail = jnp.where(lanes == 25, swapped.astype(F32), tail)
        q_out[i * BLK : (i + 1) * BLK, wide:] = tail.astype(BF16)
    n_heads = g_ref.shape[1] // wide
    lanes = lax.broadcasted_iota(jnp.int32, (g_ref.shape[0], HEAD), 1)
    for d in range(n_heads):
        g = g_ref[:, d * wide : (d + 1) * wide]
        product = g.astype(F32) * o_ref[:, d * wide : (d + 1) * wide].astype(F32)
        delta = [
            jnp.sum(product[:, h * HEAD : (h + 1) * HEAD], axis=1, keepdims=True)
            for h in range(GROUP)
        ]
        tail = in_terms(delta, lanes).astype(BF16)
        for twin in range(2):
            g_out[twin * n_heads + d, :, :wide] = g
            g_out[twin * n_heads + d, :, wide:] = tail


def join(own_ref, u_ref, w_ref, e_ref, q_ref, qx_ref, grad_ref, s_out, x_out):
    s_out[0] = own_ref[...]
    s_out[1] = u_ref[...]
    s_out[2] = w_ref[...]
    wide = (GROUP + 1) * HEAD
    x_out[0, :, :wide] = q_ref[...]
    x_out[1, :, :wide] = qx_ref[...]
    half = lax.axis_index("xh")
    x_out[0, :, wide:] = grad_ref[half]
    x_out[1, :, wide:] = grad_ref[1 - half]


def sum_first(own_ref, c_ref, d_ref, p_ref, m_ref, own_out, p_out, m_out):
    own_out[...] = own_ref[...] + c_ref[...].astype(F32) + d_ref[:NEAR].astype(F32)
    p_out[: NEAR - 1] = p_ref[: NEAR - 1]
    last = p_ref[NEAR - 1].astype(F32) + d_ref[NEAR].astype(F32)
    p_out[NEAR - 1] = last.astype(BF16)
    m_out[...] = m_ref[...]


def sum_near(own_ref, p_ref, m_ref, own_out, u_out, w_out):
    total = own_ref[...] + p_ref[...].astype(F32) + m_ref[...].astype(F32)
    own_out[...] = total[0]
    u_out[...] = total[1].astype(BF16)
    w_out[...] = total[2].astype(BF16)


def sum_cores(dq_ref, core_ref, x_ref, dq_out, dqx_out, flag_out):
    dq_out[...] = dq_ref[0] + core_ref[0].astype(F32)
    dqx_out[...] = (dq_ref[1] + core_ref[1].astype(F32)).astype(BF16)
    at = GROUP * HEAD + 25
    flag_out[...] = jnp.broadcast_to(x_ref[0, :BLK, at : at + 1].astype(F32), flag_out.shape)


def finish(flag_ref, own_ref, u_ref, w_ref, dq_ref, dqx_ref, q_out, k_out, v_out):
    swapped = flag_ref[...] > 0.5
    total = own_ref[...] + u_ref[...].astype(F32) + w_ref[...].astype(F32)
    dq = dq_ref[...] + dqx_ref[...].astype(F32)
    for i in range(2):
        here, there = slice(i * BLK, (i + 1) * BLK), slice((1 - i) * BLK, (2 - i) * BLK)
        for h in range(GROUP):
            cols = slice(h * HEAD, (h + 1) * HEAD)
            q_out[here, cols] = jnp.where(swapped, dq[there, cols], dq[here, cols]).astype(BF16)
        k_out[here, :] = jnp.where(swapped, total[there], total[here]).astype(BF16)
        there, of_v = slice((3 - i) * BLK, (4 - i) * BLK), slice((2 + i) * BLK, (3 + i) * BLK)
        v_out[here, :] = jnp.where(swapped, total[there], total[of_v]).astype(BF16)


HEADS = ("xl", "y")


def by_parity(x, distance):
    n = lax.axis_size("z")
    to = [(i + (distance if i % 2 == 0 else -distance)) % n for i in range(n)]
    return lax.ppermute(x, "z", list(enumerate(to)))


def swapped_with(x, axis):
    return lax.ppermute(x, axis, [(0, 1), (1, 0)])


def local_call(body, out_shape, mib, stream_in=False, stream_out=False):
    vmem, smem = pl.BlockSpec(memory_space=pltpu.VMEM), pl.BlockSpec(memory_space=pltpu.SMEM)
    free = pl.BlockSpec()

    def call(*args, scratch=()):
        return pl.pallas_call(
            body,
            out_shape=out_shape,
            in_specs=[
                smem if a.dtype == jnp.int32 else free if stream_in else vmem for a in args
            ],
            out_specs=jax.tree.map(lambda _: free if stream_out else vmem, out_shape),
            scratch_shapes=scratch,
            compiler_params=pltpu.CompilerParams(vmem_limit_bytes=mib * 1024 * 1024),
            name=body.__name__,
        )(*args)

    return call


def shards(queries, keys, values, outputs, out_grad, lse, positions):
    n_heads = lax.axis_size(HEADS)
    wide = (GROUP + 1) * HEAD

    def like(shape, dtype=BF16):
        return jax.ShapeDtypeStruct(shape, dtype)

    packed, block = (4 * BLK + 16, HEAD), (4 * BLK, HEAD)
    own = local_call(pack_keys, like(packed), 56, stream_in=True)(positions, keys, values)
    u, w = by_parity(own, 5), by_parity(own, -5)
    e_one = by_parity(w, 3)

    own_q, send = local_call(
        pack_queries,
        (like((TOK, wide)), like((2 * n_heads, TOK // n_heads, wide))),
        8,
        stream_in=True,
    )(positions, queries, lse.T, outputs, out_grad, u, w)
    grad = lax.all_to_all(send, ("xh",) + HEADS, split_axis=0, concat_axis=0, tiled=True)
    other_q = swapped_with(own_q, "xh")
    s_set, x = local_call(
        join, (like((NEAR,) + packed), like((2, TOK, 2 * wide))), 8, stream_in=True
    )(own, u, w, e_one, own_q, other_q, grad.reshape(2, TOK, wide))
    p1, m1, p2, m2 = [by_parity(s_set, by) for by in (1, -1, 2, -2)]
    y = swapped_with(x, "core")

    near, dq_shape = (NEAR,) + block, (2, TOK, GROUP * HEAD)
    p2_g, m2_g, dq = local_call(
        with_next,
        (like(near), like((NEAR + 1,) + block), like((4,) + dq_shape[1:], F32)),
        16,
    )(
        x,
        y,
        p2,
        m2,
        e_one,
        scratch=[
            pltpu.VMEM((2 * NEAR + 1,) + packed, BF16),
            pltpu.VMEM((2 * NEAR + 1,) + block, F32),
        ],
    )
    own_g, p1_g, m1_g, dq, dq_core = local_call(
        with_nearest,
        (like(near, F32), like(near), like(near), like(dq_shape, F32), like(dq_shape)),
        16,
    )(
        x,
        y,
        s_set,
        p1,
        m1,
        dq,
        scratch=[
            pltpu.VMEM((3 * NEAR,) + packed, BF16),
            pltpu.VMEM((3 * NEAR,) + block, F32),
            pltpu.VMEM((4,) + dq_shape[1:], F32),
        ],
    )

    p2_in, m2_in = by_parity(p2_g, -2), by_parity(m2_g, 2)
    own_g, p1_g, m1_g = local_call(sum_first, (like(near, F32), like(near), like(near)), 8)(
        own_g, p2_in, m2_in, p1_g, m1_g
    )
    p1_in, m1_in = by_parity(p1_g, 1), by_parity(m1_g, -1)
    dq_core = swapped_with(dq_core, "core")
    dq, dqx, flag = local_call(
        sum_cores, (like(dq_shape[1:], F32), like(dq_shape[1:]), like((BLK, HEAD), F32)), 8
    )(dq, dq_core, x)
    dqx = swapped_with(dqx, "xh")
    own_g, u_g, w_g = local_call(sum_near, (like(block, F32), like(block), like(block)), 8)(
        own_g, p1_in, m1_in
    )
    u_g, w_g = by_parity(u_g, 5), by_parity(w_g, -5)
    return local_call(
        finish,
        (like(queries.shape), like(keys.shape), like(values.shape)),
        8,
        stream_out=True,
    )(flag, own_g, u_g, w_g, dq, dqx)


def solution(mesh):
    shape = FOLD or (2, 16, 2, 2, 4)
    split = jax.sharding.Mesh(mesh.devices.reshape(shape), ("xh", "z", "core", "xl", "y"))
    ctx, heads = ("xh", "z", "core"), ("xl", "y")
    return jax.shard_map(
        shards,
        mesh=split,
        in_specs=(
            P(ctx, heads),
            P(ctx, heads),
            P(ctx, heads),
            P(ctx + heads, None),
            P(ctx + heads, None),
            P(ctx, heads),
            P(ctx),
        ),
        out_specs=(P(ctx, heads), P(ctx, heads), P(ctx, heads)),
        check_vma=False,
    )
```

```python
import math

import jax
import jax.numpy as jnp
from jax import lax
from jax.experimental import pallas as pl
from jax.experimental.pallas import tpu as pltpu
from jax.sharding import PartitionSpec as P

HEAD = 128
BLK = 64
TOK = 2 * BLK
GROUP = 4
ROWS = GROUP * BLK
NEAR = 3
LOG2E = math.log2(math.e)
SCALE = 1.0 / math.sqrt(HEAD)
FAR = 1e30
F32 = jnp.float32
BF16 = jnp.bfloat16
FOLD = None


def dot_nt(a, b):
    return lax.dot_general(a, b, (((1,), (1,)), ((), ())), preferred_element_type=F32)


def dot_nn(a, b):
    return lax.dot_general(a, b, (((1,), (0,)), ((), ())), preferred_element_type=F32)


def dot_tn(a, b):
    return lax.dot_general(a, b, (((0,), (0,)), ((), ())), preferred_element_type=F32)


def backward(x_ref, y_ref, kv, acc, dq_acc, tiles, own):
    seen = lax.broadcasted_iota(jnp.int32, (BLK, ROWS), 0) <= (
        lax.broadcasted_iota(jnp.int32, (BLK, ROWS), 1) % BLK
    )

    def grads(scores, dprob, lse, delta):
        probs = jnp.exp2(scores * (SCALE * LOG2E) - lse)
        dscore = probs * (dprob - delta)
        return probs.astype(BF16), dscore.astype(BF16)

    def row_vectors(table):
        return [
            jnp.concatenate([table[h : h + 1, s : s + BLK] for h in range(GROUP)], axis=1)
            for s in (0, BLK)
        ]

    def half_rows(block):
        return [
            jnp.concatenate(
                [block[s : s + BLK, h * HEAD : (h + 1) * HEAD] for h in range(GROUP)], axis=0
            )
            for s in (0, BLK)
        ]

    def query_side(block):
        wide = GROUP * HEAD
        tail = jnp.transpose(block[:, wide : wide + HEAD].astype(F32))
        lse = tail[0:8, :] + tail[8:16, :] + tail[16:24, :]
        c_row, swapped = tail[24:25, :], tail[25:26, :] > 0.5
        tail = jnp.transpose(block[:, 2 * wide + HEAD :].astype(F32))
        delta = tail[0:8, :] + tail[8:16, :] + tail[16:24, :]
        d0, d1 = row_vectors(delta)
        g0, g1 = half_rows(block[:, wide + HEAD : 2 * wide + HEAD])
        two = jnp.concatenate([swapped, swapped], axis=1)
        tall = jnp.broadcast_to(swapped, (ROWS, HEAD))
        return (
            c_row,
            row_vectors(lse * LOG2E),
            (jnp.where(two, d1, d0), jnp.where(two, d0, d1)),
            half_rows(block[:, :wide]),
            (jnp.where(tall, g1, g0), jnp.where(tall, g0, g1)),
        )

    def flat(x):
        return x.reshape(x.shape[0] * x.shape[1], x.shape[2])

    def visit(block, e, own=False):
        own_c, lse, delta, q, g = query_side(block)
        (lse_early, lse_late), (delta_early, delta_late) = lse, delta
        q_late, g_late = q[1], g[1]
        q_both = jnp.concatenate(q, axis=1)
        g_both = jnp.concatenate(g, axis=1)
        dq_a = jnp.zeros((HEAD, ROWS), F32)
        dq_b = jnp.zeros((2 * HEAD, ROWS), F32)
        for first, last in tiles:
            size = last - first

            def pick(j):
                return kv[first:last, j * BLK : (j + 1) * BLK]

            c = kv[first:last, 4 * BLK : 4 * BLK + 16].astype(F32)[:, 0:1, :]
            before = c < own_c[None]
            after = c > own_c[None]
            wide = jnp.broadcast_to(before, (size, BLK, HEAD))
            k_early, k_late, v_early, v_late = [pick(j) for j in range(4)]
            k_both = jnp.concatenate(
                [flat(jnp.where(wide, k_early, 0)), flat(jnp.where(wide, 0, k_late))], axis=1
            )
            v_both = jnp.concatenate(
                [flat(jnp.where(wide, v_early, 0)), flat(jnp.where(wide, 0, v_late))], axis=1
            )
            k_early, v_early = flat(k_early), flat(v_early)
            before2 = jnp.concatenate([before, before], axis=2)
            after2 = jnp.concatenate([after, after], axis=2)
            lse_b = jnp.where(before2, lse_early[None], jnp.where(after2, lse_late[None], FAR))
            delta_b = jnp.where(before2, delta_early[None], delta_late[None])
            lse_b = jnp.broadcast_to(lse_b, (size, BLK, ROWS)).reshape(size * BLK, ROWS)
            delta_b = jnp.broadcast_to(delta_b, (size, BLK, ROWS)).reshape(size * BLK, ROWS)

            p_a, ds_a = grads(
                dot_nt(k_early, q_late), dot_nt(v_early, g_late), lse_late, delta_late
            )
            p_b, ds_b = grads(dot_nt(k_both, q_both), dot_nt(v_both, g_both), lse_b, delta_b)
            dv_a, dk_a = dot_nn(p_a, g_late), dot_nn(ds_a, q_late)
            dv_b, dk_b = dot_nn(p_b, g_both), dot_nn(ds_b, q_both)
            dq_a = dq_a + dot_tn(k_early, ds_a)
            dq_b = dq_b + dot_tn(k_both, ds_b)
            for j, one, two in ((0, dk_a, dk_b), (2, dv_a, dv_b)):
                one = one.reshape(size, BLK, HEAD)
                two = two.reshape(size, BLK, 2 * HEAD)
                acc[first:last, j * BLK : (j + 1) * BLK] += one + jnp.where(wide, two[:, :, :HEAD], 0.0)
                acc[first:last, (j + 1) * BLK : (j + 2) * BLK] += jnp.where(
                    wide, 0.0, two[:, :, HEAD:]
                )
        dq = [dq_b[:HEAD], dq_b[HEAD:] + dq_a]
        if own:
            for i in range(2):
                at = slice(i * BLK, (i + 1) * BLK)
                k, v = kv[0, at], kv[0, (2 + i) * BLK : (3 + i) * BLK]
                scores = jnp.where(seen, dot_nt(k, q[i]), -FAR)
                p, ds = grads(scores, dot_nt(v, g[i]), lse[i], delta[i])
                acc[0, at] += dot_nn(ds, q[i])
                acc[0, (2 + i) * BLK : (3 + i) * BLK] += dot_nn(p, g[i])
                dq[i] = dq[i] + dot_tn(k, ds)
        for i in range(2):
            grad = jnp.transpose(dq[i]) * SCALE
            for h in range(GROUP):
                dq_acc[e, i * BLK : (i + 1) * BLK, h * HEAD : (h + 1) * HEAD] += grad[
                    h * BLK : (h + 1) * BLK
                ]

    acc[...] = jnp.zeros_like(acc)
    visit(x_ref[0], 0, own=own)
    visit(x_ref[1], 1)

    @pl.loop(0, 2)
    def _(e):
        visit(y_ref[e], e + 2)


def scaled(acc, rows):
    return jnp.concatenate([acc[rows, : 2 * BLK] * SCALE, acc[rows, 2 * BLK :]], axis=-2)


GATHERED = ((0, 4, -4, 8), (1, -3, 5, -7), (-1, -5, 3, 7), (2, 6, -2, -6))
NEXT = (-2, 3, -7, 2, 7, -3, 8)
NEAREST = (0, 5, -5, 1, -4, 6, -1, -6, 4)


def arrange(kv, sets, order):
    at = {d: (ref, i) for ref, held in zip(sets, GATHERED) for i, d in enumerate(held)}
    for j, d in enumerate(order):
        ref, i = at[d]
        kv[j] = ref[i]


def with_next(x_ref, y_ref, s_ref, p_ref, m_ref, h_ref, p_out, m_out, dq_out, kv, acc):
    arrange(kv, (s_ref, p_ref, m_ref, h_ref), NEXT)
    dq_out[...] = jnp.zeros_like(dq_out)
    backward(x_ref, y_ref, kv, acc, dq_out, ((0, 4), (4, 7)), False)
    p_out[...] = scaled(acc, slice(0, NEAR)).astype(BF16)
    m_out[...] = scaled(acc, slice(NEAR, 2 * NEAR + 1)).astype(BF16)


def with_nearest(x_ref, y_ref, s_ref, p_ref, m_ref, h_ref, dq_ref, *rest):
    own_out, p_out, m_out, dq_out, dq_core_out, kv, acc, dq = rest
    arrange(kv, (s_ref, p_ref, m_ref, h_ref), NEAREST)
    dq[...] = dq_ref[...]
    backward(x_ref, y_ref, kv, acc, dq, ((0, 5), (5, 9)), True)
    own_out[...] = scaled(acc, slice(0, NEAR))
    p_out[...] = scaled(acc, slice(NEAR, 2 * NEAR)).astype(BF16)
    m_out[...] = scaled(acc, slice(2 * NEAR, 3 * NEAR)).astype(BF16)
    dq_out[...] = dq[:2]
    dq_core_out[...] = dq[2:].astype(BF16)


def in_terms(x, lanes):
    out = jnp.zeros(lanes.shape, F32)
    for h in range(GROUP):
        rest = x[h]
        for n in range(3):
            term = rest.astype(BF16).astype(F32)
            out = jnp.where(lanes == 8 * n + h, term, out)
            rest = rest - term
    return out


def pack_keys(pos, k_ref, v_ref, out):
    start = pl.multiple_of(jnp.where(pos[0] > pos[BLK], BLK, 0), BLK)
    other = pl.multiple_of(BLK - start, BLK)
    out[:BLK] = k_ref[pl.ds(start, BLK), :]
    out[BLK : 2 * BLK] = k_ref[pl.ds(other, BLK), :]
    out[2 * BLK : 3 * BLK] = v_ref[pl.ds(start, BLK), :]
    out[3 * BLK : 4 * BLK] = v_ref[pl.ds(other, BLK), :]
    c = jnp.minimum(pos[0], pos[BLK]) // BLK
    out[4 * BLK :] = jnp.full((16, HEAD), c, jnp.int32).astype(F32).astype(BF16)


def pack_queries(pos, q_ref, lse_ref, o_ref, g_ref, after_ref, q_out, g_out):
    wide = GROUP * HEAD
    swapped = pos[0] > pos[BLK]
    start = pl.multiple_of(jnp.where(swapped, BLK, 0), BLK)
    lanes = lax.broadcasted_iota(jnp.int32, (BLK, HEAD), 1)
    c = jnp.minimum(pos[0], pos[BLK]) // BLK
    lse = jnp.concatenate([lse_ref[...], jnp.zeros((HEAD - GROUP, TOK), F32)])
    turned = jnp.transpose(lse)
    turned = jnp.where(swapped, jnp.concatenate([turned[BLK:], turned[:BLK]]), turned)
    for i in range(2):
        rows = pl.ds(start if i == 0 else pl.multiple_of(BLK - start, BLK), BLK)
        q_out[i * BLK : (i + 1) * BLK, :wide] = q_ref[rows, :]
        lse = turned[i * BLK : (i + 1) * BLK, :]
        tail = in_terms([lse[:, h : h + 1] for h in range(GROUP)], lanes)
        tail = jnp.where(lanes == 24, c.astype(F32), tail)
        tail = jnp.where(lanes == 25, swapped.astype(F32), tail)
        q_out[i * BLK : (i + 1) * BLK, wide:] = tail.astype(BF16)
    n_heads = g_ref.shape[1] // wide
    lanes = lax.broadcasted_iota(jnp.int32, (g_ref.shape[0], HEAD), 1)
    for d in range(n_heads):
        g = g_ref[:, d * wide : (d + 1) * wide]
        product = g.astype(F32) * o_ref[:, d * wide : (d + 1) * wide].astype(F32)
        delta = [
            jnp.sum(product[:, h * HEAD : (h + 1) * HEAD], axis=1, keepdims=True)
            for h in range(GROUP)
        ]
        tail = in_terms(delta, lanes).astype(BF16)
        for twin in range(2):
            g_out[twin * n_heads + d, :, :wide] = g
            g_out[twin * n_heads + d, :, wide:] = tail


def join(own_ref, a_ref, b_ref, c_ref, q_ref, qx_ref, grad_ref, s_out, x_out):
    for i, ref in enumerate((own_ref, a_ref, b_ref, c_ref)):
        s_out[i] = ref[...]
    wide = (GROUP + 1) * HEAD
    x_out[0, :, :wide] = q_ref[...]
    x_out[1, :, :wide] = qx_ref[...]
    half = lax.axis_index("xh")
    x_out[0, :, wide:] = grad_ref[half]
    x_out[1, :, wide:] = grad_ref[1 - half]


def sum_first(own_ref, c_ref, d_ref, p_ref, m_ref, own_out, p_out, m_out):
    own_out[...] = own_ref[...] + c_ref[...].astype(F32) + d_ref[:NEAR].astype(F32)
    p_out[: NEAR - 1] = p_ref[: NEAR - 1]
    last = p_ref[NEAR - 1].astype(F32) + d_ref[NEAR].astype(F32)
    p_out[NEAR - 1] = last.astype(BF16)
    m_out[...] = m_ref[...]


def sum_near(own_ref, p_ref, m_ref, own_out, u_out, w_out):
    total = own_ref[...] + p_ref[...].astype(F32) + m_ref[...].astype(F32)
    own_out[...] = total[0]
    u_out[...] = total[1].astype(BF16)
    w_out[...] = total[2].astype(BF16)


def sum_cores(dq_ref, core_ref, x_ref, dq_out, dqx_out, flag_out):
    dq_out[...] = dq_ref[0] + core_ref[0].astype(F32)
    dqx_out[...] = (dq_ref[1] + core_ref[1].astype(F32)).astype(BF16)
    at = GROUP * HEAD + 25
    flag_out[...] = jnp.broadcast_to(x_ref[0, :BLK, at : at + 1].astype(F32), flag_out.shape)


def finish(flag_ref, own_ref, u_ref, w_ref, dq_ref, dqx_ref, q_out, k_out, v_out):
    swapped = flag_ref[...] > 0.5
    total = own_ref[...] + u_ref[...].astype(F32) + w_ref[...].astype(F32)
    dq = dq_ref[...] + dqx_ref[...].astype(F32)
    for i in range(2):
        here, there = slice(i * BLK, (i + 1) * BLK), slice((1 - i) * BLK, (2 - i) * BLK)
        for h in range(GROUP):
            cols = slice(h * HEAD, (h + 1) * HEAD)
            q_out[here, cols] = jnp.where(swapped, dq[there, cols], dq[here, cols]).astype(BF16)
        k_out[here, :] = jnp.where(swapped, total[there], total[here]).astype(BF16)
        there, of_v = slice((3 - i) * BLK, (4 - i) * BLK), slice((2 + i) * BLK, (3 + i) * BLK)
        v_out[here, :] = jnp.where(swapped, total[there], total[of_v]).astype(BF16)


HEADS = ("xl", "y")


def by_parity(x, distance):
    n = lax.axis_size("z")
    to = [(i + (distance if i % 2 == 0 else -distance)) % n for i in range(n)]
    return lax.ppermute(x, "z", list(enumerate(to)))


def half_round(x):
    n = lax.axis_size("z")
    return lax.ppermute(x, "z", [(i, (i + n // 2) % n) for i in range(n)])


def swapped_with(x, axis):
    return lax.ppermute(x, axis, [(0, 1), (1, 0)])


def local_call(body, out_shape, mib, stream_in=False, stream_out=False):
    vmem, smem = pl.BlockSpec(memory_space=pltpu.VMEM), pl.BlockSpec(memory_space=pltpu.SMEM)
    free = pl.BlockSpec()

    def call(*args, scratch=()):
        return pl.pallas_call(
            body,
            out_shape=out_shape,
            in_specs=[
                smem if a.dtype == jnp.int32 else free if stream_in else vmem for a in args
            ],
            out_specs=jax.tree.map(lambda _: free if stream_out else vmem, out_shape),
            scratch_shapes=scratch,
            compiler_params=pltpu.CompilerParams(vmem_limit_bytes=mib * 1024 * 1024),
            name=body.__name__,
        )(*args)

    return call


def shards(queries, keys, values, outputs, out_grad, lse, positions):
    n_heads = lax.axis_size(HEADS)
    wide = (GROUP + 1) * HEAD

    def like(shape, dtype=BF16):
        return jax.ShapeDtypeStruct(shape, dtype)

    packed, block = (4 * BLK + 16, HEAD), (4 * BLK, HEAD)
    own = local_call(pack_keys, like(packed), 56, stream_in=True)(positions, keys, values)
    far = [by_parity(own, -4), by_parity(own, 4), half_round(own)]

    own_q, send = local_call(
        pack_queries,
        (like((TOK, wide)), like((2 * n_heads, TOK // n_heads, wide))),
        56,
        stream_in=True,
    )(positions, queries, lse.T, outputs, out_grad, own)
    grad = lax.all_to_all(send, ("xh",) + HEADS, split_axis=0, concat_axis=0, tiled=True)
    other_q = swapped_with(own_q, "xh")
    s_set, x = local_call(
        join, (like((4,) + packed), like((2, TOK, 2 * wide))), 8, stream_in=True
    )(own, *far, own_q, other_q, grad.reshape(2, TOK, wide))
    sets = [s_set] + [by_parity(s_set, by) for by in (1, -1, -2)]
    y = swapped_with(x, "core")

    near, dq_shape = (NEAR,) + block, (2, TOK, GROUP * HEAD)
    p2_g, m2_g, dq = local_call(
        with_next,
        (like(near), like((NEAR + 1,) + block), like((4,) + dq_shape[1:], F32)),
        16,
    )(
        x,
        y,
        *sets,
        scratch=[
            pltpu.VMEM((2 * NEAR + 1,) + packed, BF16),
            pltpu.VMEM((2 * NEAR + 1,) + block, F32),
        ],
    )
    own_g, p1_g, m1_g, dq, dq_core = local_call(
        with_nearest,
        (like(near, F32), like(near), like(near), like(dq_shape, F32), like(dq_shape)),
        16,
    )(
        x,
        y,
        *sets,
        dq,
        scratch=[
            pltpu.VMEM((3 * NEAR,) + packed, BF16),
            pltpu.VMEM((3 * NEAR,) + block, F32),
            pltpu.VMEM((4,) + dq_shape[1:], F32),
        ],
    )

    p2_in, m2_in = by_parity(p2_g, -2), by_parity(m2_g, 2)
    own_g, p1_g, m1_g = local_call(sum_first, (like(near, F32), like(near), like(near)), 8)(
        own_g, p2_in, m2_in, p1_g, m1_g
    )
    p1_in, m1_in = by_parity(p1_g, 1), by_parity(m1_g, -1)
    dq_core = swapped_with(dq_core, "core")
    dq, dqx, flag = local_call(
        sum_cores, (like(dq_shape[1:], F32), like(dq_shape[1:]), like((BLK, HEAD), F32)), 8
    )(dq, dq_core, x)
    dqx = swapped_with(dqx, "xh")
    own_g, u_g, w_g = local_call(sum_near, (like(block, F32), like(block), like(block)), 8)(
        own_g, p1_in, m1_in
    )
    u_g, w_g = by_parity(u_g, 5), by_parity(w_g, -5)
    return local_call(
        finish,
        (like(queries.shape), like(keys.shape), like(values.shape)),
        8,
        stream_out=True,
    )(flag, own_g, u_g, w_g, dq, dqx)


def solution(mesh):
    shape = FOLD or (2, 16, 2, 2, 4)
    split = jax.sharding.Mesh(mesh.devices.reshape(shape), ("xh", "z", "core", "xl", "y"))
    ctx, heads = ("xh", "z", "core"), ("xl", "y")
    return jax.shard_map(
        shards,
        mesh=split,
        in_specs=(
            P(ctx, heads),
            P(ctx, heads),
            P(ctx, heads),
            P(ctx + heads, None),
            P(ctx + heads, None),
            P(ctx, heads),
            P(ctx),
        ),
        out_specs=(P(ctx, heads), P(ctx, heads), P(ctx, heads)),
        check_vma=False,
    )
```

```python
import math

import jax
import jax.numpy as jnp
from jax import lax
from jax.experimental import pallas as pl
from jax.experimental.pallas import tpu as pltpu
from jax.sharding import PartitionSpec as P

HEAD = 128
BLK = 64
TOK = 2 * BLK
GROUP = 4
ROWS = GROUP * BLK
NEAR = 3
LOG2E = math.log2(math.e)
SCALE = 1.0 / math.sqrt(HEAD)
FAR = 1e30
F32 = jnp.float32
BF16 = jnp.bfloat16
FOLD = None


def dot_nt(a, b):
    return lax.dot_general(a, b, (((1,), (1,)), ((), ())), preferred_element_type=F32)


def dot_nn(a, b):
    return lax.dot_general(a, b, (((1,), (0,)), ((), ())), preferred_element_type=F32)


def dot_tn(a, b):
    return lax.dot_general(a, b, (((0,), (0,)), ((), ())), preferred_element_type=F32)


def backward(x_ref, y_ref, kv, acc, dq_acc, tiles, own):
    seen = lax.broadcasted_iota(jnp.int32, (BLK, ROWS), 0) <= (
        lax.broadcasted_iota(jnp.int32, (BLK, ROWS), 1) % BLK
    )

    def grads(scores, dprob, lse, delta):
        probs = jnp.exp2(scores * (SCALE * LOG2E) - lse)
        dscore = probs * (dprob - delta)
        return probs.astype(BF16), dscore.astype(BF16)

    def row_vectors(table):
        return [
            jnp.concatenate([table[h : h + 1, s : s + BLK] for h in range(GROUP)], axis=1)
            for s in (0, BLK)
        ]

    def half_rows(block):
        return [
            jnp.concatenate(
                [block[s : s + BLK, h * HEAD : (h + 1) * HEAD] for h in range(GROUP)], axis=0
            )
            for s in (0, BLK)
        ]

    def query_side(block):
        wide = GROUP * HEAD
        tail = jnp.transpose(block[:, wide : wide + HEAD].astype(F32))
        lse = tail[0:8, :] + tail[8:16, :] + tail[16:24, :]
        c_row, swapped = tail[24:25, :], tail[25:26, :] > 0.5
        tail = jnp.transpose(block[:, 2 * wide + HEAD :].astype(F32))
        delta = tail[0:8, :] + tail[8:16, :] + tail[16:24, :]
        d0, d1 = row_vectors(delta)
        g0, g1 = half_rows(block[:, wide + HEAD : 2 * wide + HEAD])
        two = jnp.concatenate([swapped, swapped], axis=1)
        tall = jnp.broadcast_to(swapped, (ROWS, HEAD))
        return (
            c_row,
            row_vectors(lse * LOG2E),
            (jnp.where(two, d1, d0), jnp.where(two, d0, d1)),
            half_rows(block[:, :wide]),
            (jnp.where(tall, g1, g0), jnp.where(tall, g0, g1)),
        )

    def flat(x):
        return x.reshape(x.shape[0] * x.shape[1], x.shape[2])

    def visit(block, e, own=False):
        own_c, lse, delta, q, g = query_side(block)
        (lse_early, lse_late), (delta_early, delta_late) = lse, delta
        q_late, g_late = q[1], g[1]
        q_both = jnp.concatenate(q, axis=1)
        g_both = jnp.concatenate(g, axis=1)
        dq_a = jnp.zeros((HEAD, ROWS), F32)
        dq_b = jnp.zeros((2 * HEAD, ROWS), F32)
        for first, last in tiles:
            size = last - first

            def pick(j):
                return kv[first:last, j * BLK : (j + 1) * BLK]

            c = kv[first:last, 4 * BLK : 4 * BLK + 16].astype(F32)[:, 0:1, :]
            before = c < own_c[None]
            after = c > own_c[None]
            wide = jnp.broadcast_to(before, (size, BLK, HEAD))
            k_early, k_late, v_early, v_late = [pick(j) for j in range(4)]
            k_both = jnp.concatenate(
                [flat(jnp.where(wide, k_early, 0)), flat(jnp.where(wide, 0, k_late))], axis=1
            )
            v_both = jnp.concatenate(
                [flat(jnp.where(wide, v_early, 0)), flat(jnp.where(wide, 0, v_late))], axis=1
            )
            k_early, v_early = flat(k_early), flat(v_early)
            before2 = jnp.concatenate([before, before], axis=2)
            after2 = jnp.concatenate([after, after], axis=2)
            lse_b = jnp.where(before2, lse_early[None], jnp.where(after2, lse_late[None], FAR))
            delta_b = jnp.where(before2, delta_early[None], delta_late[None])
            lse_b = jnp.broadcast_to(lse_b, (size, BLK, ROWS)).reshape(size * BLK, ROWS)
            delta_b = jnp.broadcast_to(delta_b, (size, BLK, ROWS)).reshape(size * BLK, ROWS)

            p_a, ds_a = grads(
                dot_nt(k_early, q_late), dot_nt(v_early, g_late), lse_late, delta_late
            )
            p_b, ds_b = grads(dot_nt(k_both, q_both), dot_nt(v_both, g_both), lse_b, delta_b)
            dv_a, dk_a = dot_nn(p_a, g_late), dot_nn(ds_a, q_late)
            dv_b, dk_b = dot_nn(p_b, g_both), dot_nn(ds_b, q_both)
            dq_a = dq_a + dot_tn(k_early, ds_a)
            dq_b = dq_b + dot_tn(k_both, ds_b)
            for j, one, two in ((0, dk_a, dk_b), (2, dv_a, dv_b)):
                one = one.reshape(size, BLK, HEAD)
                two = two.reshape(size, BLK, 2 * HEAD)
                acc[first:last, j * BLK : (j + 1) * BLK] += one + jnp.where(wide, two[:, :, :HEAD], 0.0)
                acc[first:last, (j + 1) * BLK : (j + 2) * BLK] += jnp.where(
                    wide, 0.0, two[:, :, HEAD:]
                )
        dq = [dq_b[:HEAD], dq_b[HEAD:] + dq_a]
        if own:
            for i in range(2):
                at = slice(i * BLK, (i + 1) * BLK)
                k, v = kv[0, at], kv[0, (2 + i) * BLK : (3 + i) * BLK]
                scores = jnp.where(seen, dot_nt(k, q[i]), -FAR)
                p, ds = grads(scores, dot_nt(v, g[i]), lse[i], delta[i])
                acc[0, at] += dot_nn(ds, q[i])
                acc[0, (2 + i) * BLK : (3 + i) * BLK] += dot_nn(p, g[i])
                dq[i] = dq[i] + dot_tn(k, ds)
        for i in range(2):
            grad = jnp.transpose(dq[i]) * SCALE
            for h in range(GROUP):
                dq_acc[e, i * BLK : (i + 1) * BLK, h * HEAD : (h + 1) * HEAD] += grad[
                    h * BLK : (h + 1) * BLK
                ]

    acc[...] = jnp.zeros_like(acc)
    visit(x_ref[0], 0, own=own)
    visit(x_ref[1], 1)

    @pl.loop(0, 2)
    def _(e):
        visit(y_ref[e], e + 2)


def scaled(acc, rows):
    return jnp.concatenate([acc[rows, : 2 * BLK] * SCALE, acc[rows, 2 * BLK :]], axis=-2)


OWN = (0, 4, -4, 8)
GATHERED = ((1, -3, 5, -7), (-1, -5, 3, 7), (2, 6, -2, -6))
NEXT = (-2, 3, -7, 2, 7, -3)
NEAREST = (5, -5, 1, 6, -1, -6)


def arrange(kv, sets, order):
    at = {d: (ref, i) for ref, held in zip(sets, GATHERED) for i, d in enumerate(held)}
    for j, d in enumerate(order):
        ref, i = at[d]
        kv[j] = ref[i]


def with_own(x_ref, y_ref, s_ref, grad_out, dq_out, acc):
    dq_out[...] = jnp.zeros_like(dq_out)
    backward(x_ref, y_ref, s_ref, acc, dq_out, ((0, 4),), True)
    grad_out[...] = scaled(acc, slice(0, 4))


def with_next(x_ref, y_ref, p_ref, m_ref, h_ref, g_ref, dq_ref, p_out, m_out, dq_out, kv, acc):
    arrange(kv, (p_ref, m_ref, h_ref), NEXT)
    dq_out[...] = dq_ref[...]
    backward(x_ref, y_ref, kv, acc, dq_out, ((0, 3), (3, 6)), False)
    p_out[...] = scaled(acc, slice(0, NEAR)).astype(BF16)
    m_out[:NEAR] = scaled(acc, slice(NEAR, 2 * NEAR)).astype(BF16)
    m_out[NEAR] = g_ref[OWN.index(8)].astype(BF16)


def with_nearest(x_ref, y_ref, p_ref, m_ref, h_ref, g_ref, dq_ref, *rest):
    own_out, p_out, m_out, dq_out, dq_core_out, kv, acc, dq = rest
    arrange(kv, (p_ref, m_ref, h_ref), NEAREST)
    dq[...] = dq_ref[...]
    backward(x_ref, y_ref, kv, acc, dq, ((0, 3), (3, 6)), False)
    for out, held in ((own_out, (0, 5, -5)), (p_out, (1, -4, 6)), (m_out, (-1, -6, 4))):
        for i, d in enumerate(held):
            grad = g_ref[OWN.index(d)] if d in OWN else scaled(acc, NEAREST.index(d))
            out[i] = grad.astype(out.dtype)
    dq_out[...] = dq[:2]
    dq_core_out[...] = dq[2:].astype(BF16)


def in_terms(x, lanes):
    out = jnp.zeros(lanes.shape, F32)
    for h in range(GROUP):
        rest = x[h]
        for n in range(3):
            term = rest.astype(BF16).astype(F32)
            out = jnp.where(lanes == 8 * n + h, term, out)
            rest = rest - term
    return out


def pack_keys(pos, k_ref, v_ref, out):
    start = pl.multiple_of(jnp.where(pos[0] > pos[BLK], BLK, 0), BLK)
    other = pl.multiple_of(BLK - start, BLK)
    out[:BLK] = k_ref[pl.ds(start, BLK), :]
    out[BLK : 2 * BLK] = k_ref[pl.ds(other, BLK), :]
    out[2 * BLK : 3 * BLK] = v_ref[pl.ds(start, BLK), :]
    out[3 * BLK : 4 * BLK] = v_ref[pl.ds(other, BLK), :]
    c = jnp.minimum(pos[0], pos[BLK]) // BLK
    out[4 * BLK :] = jnp.full((16, HEAD), c, jnp.int32).astype(F32).astype(BF16)


def pack_queries(pos, q_ref, lse_ref, o_ref, g_ref, after_ref, q_out, g_out):
    wide = GROUP * HEAD
    swapped = pos[0] > pos[BLK]
    start = pl.multiple_of(jnp.where(swapped, BLK, 0), BLK)
    lanes = lax.broadcasted_iota(jnp.int32, (BLK, HEAD), 1)
    c = jnp.minimum(pos[0], pos[BLK]) // BLK
    lse = jnp.concatenate([lse_ref[...], jnp.zeros((HEAD - GROUP, TOK), F32)])
    turned = jnp.transpose(lse)
    turned = jnp.where(swapped, jnp.concatenate([turned[BLK:], turned[:BLK]]), turned)
    for i in range(2):
        rows = pl.ds(start if i == 0 else pl.multiple_of(BLK - start, BLK), BLK)
        q_out[i * BLK : (i + 1) * BLK, :wide] = q_ref[rows, :]
        lse = turned[i * BLK : (i + 1) * BLK, :]
        tail = in_terms([lse[:, h : h + 1] for h in range(GROUP)], lanes)
        tail = jnp.where(lanes == 24, c.astype(F32), tail)
        tail = jnp.where(lanes == 25, swapped.astype(F32), tail)
        q_out[i * BLK : (i + 1) * BLK, wide:] = tail.astype(BF16)
    n_heads = g_ref.shape[1] // wide
    lanes = lax.broadcasted_iota(jnp.int32, (g_ref.shape[0], HEAD), 1)
    for d in range(n_heads):
        g = g_ref[:, d * wide : (d + 1) * wide]
        product = g.astype(F32) * o_ref[:, d * wide : (d + 1) * wide].astype(F32)
        delta = [
            jnp.sum(product[:, h * HEAD : (h + 1) * HEAD], axis=1, keepdims=True)
            for h in range(GROUP)
        ]
        tail = in_terms(delta, lanes).astype(BF16)
        for twin in range(2):
            g_out[twin * n_heads + d, :, :wide] = g
            g_out[twin * n_heads + d, :, wide:] = tail


def join(own_ref, a_ref, b_ref, c_ref, q_ref, qx_ref, grad_ref, s_out, x_out):
    for i, ref in enumerate((own_ref, a_ref, b_ref, c_ref)):
        s_out[i] = ref[...]
    wide = (GROUP + 1) * HEAD
    x_out[0, :, :wide] = q_ref[...]
    x_out[1, :, :wide] = qx_ref[...]
    half = lax.axis_index("xh")
    x_out[0, :, wide:] = grad_ref[half]
    x_out[1, :, wide:] = grad_ref[1 - half]


def sum_first(own_ref, c_ref, d_ref, p_ref, m_ref, own_out, p_out, m_out):
    own_out[...] = own_ref[...] + c_ref[...].astype(F32) + d_ref[:NEAR].astype(F32)
    p_out[: NEAR - 1] = p_ref[: NEAR - 1]
    last = p_ref[NEAR - 1].astype(F32) + d_ref[NEAR].astype(F32)
    p_out[NEAR - 1] = last.astype(BF16)
    m_out[...] = m_ref[...]


def sum_near(own_ref, p_ref, m_ref, own_out, u_out, w_out):
    total = own_ref[...] + p_ref[...].astype(F32) + m_ref[...].astype(F32)
    own_out[...] = total[0]
    u_out[...] = total[1].astype(BF16)
    w_out[...] = total[2].astype(BF16)


def sum_cores(dq_ref, core_ref, x_ref, dq_out, dqx_out, flag_out):
    dq_out[...] = dq_ref[0] + core_ref[0].astype(F32)
    dqx_out[...] = (dq_ref[1] + core_ref[1].astype(F32)).astype(BF16)
    at = GROUP * HEAD + 25
    flag_out[...] = jnp.broadcast_to(x_ref[0, :BLK, at : at + 1].astype(F32), flag_out.shape)


def finish(flag_ref, own_ref, u_ref, w_ref, dq_ref, dqx_ref, q_out, k_out, v_out):
    swapped = flag_ref[...] > 0.5
    total = own_ref[...] + u_ref[...].astype(F32) + w_ref[...].astype(F32)
    dq = dq_ref[...] + dqx_ref[...].astype(F32)
    for i in range(2):
        here, there = slice(i * BLK, (i + 1) * BLK), slice((1 - i) * BLK, (2 - i) * BLK)
        for h in range(GROUP):
            cols = slice(h * HEAD, (h + 1) * HEAD)
            q_out[here, cols] = jnp.where(swapped, dq[there, cols], dq[here, cols]).astype(BF16)
        k_out[here, :] = jnp.where(swapped, total[there], total[here]).astype(BF16)
        there, of_v = slice((3 - i) * BLK, (4 - i) * BLK), slice((2 + i) * BLK, (3 + i) * BLK)
        v_out[here, :] = jnp.where(swapped, total[there], total[of_v]).astype(BF16)


HEADS = ("xl", "y")


def by_parity(x, distance):
    n = lax.axis_size("z")
    to = [(i + (distance if i % 2 == 0 else -distance)) % n for i in range(n)]
    return lax.ppermute(x, "z", list(enumerate(to)))


def half_round(x):
    n = lax.axis_size("z")
    return lax.ppermute(x, "z", [(i, (i + n // 2) % n) for i in range(n)])


def swapped_with(x, axis):
    return lax.ppermute(x, axis, [(0, 1), (1, 0)])


def local_call(body, out_shape, mib, stream_in=False, stream_out=False):
    vmem, smem = pl.BlockSpec(memory_space=pltpu.VMEM), pl.BlockSpec(memory_space=pltpu.SMEM)
    free = pl.BlockSpec()

    def call(*args, scratch=()):
        return pl.pallas_call(
            body,
            out_shape=out_shape,
            in_specs=[
                smem if a.dtype == jnp.int32 else free if stream_in else vmem for a in args
            ],
            out_specs=jax.tree.map(lambda _: free if stream_out else vmem, out_shape),
            scratch_shapes=scratch,
            compiler_params=pltpu.CompilerParams(vmem_limit_bytes=mib * 1024 * 1024),
            name=body.__name__,
        )(*args)

    return call


def shards(queries, keys, values, outputs, out_grad, lse, positions):
    n_heads = lax.axis_size(HEADS)
    wide = (GROUP + 1) * HEAD

    def like(shape, dtype=BF16):
        return jax.ShapeDtypeStruct(shape, dtype)

    packed, block = (4 * BLK + 16, HEAD), (4 * BLK, HEAD)
    own = local_call(pack_keys, like(packed), 56, stream_in=True)(positions, keys, values)
    far = [by_parity(own, -4), by_parity(own, 4), half_round(own)]

    own_q, send = local_call(
        pack_queries,
        (like((TOK, wide)), like((2 * n_heads, TOK // n_heads, wide))),
        56,
        stream_in=True,
    )(positions, queries, lse.T, outputs, out_grad, own)
    grad = lax.all_to_all(send, ("xh",) + HEADS, split_axis=0, concat_axis=0, tiled=True)
    other_q = swapped_with(own_q, "xh")
    s_set, x = local_call(
        join, (like((4,) + packed), like((2, TOK, 2 * wide))), 8, stream_in=True
    )(own, *far, own_q, other_q, grad.reshape(2, TOK, wide))
    sets = [by_parity(s_set, by) for by in (1, -1, -2)]
    y = swapped_with(x, "core")

    near, dq_shape = (NEAR,) + block, (2, TOK, GROUP * HEAD)
    own_g, dq = local_call(
        with_own, (like((4,) + block, F32), like((4,) + dq_shape[1:], F32)), 16
    )(x, y, s_set, scratch=[pltpu.VMEM((4,) + block, F32)])
    p2_g, m2_g, dq = local_call(
        with_next,
        (like(near), like((NEAR + 1,) + block), like((4,) + dq_shape[1:], F32)),
        16,
    )(
        x,
        y,
        *sets,
        own_g,
        dq,
        scratch=[
            pltpu.VMEM((2 * NEAR,) + packed, BF16),
            pltpu.VMEM((2 * NEAR,) + block, F32),
        ],
    )
    own_g, p1_g, m1_g, dq, dq_core = local_call(
        with_nearest,
        (like(near, F32), like(near), like(near), like(dq_shape, F32), like(dq_shape)),
        16,
    )(
        x,
        y,
        *sets,
        own_g,
        dq,
        scratch=[
            pltpu.VMEM((2 * NEAR,) + packed, BF16),
            pltpu.VMEM((2 * NEAR,) + block, F32),
            pltpu.VMEM((4,) + dq_shape[1:], F32),
        ],
    )

    p2_in, m2_in = by_parity(p2_g, -2), by_parity(m2_g, 2)
    own_g, p1_g, m1_g = local_call(sum_first, (like(near, F32), like(near), like(near)), 8)(
        own_g, p2_in, m2_in, p1_g, m1_g
    )
    p1_in, m1_in = by_parity(p1_g, 1), by_parity(m1_g, -1)
    dq_core = swapped_with(dq_core, "core")
    dq, dqx, flag = local_call(
        sum_cores, (like(dq_shape[1:], F32), like(dq_shape[1:]), like((BLK, HEAD), F32)), 8
    )(dq, dq_core, x)
    dqx = swapped_with(dqx, "xh")
    own_g, u_g, w_g = local_call(sum_near, (like(block, F32), like(block), like(block)), 8)(
        own_g, p1_in, m1_in
    )
    u_g, w_g = by_parity(u_g, 5), by_parity(w_g, -5)
    return local_call(
        finish,
        (like(queries.shape), like(keys.shape), like(values.shape)),
        8,
        stream_out=True,
    )(flag, own_g, u_g, w_g, dq, dqx)


def solution(mesh):
    shape = FOLD or (2, 16, 2, 2, 4)
    split = jax.sharding.Mesh(mesh.devices.reshape(shape), ("xh", "z", "core", "xl", "y"))
    ctx, heads = ("xh", "z", "core"), ("xl", "y")
    return jax.shard_map(
        shards,
        mesh=split,
        in_specs=(
            P(ctx, heads),
            P(ctx, heads),
            P(ctx, heads),
            P(ctx + heads, None),
            P(ctx + heads, None),
            P(ctx, heads),
            P(ctx),
        ),
        out_specs=(P(ctx, heads), P(ctx, heads), P(ctx, heads)),
        check_vma=False,
    )
```

```python
import math

import jax
import jax.numpy as jnp
from jax import lax
from jax.experimental import pallas as pl
from jax.experimental.pallas import tpu as pltpu
from jax.sharding import PartitionSpec as P

HEAD = 128
BLK = 64
TOK = 2 * BLK
GROUP = 4
ROWS = GROUP * BLK
NEAR = 3
LOG2E = math.log2(math.e)
SCALE = 1.0 / math.sqrt(HEAD)
FAR = 1e30
F32 = jnp.float32
BF16 = jnp.bfloat16
FOLD = None


def dot_nt(a, b):
    return lax.dot_general(a, b, (((1,), (1,)), ((), ())), preferred_element_type=F32)


def dot_nn(a, b):
    return lax.dot_general(a, b, (((1,), (0,)), ((), ())), preferred_element_type=F32)


def dot_tn(a, b):
    return lax.dot_general(a, b, (((0,), (0,)), ((), ())), preferred_element_type=F32)


def backward(x_ref, y_ref, kv, acc, dq_acc, tiles, own):
    seen = lax.broadcasted_iota(jnp.int32, (BLK, ROWS), 0) <= (
        lax.broadcasted_iota(jnp.int32, (BLK, ROWS), 1) % BLK
    )

    def grads(scores, dprob, lse, delta):
        probs = jnp.exp2(scores * (SCALE * LOG2E) - lse)
        dscore = probs * (dprob - delta)
        return probs.astype(BF16), dscore.astype(BF16)

    def row_vectors(table):
        return [
            jnp.concatenate([table[h : h + 1, s : s + BLK] for h in range(GROUP)], axis=1)
            for s in (0, BLK)
        ]

    def half_rows(block):
        return [
            jnp.concatenate(
                [block[s : s + BLK, h * HEAD : (h + 1) * HEAD] for h in range(GROUP)], axis=0
            )
            for s in (0, BLK)
        ]

    def query_side(block):
        wide = GROUP * HEAD
        tail = jnp.transpose(block[:, wide : wide + HEAD].astype(F32))
        lse = tail[0:8, :] + tail[8:16, :] + tail[16:24, :]
        c_row, swapped = tail[24:25, :], tail[25:26, :] > 0.5
        tail = jnp.transpose(block[:, 2 * wide + HEAD :].astype(F32))
        delta = tail[0:8, :] + tail[8:16, :] + tail[16:24, :]
        d0, d1 = row_vectors(delta)
        g0, g1 = half_rows(block[:, wide + HEAD : 2 * wide + HEAD])
        two = jnp.concatenate([swapped, swapped], axis=1)
        tall = jnp.broadcast_to(swapped, (ROWS, HEAD))
        return (
            c_row,
            row_vectors(lse * LOG2E),
            (jnp.where(two, d1, d0), jnp.where(two, d0, d1)),
            half_rows(block[:, :wide]),
            (jnp.where(tall, g1, g0), jnp.where(tall, g0, g1)),
        )

    def flat(x):
        return x.reshape(x.shape[0] * x.shape[1], x.shape[2])

    def visit(block, e, own=False):
        own_c, lse, delta, q, g = query_side(block)
        (lse_early, lse_late), (delta_early, delta_late) = lse, delta
        q_late, g_late = q[1], g[1]
        q_both = jnp.concatenate(q, axis=1)
        g_both = jnp.concatenate(g, axis=1)
        dq_a = jnp.zeros((HEAD, ROWS), F32)
        dq_b = jnp.zeros((2 * HEAD, ROWS), F32)
        for first, last in tiles:
            size = last - first

            def pick(j):
                return kv[first:last, j * BLK : (j + 1) * BLK]

            c = kv[first:last, 4 * BLK : 4 * BLK + 16].astype(F32)[:, 0:1, :]
            before = c < own_c[None]
            after = c > own_c[None]
            wide = jnp.broadcast_to(before, (size, BLK, HEAD))
            k_early, k_late, v_early, v_late = [pick(j) for j in range(4)]
            k_both = jnp.concatenate(
                [flat(jnp.where(wide, k_early, 0)), flat(jnp.where(wide, 0, k_late))], axis=1
            )
            v_both = jnp.concatenate(
                [flat(jnp.where(wide, v_early, 0)), flat(jnp.where(wide, 0, v_late))], axis=1
            )
            k_early, v_early = flat(k_early), flat(v_early)
            before2 = jnp.concatenate([before, before], axis=2)
            after2 = jnp.concatenate([after, after], axis=2)
            lse_b = jnp.where(before2, lse_early[None], jnp.where(after2, lse_late[None], FAR))
            delta_b = jnp.where(before2, delta_early[None], delta_late[None])
            lse_b = jnp.broadcast_to(lse_b, (size, BLK, ROWS)).reshape(size * BLK, ROWS)
            delta_b = jnp.broadcast_to(delta_b, (size, BLK, ROWS)).reshape(size * BLK, ROWS)

            p_a, ds_a = grads(
                dot_nt(k_early, q_late), dot_nt(v_early, g_late), lse_late, delta_late
            )
            p_b, ds_b = grads(dot_nt(k_both, q_both), dot_nt(v_both, g_both), lse_b, delta_b)
            dv_a, dk_a = dot_nn(p_a, g_late), dot_nn(ds_a, q_late)
            dv_b, dk_b = dot_nn(p_b, g_both), dot_nn(ds_b, q_both)
            dq_a = dq_a + dot_tn(k_early, ds_a)
            dq_b = dq_b + dot_tn(k_both, ds_b)
            for j, one, two in ((0, dk_a, dk_b), (2, dv_a, dv_b)):
                one = one.reshape(size, BLK, HEAD)
                two = two.reshape(size, BLK, 2 * HEAD)
                acc[first:last, j * BLK : (j + 1) * BLK] += one + jnp.where(wide, two[:, :, :HEAD], 0.0)
                acc[first:last, (j + 1) * BLK : (j + 2) * BLK] += jnp.where(
                    wide, 0.0, two[:, :, HEAD:]
                )
        dq = [dq_b[:HEAD], dq_b[HEAD:] + dq_a]
        if own:
            for i in range(2):
                at = slice(i * BLK, (i + 1) * BLK)
                k, v = kv[0, at], kv[0, (2 + i) * BLK : (3 + i) * BLK]
                scores = jnp.where(seen, dot_nt(k, q[i]), -FAR)
                p, ds = grads(scores, dot_nt(v, g[i]), lse[i], delta[i])
                acc[0, at] += dot_nn(ds, q[i])
                acc[0, (2 + i) * BLK : (3 + i) * BLK] += dot_nn(p, g[i])
                dq[i] = dq[i] + dot_tn(k, ds)
        for i in range(2):
            grad = jnp.transpose(dq[i]) * SCALE
            for h in range(GROUP):
                dq_acc[e, i * BLK : (i + 1) * BLK, h * HEAD : (h + 1) * HEAD] += grad[
                    h * BLK : (h + 1) * BLK
                ]

    acc[...] = jnp.zeros_like(acc)
    visit(x_ref[0], 0, own=own)
    visit(x_ref[1], 1)

    @pl.loop(0, 2)
    def _(e):
        visit(y_ref[e], e + 2)


def scaled(acc, rows):
    return jnp.concatenate([acc[rows, : 2 * BLK] * SCALE, acc[rows, 2 * BLK :]], axis=-2)


OWN = (0, 4, -4, 8)
GATHERED = ((1, -3, 5, -7), (-1, -5, 3, 7), (2, 6, -2, -6))
NEXT = (-2, 3, -7, 2, 7, -3)
NEAREST = (5, -5, 1, 6, -1, -6)


def arrange(kv, sets, order):
    at = {d: (ref, i) for ref, held in zip(sets, GATHERED) for i, d in enumerate(held)}
    for j, d in enumerate(order):
        ref, i = at[d]
        kv[j] = ref[i]


def with_own(x_ref, y_ref, s_ref, grad_out, dq_out, acc):
    dq_out[...] = jnp.zeros_like(dq_out)
    backward(x_ref, y_ref, s_ref, acc, dq_out, ((0, 4),), True)
    grad_out[...] = scaled(acc, slice(0, 4))


def with_next(x_ref, y_ref, p_ref, m_ref, h_ref, g_ref, dq_ref, p_out, m_out, dq_out, kv, acc):
    arrange(kv, (p_ref, m_ref, h_ref), NEXT)
    dq_out[...] = dq_ref[...]
    backward(x_ref, y_ref, kv, acc, dq_out, ((0, 3), (3, 6)), False)
    p_out[...] = scaled(acc, slice(0, NEAR)).astype(BF16)
    m_out[:NEAR] = scaled(acc, slice(NEAR, 2 * NEAR)).astype(BF16)
    m_out[NEAR] = g_ref[OWN.index(8)].astype(BF16)


def with_nearest(x_ref, y_ref, p_ref, m_ref, h_ref, g_ref, dq_ref, *rest):
    own_out, p_out, m_out, dq_out, dq_core_out, kv, acc, dq = rest
    arrange(kv, (p_ref, m_ref, h_ref), NEAREST)
    dq[...] = dq_ref[...]
    backward(x_ref, y_ref, kv, acc, dq, ((0, 3), (3, 6)), False)
    for out, held in ((own_out, (0, 5, -5)), (p_out, (1, -4, 6)), (m_out, (-1, -6, 4))):
        for i, d in enumerate(held):
            grad = g_ref[OWN.index(d)] if d in OWN else scaled(acc, NEAREST.index(d))
            out[i] = grad.astype(out.dtype)
    dq_out[...] = dq[:2]
    dq_core_out[...] = dq[2:].astype(BF16)


def in_terms(x, lanes):
    out = jnp.zeros(lanes.shape, F32)
    for h in range(GROUP):
        rest = x[h]
        for n in range(3):
            term = rest.astype(BF16).astype(F32)
            out = jnp.where(lanes == 8 * n + h, term, out)
            rest = rest - term
    return out


def pack_keys(pos, k_ref, v_ref, out):
    start = pl.multiple_of(jnp.where(pos[0] > pos[BLK], BLK, 0), BLK)
    other = pl.multiple_of(BLK - start, BLK)
    out[:BLK] = k_ref[pl.ds(start, BLK), :]
    out[BLK : 2 * BLK] = k_ref[pl.ds(other, BLK), :]
    out[2 * BLK : 3 * BLK] = v_ref[pl.ds(start, BLK), :]
    out[3 * BLK : 4 * BLK] = v_ref[pl.ds(other, BLK), :]
    c = jnp.minimum(pos[0], pos[BLK]) // BLK
    out[4 * BLK :] = jnp.full((16, HEAD), c, jnp.int32).astype(F32).astype(BF16)


def pack_queries(pos, q_ref, lse_ref, o_ref, g_ref, after_ref, q_out, g_out):
    wide = GROUP * HEAD
    swapped = pos[0] > pos[BLK]
    start = pl.multiple_of(jnp.where(swapped, BLK, 0), BLK)
    lanes = lax.broadcasted_iota(jnp.int32, (BLK, HEAD), 1)
    c = jnp.minimum(pos[0], pos[BLK]) // BLK
    lse = jnp.concatenate([lse_ref[...], jnp.zeros((HEAD - GROUP, TOK), F32)])
    turned = jnp.transpose(lse)
    turned = jnp.where(swapped, jnp.concatenate([turned[BLK:], turned[:BLK]]), turned)
    for i in range(2):
        rows = pl.ds(start if i == 0 else pl.multiple_of(BLK - start, BLK), BLK)
        q_out[i * BLK : (i + 1) * BLK, :wide] = q_ref[rows, :]
        lse = turned[i * BLK : (i + 1) * BLK, :]
        tail = in_terms([lse[:, h : h + 1] for h in range(GROUP)], lanes)
        tail = jnp.where(lanes == 24, c.astype(F32), tail)
        tail = jnp.where(lanes == 25, swapped.astype(F32), tail)
        q_out[i * BLK : (i + 1) * BLK, wide:] = tail.astype(BF16)
    n_heads = g_ref.shape[1] // wide
    lanes = lax.broadcasted_iota(jnp.int32, (g_ref.shape[0], HEAD), 1)
    for d in range(n_heads):
        g = g_ref[:, d * wide : (d + 1) * wide]
        product = g.astype(F32) * o_ref[:, d * wide : (d + 1) * wide].astype(F32)
        delta = [
            jnp.sum(product[:, h * HEAD : (h + 1) * HEAD], axis=1, keepdims=True)
            for h in range(GROUP)
        ]
        tail = in_terms(delta, lanes).astype(BF16)
        for twin in range(2):
            g_out[twin * n_heads + d, :, :wide] = g
            g_out[twin * n_heads + d, :, wide:] = tail


def join(own_ref, a_ref, b_ref, c_ref, q_ref, qx_ref, grad_ref, s_out, x_out):
    for i, ref in enumerate((own_ref, a_ref, b_ref, c_ref)):
        s_out[i] = ref[...]
    wide = (GROUP + 1) * HEAD
    x_out[0, :, :wide] = q_ref[...]
    x_out[1, :, :wide] = qx_ref[...]
    half = lax.axis_index("xh")
    x_out[0, :, wide:] = grad_ref[half]
    x_out[1, :, wide:] = grad_ref[1 - half]


def sum_first(own_ref, c_ref, d_ref, p_ref, own_out, p_out):
    own_out[...] = own_ref[...] + c_ref[...].astype(F32) + d_ref[:NEAR].astype(F32)
    p_out[: NEAR - 1] = p_ref[: NEAR - 1]
    last = p_ref[NEAR - 1].astype(F32) + d_ref[NEAR].astype(F32)
    p_out[NEAR - 1] = last.astype(BF16)


def sum_near(own_ref, p_ref, m_ref, own_out, u_out, w_out):
    total = own_ref[...] + p_ref[...].astype(F32) + m_ref[...].astype(F32)
    own_out[...] = total[0]
    u_out[...] = total[1].astype(BF16)
    w_out[...] = total[2].astype(BF16)


def sum_cores(dq_ref, core_ref, x_ref, dq_out, dqx_out, flag_out):
    dq_out[...] = dq_ref[0] + core_ref[0].astype(F32)
    dqx_out[...] = (dq_ref[1] + core_ref[1].astype(F32)).astype(BF16)
    at = GROUP * HEAD + 25
    flag_out[...] = jnp.broadcast_to(x_ref[0, :BLK, at : at + 1].astype(F32), flag_out.shape)


def finish(flag_ref, own_ref, u_ref, w_ref, dq_ref, dqx_ref, q_out, k_out, v_out):
    swapped = flag_ref[...] > 0.5
    total = own_ref[...] + u_ref[...].astype(F32) + w_ref[...].astype(F32)
    dq = dq_ref[...] + dqx_ref[...].astype(F32)
    for i in range(2):
        here, there = slice(i * BLK, (i + 1) * BLK), slice((1 - i) * BLK, (2 - i) * BLK)
        for h in range(GROUP):
            cols = slice(h * HEAD, (h + 1) * HEAD)
            q_out[here, cols] = jnp.where(swapped, dq[there, cols], dq[here, cols]).astype(BF16)
        k_out[here, :] = jnp.where(swapped, total[there], total[here]).astype(BF16)
        there, of_v = slice((3 - i) * BLK, (4 - i) * BLK), slice((2 + i) * BLK, (3 + i) * BLK)
        v_out[here, :] = jnp.where(swapped, total[there], total[of_v]).astype(BF16)


HEADS = ("xl", "y")


def by_parity(x, distance):
    n = lax.axis_size("z")
    to = [(i + (distance if i % 2 == 0 else -distance)) % n for i in range(n)]
    return lax.ppermute(x, "z", list(enumerate(to)))


def half_round(x):
    n = lax.axis_size("z")
    return lax.ppermute(x, "z", [(i, (i + n // 2) % n) for i in range(n)])


def swapped_with(x, axis):
    return lax.ppermute(x, axis, [(0, 1), (1, 0)])


def local_call(body, out_shape, mib, stream_in=False, stream_out=False):
    vmem, smem = pl.BlockSpec(memory_space=pltpu.VMEM), pl.BlockSpec(memory_space=pltpu.SMEM)
    free = pl.BlockSpec()

    def call(*args, scratch=()):
        return pl.pallas_call(
            body,
            out_shape=out_shape,
            in_specs=[
                smem if a.dtype == jnp.int32 else free if stream_in else vmem for a in args
            ],
            out_specs=jax.tree.map(lambda _: free if stream_out else vmem, out_shape),
            scratch_shapes=scratch,
            compiler_params=pltpu.CompilerParams(vmem_limit_bytes=mib * 1024 * 1024),
            name=body.__name__,
        )(*args)

    return call


def shards(queries, keys, values, outputs, out_grad, lse, positions):
    n_heads = lax.axis_size(HEADS)
    wide = (GROUP + 1) * HEAD

    def like(shape, dtype=BF16):
        return jax.ShapeDtypeStruct(shape, dtype)

    packed, block = (4 * BLK + 16, HEAD), (4 * BLK, HEAD)
    own = local_call(pack_keys, like(packed), 56, stream_in=True)(positions, keys, values)
    far = [by_parity(own, -4), by_parity(own, 4), half_round(own)]

    own_q, send = local_call(
        pack_queries,
        (like((TOK, wide)), like((2 * n_heads, TOK // n_heads, wide))),
        56,
        stream_in=True,
    )(positions, queries, lse.T, outputs, out_grad, own)
    grad = lax.all_to_all(send, ("xh",) + HEADS, split_axis=0, concat_axis=0, tiled=True)
    other_q = swapped_with(own_q, "xh")
    s_set, x = local_call(
        join, (like((4,) + packed), like((2, TOK, 2 * wide))), 8, stream_in=True
    )(own, *far, own_q, other_q, grad.reshape(2, TOK, wide))
    sets = [by_parity(s_set, by) for by in (1, -1, -2)]
    y = swapped_with(x, "core")

    near, dq_shape = (NEAR,) + block, (2, TOK, GROUP * HEAD)
    own_g, dq = local_call(
        with_own, (like((4,) + block, F32), like((4,) + dq_shape[1:], F32)), 16
    )(x, y, s_set, scratch=[pltpu.VMEM((4,) + block, F32)])
    p2_g, m2_g, dq = local_call(
        with_next,
        (like(near), like((NEAR + 1,) + block), like((4,) + dq_shape[1:], F32)),
        16,
    )(
        x,
        y,
        *sets,
        own_g,
        dq,
        scratch=[
            pltpu.VMEM((2 * NEAR,) + packed, BF16),
            pltpu.VMEM((2 * NEAR,) + block, F32),
        ],
    )
    own_g, p1_g, m1_g, dq, dq_core = local_call(
        with_nearest,
        (like(near, F32), like(near), like(near), like(dq_shape, F32), like(dq_shape)),
        16,
    )(
        x,
        y,
        *sets,
        own_g,
        dq,
        scratch=[
            pltpu.VMEM((2 * NEAR,) + packed, BF16),
            pltpu.VMEM((2 * NEAR,) + block, F32),
            pltpu.VMEM((4,) + dq_shape[1:], F32),
        ],
    )

    p2_in, m2_in = by_parity(p2_g, -2), by_parity(m2_g, 2)
    m1_in = by_parity(m1_g, -1)
    own_g, p1_g = local_call(sum_first, (like(near, F32), like(near)), 8)(
        own_g, p2_in, m2_in, p1_g
    )
    p1_in = by_parity(p1_g, 1)
    dq_core = swapped_with(dq_core, "core")
    dq, dqx, flag = local_call(
        sum_cores, (like(dq_shape[1:], F32), like(dq_shape[1:]), like((BLK, HEAD), F32)), 8
    )(dq, dq_core, x)
    dqx = swapped_with(dqx, "xh")
    own_g, u_g, w_g = local_call(sum_near, (like(block, F32), like(block), like(block)), 8)(
        own_g, p1_in, m1_in
    )
    u_g, w_g = by_parity(u_g, 5), by_parity(w_g, -5)
    return local_call(
        finish,
        (like(queries.shape), like(keys.shape), like(values.shape)),
        8,
        stream_out=True,
    )(flag, own_g, u_g, w_g, dq, dqx)


def solution(mesh):
    shape = FOLD or (2, 16, 2, 2, 4)
    split = jax.sharding.Mesh(mesh.devices.reshape(shape), ("xh", "z", "core", "xl", "y"))
    ctx, heads = ("xh", "z", "core"), ("xl", "y")
    return jax.shard_map(
        shards,
        mesh=split,
        in_specs=(
            P(ctx, heads),
            P(ctx, heads),
            P(ctx, heads),
            P(ctx + heads, None),
            P(ctx + heads, None),
            P(ctx, heads),
            P(ctx),
        ),
        out_specs=(P(ctx, heads), P(ctx, heads), P(ctx, heads)),
        check_vma=False,
    )
```
